256 devices in a mesh: row: 8 (over z_hi, x), col: 32 (over y, z_lo, core).
Axes of the slice: x: 4, y: 4, z: 8 (z_hi: 2, z_lo: 4; z = z_hi * 4 + z_lo), core: 2. Of those that a mesh axis runs over, the one named last changes fastest.
Arguments:
- tokens: bfloat16 [192, 256, 512], P('row', 'col'), may hold values from -6 to 6
- cotangent: bfloat16 [192, 256, 512], P('row', 'col'), may hold values from -6 to 6
- gains: float32 [2, 512], replicated, may hold values from 0.25 to 1.75
- w_qkv: bfloat16 [512, 1536], replicated, may hold values from -2 to 2
- w_out: bfloat16 [512, 512], replicated, may hold values from -0.25 to 0.25
- w_up: bfloat16 [512, 2048], replicated, may hold values from -0.25 to 0.25
- w_down: bfloat16 [2048, 512], replicated, may hold values from -0.125 to 0.125
- tile_mask: int32 [24, 32, 49], P('row', 'col'), may hold values from 0 to 1, as said below
Outputs:
- grad_tokens: bfloat16 [192, 256, 512], P('row', 'col')
- grad_qkv: float32 [786432], P(('row', 'col'))
- grad_out: float32 [262144], P(('row', 'col'))
- grad_up: float32 [1048576], P(('row', 'col'))
- grad_down: float32 [1048576], P(('row', 'col'))
- grad_gains: float32 [2, 512], replicated
The draws below stay inside these ranges and needn't reach their ends.
Inputs may be any that keep to these rules, and one draw needn't show every extreme that they name: `tile_mask`: the middle entry, the token's own cell, is 1 for every tile.
All inputs are finite; a program needn't handle non-finite values.
Results may differ from the reference program's by a relative error of at most 0.02.
Values may be sent and summed in bfloat16 or wider, within the bound.
No kernel may reach another device: no remote copies, remote signals or barrier semaphores. Data moves between devices by JAX's collectives and lax.ppermute only.
A program may use at most 128 MiB of HBM per device.

```python
import math
import jax
import jax.numpy as jnp
from jax import lax

D = 512
HEADS = 8
FF = 2048
WINDOW = 7
TILE = 8
GRID_ROWS = 192
GRID_COLS = 256
N_ROW = 8


def draw_w_qkv(key, part):
    key = jax.random.fold_in(key, 7)
    base = jnp.clip(jax.random.normal(key, (D, 3 * D), jnp.float32), -4.0, 4.0) * 0.05
    return base.astype(jnp.bfloat16)


def draw_tile_mask(key, part):
    key = jax.random.fold_in(key, 13)
    votes = jax.random.randint(key, (GRID_ROWS // TILE, GRID_COLS // TILE, WINDOW * WINDOW), 0, 100)
    middle = jnp.arange(WINDOW * WINDOW) == WINDOW * WINDOW // 2
    return jnp.where(middle[None, None, :], 1, (votes < 80).astype(jnp.int32)).astype(jnp.int32)


def with_spikes(drawn, own_key, source, target, blocks, factor):
    def block_of(dim):
        return (jnp.arange(drawn.shape[dim]) // (drawn.shape[dim] // blocks)).reshape((-1,) + (1,) * (drawn.ndim - 1 - dim))

    near = jax.random.permutation(own_key, blocks)[block_of(target)]
    other_side = (block_of(target) + blocks // 2) % blocks
    return jnp.where((block_of(source) == near) | (block_of(source) == other_side), factor * drawn, drawn)


def level_of(rng, extent, cuts, low, top_value):
    level = 1.0
    for dim, parts in cuts:
        steps = jax.random.uniform(jax.random.fold_in(jax.random.fold_in(rng, 6), dim), (parts,), jnp.float32, low / len(cuts), top_value / len(cuts))
        level = level * jnp.repeat(jnp.exp(steps), extent[dim] // parts).reshape((-1,) + (1,) * (len(extent) - 1 - dim))
    return level


def normal_values(own_key, shape, deviation, most, split=(), held_as=jnp.bfloat16):
    values = deviation * jax.random.normal(own_key, shape, jnp.float32)
    if split:
        values = values * level_of(own_key, shape, split, -0.22, 0.18)
    return jnp.clip(values, -most, most).astype(held_as)


def noise_with(rng, shape, deviation, most, cuts, heavy, held_as=jnp.bfloat16):
    drawn = deviation * jax.random.normal(rng, shape, jnp.float32)
    if cuts:
        drawn = drawn * level_of(rng, shape, cuts, -0.22, 0.18)
    return jnp.clip(with_spikes(drawn, jax.random.fold_in(rng, 3), *heavy), -most, most).astype(held_as)


def setup_inputs(seed: int = 0) -> dict:
    key_list = jax.random.split(jax.random.key(seed), 9)
    return {
        "tokens": normal_values(key_list[0], (GRID_ROWS, GRID_COLS, D), 1.0, 6.0, ((0, 8), (1, 32))),
        "cotangent": noise_with(key_list[1], (GRID_ROWS, GRID_COLS, D), 1.0, 6.0, ((0, 8), (1, 32)), (1, 2, 32, 2.75)),
        "gains": jnp.clip(1.0 + 0.15 * jax.random.normal(key_list[2], (2, D), jnp.float32), 0.25, 1.75),
        "w_qkv": draw_w_qkv(jax.random.fold_in(key_list[8], 71), 0),
        "w_out": normal_values(key_list[4], (D, D), D ** -0.5, 0.25),
        "w_up": normal_values(key_list[5], (D, FF), D ** -0.5, 0.25),
        "w_down": normal_values(key_list[6], (FF, D), FF ** -0.5, 0.125),
        "tile_mask": draw_tile_mask(jax.random.fold_in(key_list[8], 71), 0),
    }


epsilon = 1e-06
masked_value = -1e+30

def rms_forward(values_f):
    inverse = lax.rsqrt(lax.optimization_barrier(jnp.mean(values_f * values_f, axis=-1, keepdims=True)) + epsilon)
    return (values_f * inverse, inverse)

def rms_backward(unit, inverse, gain, incoming):
    scaled = incoming * gain
    inner_mean = lax.optimization_barrier(jnp.mean(scaled * unit, axis=-1, keepdims=True))
    return (inverse * (scaled - unit * inner_mean), lax.optimization_barrier(jnp.sum(incoming * unit, axis=0)))

def times_transposed(left, right):
    return lax.dot_general(left, right, (((1,), (1,)), ((), ())), preferred_element_type=jnp.float32)

def transposed_times(left, right):
    return lax.dot_general(left, right, (((0,), (0,)), ((), ())), preferred_element_type=jnp.float32)

def project_front(flattened, gains, w_qkv):
    unit_in, inverse_in = rms_forward(flattened.astype(jnp.float32))
    normed_in = (unit_in * gains[0]).astype(jnp.bfloat16)
    projected = jnp.dot(normed_in, w_qkv, preferred_element_type=jnp.float32).astype(jnp.bfloat16)
    return (normed_in, unit_in, inverse_in, projected)

def middle_and_back(flattened, attention, grad_in, gains, w_out, w_up, w_down):
    mixed = (flattened.astype(jnp.float32) + jnp.dot(attention, w_out, preferred_element_type=jnp.float32)).astype(jnp.bfloat16)
    unit_mid, inverse_mid = rms_forward(mixed.astype(jnp.float32))
    normed_mid = (unit_mid * gains[1]).astype(jnp.bfloat16)
    pre_act = jnp.dot(normed_mid, w_up, preferred_element_type=jnp.float32)
    activated, gelu_back = jax.vjp(jax.nn.gelu, pre_act)
    activated = activated.astype(jnp.bfloat16)
    grad_act = times_transposed(grad_in, w_down)
    grad_pre = gelu_back(grad_act)[0].astype(jnp.bfloat16)
    grad_normed = times_transposed(grad_pre, w_up)
    grad_inner, grad_gain = rms_backward(unit_mid, inverse_mid, gains[1], grad_normed)
    grad_mixed = (grad_in.astype(jnp.float32) + grad_inner).astype(jnp.bfloat16)
    return (normed_mid, activated, grad_pre, grad_mixed, grad_gain)

def window_allowed(tile_mask, grid_rows, grid_cols):
    rim_width = WINDOW // 2
    spread = jnp.repeat(jnp.repeat(tile_mask, TILE, axis=0), TILE, axis=1)
    row_index = jnp.arange(grid_rows)[:, None]
    col_index = jnp.arange(grid_cols)[None, :]
    result = []
    for offset_row in range(WINDOW):
        for offset_col in range(WINDOW):
            target_row = row_index + offset_row - rim_width
            target_col = col_index + offset_col - rim_width
            inside = (target_row >= 0) & (target_row < grid_rows) & (target_col >= 0) & (target_col < grid_cols)
            result.append((spread[:, :, offset_row * WINDOW + offset_col] == 1) & inside)
    return jnp.stack(result)[..., None]

def padded_heads(values, head_width):
    rim_width = WINDOW // 2
    grid_rows, grid_cols = (values.shape[0], values.shape[1])
    heads_f = values.reshape(grid_rows, grid_cols, HEADS, head_width).astype(jnp.float32)
    return jnp.pad(heads_f, ((rim_width, rim_width), (rim_width, rim_width), (0, 0), (0, 0)))

def window_forward(query, keys, values, allowed, head_width):
    grid_rows, grid_cols, model_width = query.shape
    scale_factor = head_width ** (-0.5)
    query_heads = query.reshape(grid_rows, grid_cols, HEADS, head_width).astype(jnp.float32)
    key_pad = padded_heads(keys, head_width)
    value_pad = padded_heads(values, head_width)
    score_list = []
    for offset_row in range(WINDOW):
        for offset_col in range(WINDOW):
            shifted = key_pad[offset_row:offset_row + grid_rows, offset_col:offset_col + grid_cols]
            score_list.append(lax.optimization_barrier(jnp.sum(query_heads * shifted, axis=-1)) * scale_factor)
    scores = jnp.stack(score_list)
    masked = jnp.where(allowed, scores, masked_value)
    row_peak = lax.optimization_barrier(jnp.max(masked, axis=0, keepdims=True))
    exponent = jnp.where(allowed, jnp.exp(masked - row_peak), 0.0)
    probability = exponent / lax.optimization_barrier(jnp.sum(exponent, axis=0, keepdims=True))
    weights = probability.astype(jnp.bfloat16)
    total = jnp.zeros((grid_rows, grid_cols, HEADS, head_width), jnp.float32)
    for offset_row in range(WINDOW):
        for offset_col in range(WINDOW):
            shifted = value_pad[offset_row:offset_row + grid_rows, offset_col:offset_col + grid_cols]
            total = total + weights[offset_row * WINDOW + offset_col][..., None].astype(jnp.float32) * shifted
    return (probability, weights, total.reshape(grid_rows, grid_cols, model_width).astype(jnp.bfloat16))

def window_backward(query, keys, values, probability, weights, grad_attn, head_width):
    grid_rows, grid_cols, model_width = query.shape
    rim_width = WINDOW // 2
    scale_factor = head_width ** (-0.5)
    query_heads = query.reshape(grid_rows, grid_cols, HEADS, head_width).astype(jnp.float32)
    grad_heads = grad_attn.reshape(grid_rows, grid_cols, HEADS, head_width).astype(jnp.float32)
    key_pad = padded_heads(keys, head_width)
    value_pad = padded_heads(values, head_width)
    prob_list = []
    for offset_row in range(WINDOW):
        for offset_col in range(WINDOW):
            shifted = value_pad[offset_row:offset_row + grid_rows, offset_col:offset_col + grid_cols]
            prob_list.append(lax.optimization_barrier(jnp.sum(grad_heads * shifted, axis=-1)))
    grad_prob = jnp.stack(prob_list)
    row_inner = lax.optimization_barrier(jnp.sum(probability * grad_prob, axis=0, keepdims=True))
    grad_score = (probability * (grad_prob - row_inner) * scale_factor).astype(jnp.bfloat16)
    grad_query = jnp.zeros((grid_rows, grid_cols, HEADS, head_width), jnp.float32)
    grad_key = jnp.zeros_like(key_pad)
    grad_value = jnp.zeros_like(value_pad)
    for offset_row in range(WINDOW):
        for offset_col in range(WINDOW):
            offset = offset_row * WINDOW + offset_col
            shifted = key_pad[offset_row:offset_row + grid_rows, offset_col:offset_col + grid_cols]
            score_f = grad_score[offset][..., None].astype(jnp.float32)
            grad_query = grad_query + score_f * shifted
            grad_key = grad_key.at[offset_row:offset_row + grid_rows, offset_col:offset_col + grid_cols].add(score_f * query_heads)
            weight_f = weights[offset][..., None].astype(jnp.float32)
            grad_value = grad_value.at[offset_row:offset_row + grid_rows, offset_col:offset_col + grid_cols].add(weight_f * grad_heads)
    inner_key = grad_key[rim_width:rim_width + grid_rows, rim_width:rim_width + grid_cols]
    inner_value = grad_value[rim_width:rim_width + grid_rows, rim_width:rim_width + grid_cols]
    shape_out = (grid_rows, grid_cols, model_width)
    return jnp.concatenate([grad_query.reshape(shape_out), inner_key.reshape(shape_out), inner_value.reshape(shape_out)], axis=-1)

def reference(tokens, cotangent, gains, w_qkv, w_out, w_up, w_down, tile_mask):
    grid_rows, grid_cols, model_width = tokens.shape
    head_width = model_width // HEADS
    tok_count = grid_rows * grid_cols
    flattened = tokens.reshape(tok_count, model_width)
    grad_in = cotangent.reshape(tok_count, model_width)
    normed_in, unit_in, inverse_in, projected = project_front(flattened, gains, w_qkv)
    gridded = projected.reshape(grid_rows, grid_cols, 3 * model_width)
    query = gridded[..., :model_width]
    keys = gridded[..., model_width:2 * model_width]
    values = gridded[..., 2 * model_width:]
    allowed = window_allowed(tile_mask, grid_rows, grid_cols)
    probability, weights, attention = window_forward(query, keys, values, allowed, head_width)
    attention_flat = attention.reshape(tok_count, model_width)

    def strip_step(carry, pieces):
        strip_tokens, strip_attn, strip_grad = pieces
        normed_mid, activated, grad_pre, grad_mixed, grad_gain = middle_and_back(strip_tokens, strip_attn, strip_grad, gains, w_out, w_up, w_down)
        updated = (carry[0] + transposed_times(normed_mid, grad_pre), carry[1] + transposed_times(activated, strip_grad), carry[2] + grad_gain, carry[3] + transposed_times(strip_attn, grad_mixed))
        return (updated, grad_mixed)
    start = (jnp.zeros((model_width, FF), jnp.float32), jnp.zeros((FF, model_width), jnp.float32), jnp.zeros((model_width,), jnp.float32), jnp.zeros((model_width, model_width), jnp.float32))
    pieces = (flattened.reshape(N_ROW, -1, model_width), attention_flat.reshape(N_ROW, -1, model_width), grad_in.reshape(N_ROW, -1, model_width))
    sums, grad_mixed = lax.scan(strip_step, start, pieces)
    grad_upw, grad_downw, gain_mid, grad_outw = sums
    grad_mixed = grad_mixed.reshape(tok_count, model_width)
    grad_attn = times_transposed(grad_mixed, w_out).astype(jnp.bfloat16)
    grad_projected = window_backward(query, keys, values, probability, weights, grad_attn.reshape(grid_rows, grid_cols, model_width), head_width)
    grad_projected = grad_projected.reshape(tok_count, 3 * model_width).astype(jnp.bfloat16)
    grad_normed = times_transposed(grad_projected, w_qkv)
    grad_front, gain_in = rms_backward(unit_in, inverse_in, gains[0], grad_normed)
    grad_tokens = (grad_mixed.astype(jnp.float32) + grad_front).astype(jnp.bfloat16).reshape(grid_rows, grid_cols, model_width)
    norm_scale = 1.0 / math.sqrt(tok_count)
    grad_qkvw = transposed_times(normed_in, grad_projected)
    return (grad_tokens, (grad_qkvw * norm_scale).reshape(-1), (grad_outw * norm_scale).reshape(-1), (grad_upw * norm_scale).reshape(-1), (grad_downw * norm_scale).reshape(-1), jnp.stack([gain_in, gain_mid]) * norm_scale)
```

```python
import functools
import math

import jax
import jax.numpy as jnp
import numpy as np
from jax import lax
from jax.experimental import pallas as pl
from jax.experimental.pallas import tpu as pltpu
from jax.sharding import PartitionSpec as P

D = 512
FF = 2048
HEADS = 8
WINDOW = 7
TILE = 8
RIM = WINDOW // 2
EPS = 1e-06
AXES = ("row", "col")
N_COL = 32
GRID_ROWS = 192
GRID_COLS = 256
ROWS = 24
COLS = 8
TOK = ROWS * COLS
TILES = ROWS // TILE
ER = 32
EC = 16
EXT = ER * EC
QT = TILE * TILE
KT = 256
F32 = jnp.float32
BF16 = jnp.bfloat16
GELU_C = math.sqrt(2.0 / math.pi)


def nn(a, b):
    return lax.dot_general(a, b, (((1,), (0,)), ((), ())), preferred_element_type=F32)


def nt(a, b):
    return lax.dot_general(a, b, (((1,), (1,)), ((), ())), preferred_element_type=F32)


def tn(a, b):
    return lax.dot_general(a, b, (((0,), (0,)), ((), ())), preferred_element_type=F32)


def unit_of(x):
    inv = lax.rsqrt(jnp.mean(x * x, axis=-1, keepdims=True) + EPS)
    return x * inv, inv


def head_mask(rows, h):
    lane = lax.broadcasted_iota(jnp.int32, (rows, 256), 1)
    return (lane // 64) == h


def stack_heads(x):
    zero = jnp.zeros_like(x)
    return jnp.concatenate([jnp.where(head_mask(x.shape[0], h), x, zero) for h in range(4)], axis=0)


def unstack_heads(x):
    rows = x.shape[0] // 4
    out = jnp.where(head_mask(rows, 0), x[:rows], 0.0)
    for h in range(1, 4):
        out = out + jnp.where(head_mask(rows, h), x[h * rows : (h + 1) * rows], 0.0)
    return out


def prep_kernel(coord, mask, cot, w_down, gact, bias, pt_a, pt_b, pt_d):
    for c in range(4):
        gact[:, c * 512 : (c + 1) * 512] = nt(cot[...], w_down[c * 512 : (c + 1) * 512, :])
    q = lax.broadcasted_iota(jnp.int32, (QT, KT), 0)
    k = lax.broadcasted_iota(jnp.int32, (QT, KT), 1)
    ki = k // EC
    kj = k % EC
    da = ki - q // TILE
    db = kj - q % TILE
    slot = jnp.where((da >= 0) & (da < WINDOW) & (db >= 0) & (db < WINDOW), da * WINDOW + db, -1)
    allowed = [jnp.zeros((QT, KT), jnp.int32) for _ in range(TILES)]
    for s in range(WINDOW * WINDOW):
        here = slot == s
        for t in range(TILES):
            allowed[t] = jnp.where(here, mask[t, s], allowed[t])
    gc = coord[1] * COLS + kj - RIM
    for t in range(TILES):
        gr = coord[0] * ROWS + t * TILE + ki - RIM
        ok = (allowed[t] == 1) & (gr >= 0) & (gr < GRID_ROWS) & (gc >= 0) & (gc < GRID_COLS)
        bias[t] = jnp.where(ok, 0.0, -1e30)
    me = coord[2]
    lane = lax.broadcasted_iota(jnp.int32, (512, 512), 1)
    p = lax.broadcasted_iota(jnp.int32, (512, 512), 0)
    s1 = p & 1
    z = (p >> 1) & 7
    mid1 = (p >> 4) & 3
    mid2 = (p >> 6) & 3
    co = p >> 8
    zpart = (z >> 2) * 128 + (z & 3) * 2 + co
    ka = (zpart + mid2 * 32 + mid1 * 8) ^ me
    pt_a[...] = jnp.where(lane == ka * 2 + s1, 1.0, 0.0).astype(BF16)
    kb = (zpart + mid1 * 32 + mid2 * 8) ^ me
    pt_b[...] = jnp.where(lane == kb * 2 + s1, 1.0, 0.0).astype(BF16)
    s8 = p & 7
    zl = (p >> 3) & 3
    xl = (p >> 5) & 1
    y = (p >> 6) & 3
    kd = (xl * 32 + y * 8 + zl * 2 + co) ^ (me & 63)
    pt_d[...] = jnp.where(lane == kd * 8 + s8, 1.0, 0.0).astype(BF16)


def forward_kernel(
    coord, text, tok, cot, gains, w_qkv, w_out, w_up, gact, bias, pt_a, pt_d,
    u_keep, u_send, d_keep, d_send, gm_o, q_o, kv_o, p_o, ne_o, no_o, gain_o, attn_s,
):
    unit_e, _ = unit_of(text[...].astype(F32))
    ne = (unit_e * gains[0:1, :]).astype(BF16)
    ne_o[...] = ne
    kv_o[...] = nn(ne, w_qkv[:, D:]).astype(BF16)
    xt = tok[...].astype(F32)
    unit_o, _ = unit_of(xt)
    no = (unit_o * gains[0:1, :]).astype(BF16)
    no_o[...] = no
    q_o[...] = nn(no, w_qkv[:, :D]).astype(BF16)
    for t in range(TILES):
        b4 = jnp.concatenate([bias[t]] * 4, axis=0)
        for g in range(2):
            cols = slice(g * 256, (g + 1) * 256)
            vcols = slice(D + g * 256, D + (g + 1) * 256)
            keys = kv_o[t * 128 : t * 128 + KT, cols]
            vals = kv_o[t * 128 : t * 128 + KT, vcols]
            qs = stack_heads(q_o[t * QT : (t + 1) * QT, cols])
            s = nt(qs, keys) * 0.125 + b4
            e = jnp.exp(s - jnp.max(s, axis=-1, keepdims=True))
            prob = e / jnp.sum(e, axis=-1, keepdims=True)
            p_o[t * 2 + g] = prob
            o = nn(prob.astype(BF16), vals)
            attn_s[t * QT : (t + 1) * QT, cols] = unstack_heads(o).astype(BF16)
    attn = attn_s[...]
    mixed = (xt + nn(attn, w_out[...])).astype(BF16)
    um, inv_m = unit_of(mixed.astype(F32))
    nm = (um * gains[1:2, :]).astype(BF16)
    nmt = nt(pt_a[...], nm).astype(BF16)
    c_me = (coord[2] >> 6) & 3
    gn = jnp.zeros((TOK, D), F32)
    for c in range(4):
        cols = slice(c * 512, (c + 1) * 512)
        pre = nn(nm, w_up[:, cols])
        th = jnp.tanh(GELU_C * (pre + 0.044715 * (pre * pre * pre)))
        half = 0.5 * (1.0 + th)
        act = (pre * half).astype(BF16)
        slope = half + 0.5 * pre * (1.0 - th * th) * (GELU_C * (1.0 + 0.134145 * (pre * pre)))
        gp = (gact[:, cols] * slope).astype(BF16)
        gn = gn + nt(gp, w_up[:, cols])
        gu = nn(nmt, gp).astype(BF16)
        u_keep[:, cols] = gu[:256]
        u_send[:, cols] = gu[256:]
        act_t = nt(pt_d[...], act).astype(BF16)
        gd = nn(act_t, cot[...]).astype(BF16)
        c_rel = c ^ c_me
        zh = c_rel >> 1
        xh = c_rel & 1
        for y in range(4):
            for xl in range(2):
                base = (y * 2 + xl) * 32
                d_keep[y, xh, xl, zh] = gd[base : base + 32]
                d_send[y, xh, xl, zh] = gd[256 + base : 256 + base + 32]
    g = gn * gains[1:2, :]
    gm = (cot[...].astype(F32) + inv_m * (g - um * jnp.mean(g * um, axis=-1, keepdims=True))).astype(BF16)
    gm_o[...] = gm
    gain_o[...] = jnp.sum(gn * um, axis=0, keepdims=True)
    go = nn(nt(pt_a[...], attn).astype(BF16), gm).astype(BF16)
    u_keep[:, FF:] = go[:256]
    u_send[:, FF:] = go[256:]


def backward_kernel(
    gm, w_out, w_qkv, q, kv, p_in, ne, no, text, tok, gain_mid, pt,
    k_keep, k_send, gne_o, gnq_o, dq_s, dkv_s,
):
    ga = nt(gm[...], w_out[...]).astype(BF16)
    dkv_s[...] = jnp.zeros_like(dkv_s)
    for t in range(TILES):
        for g in range(2):
            cols = slice(g * 256, (g + 1) * 256)
            vcols = slice(D + g * 256, D + (g + 1) * 256)
            rows = slice(t * 128, t * 128 + KT)
            prob = p_in[t * 2 + g]
            gas = stack_heads(ga[t * QT : (t + 1) * QT, cols])
            qs = stack_heads(q[t * QT : (t + 1) * QT, cols])
            gp = nt(gas, kv[rows, vcols])
            inner = jnp.sum(prob * gp, axis=-1, keepdims=True)
            ds = (prob * (gp - inner) * 0.125).astype(BF16)
            dq_s[t * QT : (t + 1) * QT, cols] = unstack_heads(nn(ds, kv[rows, cols])).astype(BF16)
            dkv_s[rows, cols] += tn(ds, qs)
            dkv_s[rows, vcols] += tn(prob.astype(BF16), gas)
    dkv = dkv_s[...].astype(BF16)
    dq = dq_s[...]
    gk = nn(nt(pt[...], ne[...]).astype(BF16), dkv).astype(BF16)
    gq = nn(nt(pt[...], no[...]).astype(BF16), dq).astype(BF16)
    k_keep[:256, :D] = gq[:256]
    k_send[:256, :D] = gq[256:]
    k_keep[:256, D:] = gk[:256]
    k_send[:256, D:] = gk[256:]
    gne = nt(dkv, w_qkv[:, D:])
    gnq = nt(dq, w_qkv[:, :D])
    gne_o[...] = gne
    gnq_o[...] = gnq
    unit_e, _ = unit_of(text[...].astype(F32))
    unit_o, _ = unit_of(tok[...].astype(F32))
    gain_in = jnp.sum(gne * unit_e, axis=0, keepdims=True) + jnp.sum(gnq * unit_o, axis=0, keepdims=True)
    row = jnp.concatenate([gain_in, gain_mid[...], jnp.zeros((1, D), F32)], axis=1)
    block = jnp.broadcast_to(row, (16, 3 * D)).astype(BF16)
    k_keep[256:, :] = block
    k_send[256:, :] = block


def call(body, outs, scratch, n_smem, n_in, flops, nbytes):
    smem = pl.BlockSpec(memory_space=pltpu.SMEM)
    vmem = pl.BlockSpec(memory_space=pltpu.VMEM)
    return pl.pallas_call(
        body,
        out_shape=[jax.ShapeDtypeStruct(s, d) for s, d in outs],
        in_specs=[smem] * n_smem + [vmem] * n_in,
        out_specs=[vmem] * len(outs),
        scratch_shapes=scratch,
        compiler_params=pltpu.CompilerParams(vmem_limit_bytes=50 * 1024 * 1024),
        cost_estimate=pl.CostEstimate(flops=flops, bytes_accessed=nbytes, transcendentals=0),
    )


def perm_xor(bits):
    return [(k, k ^ bits) for k in range(256)]


def shift(step):
    pairs = []
    for k in range(256):
        r, c = divmod(k, N_COL)
        if step in (1, -1):
            if 0 <= c + step < N_COL:
                pairs.append((k, k + step))
        elif 0 <= k + step < 256:
            pairs.append((k, k + step))
    return pairs


def send(x, perm):
    return lax.ppermute(x, AXES, perm)


X_BIT = 32
Y_BIT = 8


def z_bits(d):
    return (d >> 2) * 128 + (d & 3) * 2


def total(parts):
    f = [v.astype(F32) for v in parts]
    while len(f) > 1:
        f = [f[i] + f[i + 1] for i in range(0, len(f), 2)]
    return f[0]


def quarter(chunks, bit):
    got = [send(chunks[d], perm_xor(bit * d)) for d in range(1, 4)]
    return [chunks[0]] + got


def chain(keep, sent, bits, gain_rows):
    rows = keep.shape[0] - gain_rows
    recv = send(sent, perm_xor(1))
    extra = None
    step = rows // 4

    def piece(a, lo, size):
        return lax.slice_in_dim(a, lo, lo + size, axis=0)

    chunks = [total([piece(keep, d * step, step), piece(recv, d * step, step)]).astype(BF16) for d in range(4)]
    if gain_rows:
        extra = total([piece(keep, rows, 8), piece(recv, rows, 8)]).astype(BF16)
    for level, bit in enumerate(bits):
        msgs = chunks if extra is None else [jnp.concatenate([c, extra], axis=0) for c in chunks]
        got = quarter(msgs, bit)
        summed = total(got).astype(BF16)
        if extra is not None:
            extra = piece(summed, step, 8)
        if level + 1 < len(bits):
            step //= 4
            chunks = [piece(summed, d * step, step) for d in range(4)]
    return (piece(summed, 0, step), extra)


def per_device(tokens, cotangent, gains, w_qkv, w_out, w_up, w_down, tile_mask):
    row = lax.axis_index("row")
    col = lax.axis_index("col")
    coord = jnp.stack([row, col, row * N_COL + col]).astype(jnp.int32)
    tok = tokens.reshape(TOK, D)
    cot = cotangent.reshape(TOK, D)

    above = send(tokens[ROWS - RIM :], shift(N_COL))
    below = send(tokens[:RIM], shift(-N_COL))
    tall = jnp.concatenate([above, tokens, below], axis=0)
    left = send(tall[:, COLS - RIM :], shift(1))
    right = send(tall[:, :RIM], shift(-1))
    wide = jnp.concatenate([left, tall, right, jnp.zeros((ROWS + 2 * RIM, 2, D), BF16)], axis=1)
    text = jnp.concatenate([wide, jnp.zeros((2, EC, D), BF16)], axis=0).reshape(EXT, D)

    gact, bias, pt_a, pt_b, pt_d = call(
        prep_kernel,
        [((TOK, FF), F32), ((TILES, QT, KT), F32), ((D, D), BF16), ((D, D), BF16), ((D, D), BF16)],
        [], 2, 2, 2 * TOK * D * FF, 6_000_000,
    )(coord, tile_mask.reshape(TILES, WINDOW * WINDOW), cot, w_down)

    u_keep, u_send, d_keep, d_send, gm, q, kv, prob, ne, no, gain_mid = call(
        forward_kernel,
        [
            ((256, FF + D), BF16), ((256, FF + D), BF16),
            ((4, 2, 2, 2, 32, D), BF16), ((4, 2, 2, 2, 32, D), BF16),
            ((TOK, D), BF16), ((TOK, D), BF16), ((EXT, 2 * D), BF16), ((6, 256, KT), F32),
            ((EXT, D), BF16), ((TOK, D), BF16), ((1, D), F32),
        ],
        [pltpu.VMEM((TOK, D), BF16)], 1, 11, 5_000_000_000, 20_000_000,
    )(coord, text, tok, cot, gains, w_qkv, w_out, w_up, gact, bias, pt_a, pt_d)

    k_keep, k_send, gne, gnq = call(
        backward_kernel,
        [((272, 3 * D), BF16), ((272, 3 * D), BF16), ((EXT, D), F32), ((TOK, D), F32)],
        [pltpu.VMEM((TOK, D), BF16), pltpu.VMEM((EXT, 2 * D), F32)], 0, 12, 3_000_000_000, 12_000_000,
    )(gm, w_out, w_qkv, q, kv, prob, ne, no, text, tok, gain_mid, pt_b)

    su, _ = chain(u_keep, u_send, (X_BIT, Y_BIT), 0)
    sd, _ = chain(d_keep.reshape(1024, D), d_send.reshape(1024, D), (Y_BIT, X_BIT), 0)
    sk, sg = chain(k_keep, k_send, (Y_BIT, X_BIT), 16)
    su = su.reshape(8, 2, FF + D)
    sd = sd.reshape(8, 8, D)
    sk = sk.reshape(8, 2, 3 * D)
    flat = jnp.concatenate(
        [
            su[..., :FF].reshape(8, 2 * FF), sd.reshape(8, 8 * D), su[..., FF:].reshape(8, 2 * D),
            sk.reshape(8, 6 * D), jnp.broadcast_to(sg[:1, : 2 * D], (8, 2 * D)),
        ],
        axis=1,
    )
    got = [flat[0:1]] + [send(flat[d : d + 1], perm_xor(z_bits(d))) for d in range(1, 8)]
    norm_scale = 1.0 / math.sqrt(GRID_ROWS * GRID_COLS)
    summed = total(got)[0] * norm_scale
    cuts = np.cumsum([0, 2 * FF, 8 * D, 2 * D, 6 * D, 2 * D])
    g_up, g_down, g_out, g_qkv, g_gains = [summed[a:b] for a, b in zip(cuts[:-1], cuts[1:])]

    gne3 = gne.reshape(ER, EC, D)[: ROWS + 2 * RIM]
    to_left = send(gne3[:, :RIM].astype(BF16), shift(-1)).astype(F32)
    to_right = send(gne3[:, RIM + COLS : 2 * RIM + COLS].astype(BF16), shift(1)).astype(F32)
    mid = gne3[:, RIM : RIM + COLS]
    gap = COLS - RIM
    mid = mid + jnp.pad(to_right, ((0, 0), (0, gap), (0, 0))) + jnp.pad(to_left, ((0, 0), (gap, 0), (0, 0)))
    to_up = send(mid[:RIM].astype(BF16), shift(-N_COL)).astype(F32)
    to_down = send(mid[RIM + ROWS :].astype(BF16), shift(N_COL)).astype(F32)
    gap = ROWS - RIM
    gn = mid[RIM : RIM + ROWS] + jnp.pad(to_down, ((0, gap), (0, 0), (0, 0))) + jnp.pad(to_up, ((gap, 0), (0, 0), (0, 0)))
    gn = gn + gnq.reshape(ROWS, COLS, D)
    unit, inv = unit_of(tokens.astype(F32))
    g1 = gn * gains[0]
    front = inv * (g1 - unit * jnp.mean(g1 * unit, axis=-1, keepdims=True))
    grad_tokens = (gm.reshape(ROWS, COLS, D).astype(F32) + front).astype(BF16)
    return (grad_tokens, g_qkv, g_out, g_up, g_down, g_gains.reshape(2, D))


def solution(mesh):
    block = P("row", "col", None)
    flat = P(("row", "col"))
    return jax.shard_map(
        per_device,
        mesh=mesh,
        in_specs=(block, block, P(), P(), P(), P(), P(), block),
        out_specs=(block, flat, flat, flat, flat, P()),
        check_vma=False,
    )
```

```python
import math

import jax
import jax.numpy as jnp
from jax import lax
from jax.experimental import pallas as pl
from jax.experimental.pallas import tpu as pltpu
from jax.sharding import PartitionSpec as P

D = 512
FF = 2048
HEADS = 8
WINDOW = 7
TILE = 8
RIM = WINDOW // 2
EPS = 1e-06
AXES = ("row", "col")
N_COL = 32
GRID_ROWS = 192
GRID_COLS = 256
ROWS = 24
COLS = 8
TOK = ROWS * COLS
TILES = ROWS // TILE
ER = 32
EC = 16
EXT = ER * EC
QT = TILE * TILE
KT = 256
F32 = jnp.float32
BF16 = jnp.bfloat16
GELU_C = math.sqrt(2.0 / math.pi)


def nn(a, b):
    return lax.dot_general(a, b, (((1,), (0,)), ((), ())), preferred_element_type=F32)


def nt(a, b):
    return lax.dot_general(a, b, (((1,), (1,)), ((), ())), preferred_element_type=F32)


def tn(a, b):
    return lax.dot_general(a, b, (((0,), (0,)), ((), ())), preferred_element_type=F32)


def unit_of(x):
    inv = lax.rsqrt(jnp.mean(x * x, axis=-1, keepdims=True) + EPS)
    return x * inv, inv


def head_mask(rows, h):
    lane = lax.broadcasted_iota(jnp.int32, (rows, 256), 1)
    return (lane // 64) == h


def stack_heads(x):
    zero = jnp.zeros_like(x)
    return jnp.concatenate([jnp.where(head_mask(x.shape[0], h), x, zero) for h in range(4)], axis=0)


def unstack_heads(x):
    rows = x.shape[0] // 4
    out = jnp.where(head_mask(rows, 0), x[:rows], 0.0)
    for h in range(1, 4):
        out = out + jnp.where(head_mask(rows, h), x[h * rows : (h + 1) * rows], 0.0)
    return out


def prep_front_kernel(cot, w_down, gact):
    for c in range(4):
        gact[:, c * 512 : (c + 1) * 512] = nt(cot[...], w_down[c * 512 : (c + 1) * 512, :])


def prep_mask_kernel(coord, mask, bias, pt_u, pt_d):
    q = lax.broadcasted_iota(jnp.int32, (QT, KT), 0)
    k = lax.broadcasted_iota(jnp.int32, (QT, KT), 1)
    ki = k // EC
    kc = k % EC
    kj = jnp.where(kc < COLS, kc + RIM, jnp.where(kc < COLS + RIM, kc - COLS, kc))
    da = ki - q // TILE
    db = kj - q % TILE
    slot = jnp.where((da >= 0) & (da < WINDOW) & (db >= 0) & (db < WINDOW), da * WINDOW + db, -1)
    allowed = [jnp.zeros((QT, KT), jnp.int32) for _ in range(TILES)]
    for s in range(WINDOW * WINDOW):
        here = slot == s
        for t in range(TILES):
            allowed[t] = jnp.where(here, mask[t, s], allowed[t])
    gc = coord[1] * COLS + kj - RIM
    for t in range(TILES):
        gr = coord[0] * ROWS + t * TILE + ki - RIM
        ok = (allowed[t] == 1) & (gr >= 0) & (gr < GRID_ROWS) & (gc >= 0) & (gc < GRID_COLS)
        bias[t] = jnp.where(ok, 0.0, -1e30)
    me = coord[2] & 1
    lane = lax.broadcasted_iota(jnp.int32, (512, 512), 1)
    p = lax.broadcasted_iota(jnp.int32, (512, 512), 0)
    co = (p >> 8) ^ me
    k_u = ((p >> 3) & 1) * 128 + ((p >> 4) & 15) * 8 + ((p >> 1) & 3) * 2 + co
    pt_u[...] = jnp.where(lane == k_u * 2 + (p & 1), 1.0, 0.0).astype(BF16)
    k_d = ((p >> 5) & 7) * 8 + ((p >> 3) & 3) * 2 + co
    pt_d[...] = jnp.where(lane == k_d * 8 + (p & 7), 1.0, 0.0).astype(BF16)


def forward_kernel(
    mid, top, low, tok, cot, gains, w_qkv, w_out, w_up, gact, bias, pt_u, pt_d,
    u_keep, u_send, d_keep, d_send, gm_o, q_o, kv_o, p_o, ne_o, no_o, gain_o, text_s, attn_s,
):
    text_s[:RIM] = top[...]
    text_s[RIM : RIM + ROWS] = mid[...]
    text_s[RIM + ROWS : ROWS + 2 * RIM] = low[...]
    text_s[ROWS + 2 * RIM :] = jnp.zeros((ER - ROWS - 2 * RIM, EC, D), BF16)
    unit_e, _ = unit_of(text_s[...].reshape(EXT, D).astype(F32))
    ne = (unit_e * gains[0:1, :]).astype(BF16)
    ne_o[...] = ne
    kv_o[...] = nn(ne, w_qkv[:, D:]).astype(BF16)
    xt = tok[...].astype(F32)
    unit_o, _ = unit_of(xt)
    no = (unit_o * gains[0:1, :]).astype(BF16)
    no_o[...] = no
    q_o[...] = nn(no, w_qkv[:, :D]).astype(BF16)
    for t in range(TILES):
        b4 = jnp.concatenate([bias[t]] * 4, axis=0)
        for g in range(2):
            cols = slice(g * 256, (g + 1) * 256)
            vcols = slice(D + g * 256, D + (g + 1) * 256)
            keys = kv_o[t * 128 : t * 128 + KT, cols]
            vals = kv_o[t * 128 : t * 128 + KT, vcols]
            qs = stack_heads(q_o[t * QT : (t + 1) * QT, cols])
            s = nt(qs, keys) * 0.125 + b4
            e = jnp.exp(s - jnp.max(s, axis=-1, keepdims=True))
            prob = e / jnp.sum(e, axis=-1, keepdims=True)
            p_o[t * 2 + g] = prob
            o = nn(prob.astype(BF16), vals)
            attn_s[t * QT : (t + 1) * QT, cols] = unstack_heads(o).astype(BF16)
    attn = attn_s[...]
    mixed = (xt + nn(attn, w_out[...])).astype(BF16)
    um, inv_m = unit_of(mixed.astype(F32))
    nm = (um * gains[1:2, :]).astype(BF16)
    nmt = nt(pt_u[...], nm).astype(BF16)
    gn = jnp.zeros((TOK, D), F32)
    for c in range(4):
        cols = slice(c * 512, (c + 1) * 512)
        pre = nn(nm, w_up[:, cols])
        th = jnp.tanh(GELU_C * (pre + 0.044715 * (pre * pre * pre)))
        half = 0.5 * (1.0 + th)
        act = (pre * half).astype(BF16)
        slope = half + 0.5 * pre * (1.0 - th * th) * (GELU_C * (1.0 + 0.134145 * (pre * pre)))
        gp = (gact[:, cols] * slope).astype(BF16)
        gn = gn + nt(gp, w_up[:, cols])
        gu = nn(nmt, gp).astype(BF16)
        u_keep[:, c] = gu[:256].reshape(16, 16, D)
        u_send[:, c] = gu[256:].reshape(16, 16, D)
        act_t = nt(pt_d[...], act).astype(BF16)
        gd = nn(act_t, cot[...]).astype(BF16)
        for x in range(2):
            lo = (2 * (c & 1) + x) * 4
            d_keep[lo : lo + 4, c >> 1] = gd[x * 128 : x * 128 + 128].reshape(4, 32, D)
            d_send[lo : lo + 4, c >> 1] = gd[256 + x * 128 : 256 + x * 128 + 128].reshape(4, 32, D)
    g = gn * gains[1:2, :]
    gm = (cot[...].astype(F32) + inv_m * (g - um * jnp.mean(g * um, axis=-1, keepdims=True))).astype(BF16)
    gm_o[...] = gm
    gain_o[...] = jnp.sum(gn * um, axis=0, keepdims=True)
    go = nn(nt(pt_u[...], attn).astype(BF16), gm).astype(BF16)
    u_keep[:, 4] = go[:256].reshape(16, 16, D)
    u_send[:, 4] = go[256:].reshape(16, 16, D)


def backward_kernel(
    gm, w_out, w_qkv, q, kv, p_in, ne, no, mid, top, low, tok, gain_mid, pt,
    k_keep, k_send, g_keep, g_send, gne_o, gnq_o, dq_s, dkv_s,
):
    ga = nt(gm[...], w_out[...]).astype(BF16)
    dkv_s[...] = jnp.zeros_like(dkv_s)
    for t in range(TILES):
        for g in range(2):
            cols = slice(g * 256, (g + 1) * 256)
            vcols = slice(D + g * 256, D + (g + 1) * 256)
            rows = slice(t * 128, t * 128 + KT)
            prob = p_in[t * 2 + g]
            gas = stack_heads(ga[t * QT : (t + 1) * QT, cols])
            qs = stack_heads(q[t * QT : (t + 1) * QT, cols])
            gp = nt(gas, kv[rows, vcols])
            inner = jnp.sum(prob * gp, axis=-1, keepdims=True)
            ds = (prob * (gp - inner) * 0.125).astype(BF16)
            dq_s[t * QT : (t + 1) * QT, cols] = unstack_heads(nn(ds, kv[rows, cols])).astype(BF16)
            dkv_s[rows, cols] += tn(ds, qs)
            dkv_s[rows, vcols] += tn(prob.astype(BF16), gas)
    dkv = dkv_s[...].astype(BF16)
    dq = dq_s[...]
    gk = nn(nt(pt[...], ne[...]).astype(BF16), dkv).astype(BF16)
    gq = nn(nt(pt[...], no[...]).astype(BF16), dq).astype(BF16)
    for i, part in enumerate([gq, gk[:, :D], gk[:, D:]]):
        k_keep[:, i] = part[:256].reshape(16, 16, D)
        k_send[:, i] = part[256:].reshape(16, 16, D)
    gne = nt(dkv, w_qkv[:, D:])
    gnq = nt(dq, w_qkv[:, :D])
    gne_o[...] = gne
    gnq_o[...] = gnq
    gain_in = jnp.sum(gnq * unit_of(tok[...].astype(F32))[0], axis=0, keepdims=True)
    at = 0
    for ref in (top, mid, low):
        size = ref.shape[0] * EC
        unit, _ = unit_of(ref[...].reshape(size, D).astype(F32))
        gain_in = gain_in + jnp.sum(gne[at : at + size] * unit, axis=0, keepdims=True)
        at += size
    spread = jnp.concatenate([gain_in, gain_mid[...], jnp.zeros((14, D), F32)], axis=0).astype(BF16)
    g_keep[...] = spread
    g_send[...] = spread


def join_kernel(uk, ur, dk, dr, kk, kr, gk, gr, out):
    at = 0
    for a, b in ((uk, ur), (dk, dr), (kk, kr)):
        n = a.shape[1]
        out[:, at : at + n] = (a[...].astype(F32) + b[...].astype(F32)).astype(BF16)
        at += n
    gain = (gk[...].astype(F32) + gr[...].astype(F32)).astype(BF16)
    for j in range(16):
        out[j, at] = gain


def reduce_xy_kernel(got, out):
    rows = 13 * 16
    acc = got[0].reshape(rows, D).astype(F32)
    for j in range(1, 16):
        acc = acc + got[j].reshape(rows, D).astype(F32)
    acc = acc.astype(BF16)
    i = lax.broadcasted_iota(jnp.int32, (256, rows), 0)
    lane = lax.broadcasted_iota(jnp.int32, (256, rows), 1)
    z = i // 32
    r = i % 32
    up = (r % 4) * 16 + z * 2 + r // 4
    down = 80 + z * 8 + (r - 8)
    o = 64 + z * 2 + (r - 16)
    qkv = 144 + ((r - 18) % 3) * 16 + z * 2 + (r - 18) // 3
    gain = 192 + (r - 24)
    src = jnp.where(r < 8, up, jnp.where(r < 16, down, jnp.where(r < 18, o, jnp.where(r < 24, qkv, gain))))
    pick = jnp.where((lane == src) & (r < 26), 1.0, 0.0).astype(BF16)
    out[...] = nn(pick, acc).astype(BF16).reshape(8, 32, D)


def reduce_z_kernel(got, up, down, o, qkv, gain, acc_s):
    acc = got[0].astype(F32)
    for j in range(1, 8):
        acc = acc + got[j].astype(F32)
    acc_s[...] = acc * (1.0 / math.sqrt(GRID_ROWS * GRID_COLS))
    at = 0
    for ref, rows in ((up, 8), (down, 8), (o, 2), (qkv, 6)):
        for r in range(rows):
            for j in range(4):
                ref[4 * r + j : 4 * r + j + 1, :] = acc_s[at + r : at + r + 1, j * 128 : (j + 1) * 128]
        at += rows
    gain[...] = acc_s[at : at + 2, :]


def call(body, outs, scratch, n_smem, n_in, flops, nbytes, mib):
    smem = pl.BlockSpec(memory_space=pltpu.SMEM)
    vmem = pl.BlockSpec(memory_space=pltpu.VMEM)
    return pl.pallas_call(
        body,
        out_shape=[jax.ShapeDtypeStruct(s, d) for s, d in outs],
        in_specs=[smem] * n_smem + [vmem] * n_in,
        out_specs=[vmem] * len(outs),
        scratch_shapes=scratch,
        compiler_params=pltpu.CompilerParams(vmem_limit_bytes=mib * 1024 * 1024),
        cost_estimate=pl.CostEstimate(flops=flops, bytes_accessed=nbytes, transcendentals=0),
    )


def shift(step):
    pairs = []
    for k in range(256):
        c = k % N_COL
        if step in (1, -1):
            if 0 <= c + step < N_COL:
                pairs.append((k, k + step))
        elif 0 <= k + step < 256:
            pairs.append((k, k + step))
    return pairs


CORE_SWAP = [(k, k ^ 1) for k in range(256)]
XY_GROUPS = [[zh * 128 + x * 32 + y * 8 + zl * 2 + c for x in range(4) for y in range(4)] for zh in range(2) for zl in range(4) for c in range(2)]
Z_GROUPS = [[zh * 128 + x * 32 + y * 8 + zl * 2 + c for zh in range(2) for zl in range(4)] for x in range(4) for y in range(4) for c in range(2)]


def send(x, perm):
    return lax.ppermute(x, AXES, perm)


def exchange(x, groups):
    return lax.all_to_all(x, AXES, 0, 0, axis_index_groups=groups, tiled=True)


def per_device(tokens, cotangent, gains, w_qkv, w_out, w_up, w_down, tile_mask):
    row = lax.axis_index("row")
    col = lax.axis_index("col")
    coord = jnp.stack([row, col, row * N_COL + col]).astype(jnp.int32)
    tok = tokens.reshape(TOK, D)
    cot = cotangent.reshape(TOK, D)
    mask = tile_mask.reshape(TILES, WINDOW * WINDOW)

    left = send(tokens[:, COLS - RIM :], shift(1))
    right = send(tokens[:, :RIM], shift(-1))
    (gact,) = call(
        prep_front_kernel, [((TOK, FF), F32)], [], 0, 2, 2 * TOK * D * FF, 4_000_000, 16,
    )(cot, w_down)
    left, right, gact, mask = lax.optimization_barrier((left, right, gact, mask))
    mid = jnp.concatenate([tokens, left, right, jnp.zeros((ROWS, EC - COLS - 2 * RIM, D), BF16)], axis=1)
    top = send(mid[ROWS - RIM :], shift(N_COL))
    low = send(mid[:RIM], shift(-N_COL))
    bias, pt_u, pt_d = call(
        prep_mask_kernel, [((TILES, QT, KT), F32), ((D, D), BF16), ((D, D), BF16)],
        [], 2, 0, 2 * TOK * D * FF, 4_000_000, 16,
    )(coord, mask)

    half_u, half_d, half_k = ((16, 5, 16, D), BF16), ((16, 2, 32, D), BF16), ((16, 3, 16, D), BF16)
    u_keep, u_send, d_keep, d_send, gm, q, kv, prob, ne, no, gain_mid = call(
        forward_kernel,
        [
            half_u, half_u, half_d, half_d,
            ((TOK, D), BF16), ((TOK, D), BF16), ((EXT, 2 * D), BF16), ((6, 256, KT), F32),
            ((EXT, D), BF16), ((TOK, D), BF16), ((1, D), F32),
        ],
        [pltpu.VMEM((ER, EC, D), BF16), pltpu.VMEM((TOK, D), BF16)], 0, 13, 5_000_000_000, 20_000_000, 30,
    )(mid, top, low, tok, cot, gains, w_qkv, w_out, w_up, gact, bias, pt_u, pt_d)

    u_got = send(u_send, CORE_SWAP)
    d_got = send(d_send, CORE_SWAP)
    k_keep, k_send, g_keep, g_send, gne, gnq = call(
        backward_kernel,
        [half_k, half_k, ((16, D), BF16), ((16, D), BF16), ((EXT, D), F32), ((TOK, D), F32)],
        [pltpu.VMEM((TOK, D), BF16), pltpu.VMEM((EXT, 2 * D), F32)], 0, 14, 3_000_000_000, 12_000_000, 30,
    )(gm, w_out, w_qkv, q, kv, prob, ne, no, mid, top, low, tok, gain_mid, pt_u)
    u_got, d_got, k_send, g_send, gne = lax.optimization_barrier((u_got, d_got, k_send, g_send, gne))

    k_got = send(k_send, CORE_SWAP)
    g_got = send(g_send, CORE_SWAP)
    gne3 = gne.reshape(ER, EC, D)[: ROWS + 2 * RIM]
    to_left = send(gne3[:, COLS : COLS + RIM].astype(BF16), shift(-1)).astype(F32)
    to_right = send(gne3[:, COLS + RIM : COLS + 2 * RIM].astype(BF16), shift(1)).astype(F32)
    gap = COLS - RIM
    own = gne3[:, :COLS]
    own = own + jnp.pad(to_right, ((0, 0), (0, gap), (0, 0))) + jnp.pad(to_left, ((0, 0), (gap, 0), (0, 0)))
    (packed,) = call(
        join_kernel, [((16, 13, 16, D), BF16)], [], 0, 8, 4_000_000, 10_000_000, 30,
    )(u_keep, u_got, d_keep.reshape(16, 4, 16, D), d_got.reshape(16, 4, 16, D), k_keep, k_got, g_keep, g_got)
    packed, own = lax.optimization_barrier((packed, own))
    to_up = send(own[:RIM].astype(BF16), shift(-N_COL)).astype(F32)
    to_down = send(own[RIM + ROWS :].astype(BF16), shift(N_COL)).astype(F32)
    got = exchange(packed, XY_GROUPS)
    (spread,) = call(
        reduce_xy_kernel, [((8, 32, D), BF16)], [], 0, 1, 60_000_000, 4_000_000, 16,
    )(got)
    spread, to_up, to_down = lax.optimization_barrier((spread, to_up, to_down))
    got_z = exchange(spread, Z_GROUPS)
    g_up, g_down, g_out, g_qkv, g_gains = call(
        reduce_z_kernel,
        [((32, 128), F32), ((32, 128), F32), ((8, 128), F32), ((24, 128), F32), ((2, D), F32)],
        [pltpu.VMEM((32, D), F32)], 0, 1, 1_000_000, 400_000, 8,
    )(got_z)

    gap = ROWS - RIM
    gn = own[RIM : RIM + ROWS] + jnp.pad(to_down, ((0, gap), (0, 0), (0, 0))) + jnp.pad(to_up, ((gap, 0), (0, 0), (0, 0)))
    gn = gn + gnq.reshape(ROWS, COLS, D)
    unit, inv = unit_of(tokens.astype(F32))
    g1 = gn * gains[0]
    front = inv * (g1 - unit * jnp.mean(g1 * unit, axis=-1, keepdims=True))
    grad_tokens = (gm.reshape(ROWS, COLS, D).astype(F32) + front).astype(BF16)
    return (grad_tokens, g_qkv.reshape(-1), g_out.reshape(-1), g_up.reshape(-1), g_down.reshape(-1), g_gains)


def solution(mesh):
    block = P("row", "col", None)
    flat = P(("row", "col"))
    return jax.shard_map(
        per_device,
        mesh=mesh,
        in_specs=(block, block, P(), P(), P(), P(), P(), block),
        out_specs=(block, flat, flat, flat, flat, P()),
        check_vma=False,
    )
```

```python
import math

import jax
import jax.numpy as jnp
from jax import lax
from jax.experimental import pallas as pl
from jax.experimental.pallas import tpu as pltpu
from jax.sharding import PartitionSpec as P

D = 512
FF = 2048
HEADS = 8
WINDOW = 7
TILE = 8
RIM = WINDOW // 2
EPS = 1e-06
AXES = ("row", "col")
N_COL = 32
GRID_ROWS = 192
GRID_COLS = 256
ROWS = 24
COLS = 8
TOK = ROWS * COLS
TILES = ROWS // TILE
ER = 32
EC = 16
EXT = ER * EC
QT = TILE * TILE
KT = 256
F32 = jnp.float32
BF16 = jnp.bfloat16
GELU_C = math.sqrt(2.0 / math.pi)


def nn(a, b):
    return lax.dot_general(a, b, (((1,), (0,)), ((), ())), preferred_element_type=F32)


def nt(a, b):
    return lax.dot_general(a, b, (((1,), (1,)), ((), ())), preferred_element_type=F32)


def tn(a, b):
    return lax.dot_general(a, b, (((0,), (0,)), ((), ())), preferred_element_type=F32)


def unit_of(x):
    inv = lax.rsqrt(jnp.mean(x * x, axis=-1, keepdims=True) + EPS)
    return x * inv, inv


def head_mask(rows, h):
    lane = lax.broadcasted_iota(jnp.int32, (rows, 256), 1)
    return (lane // 64) == h


def stack_heads(x):
    zero = jnp.zeros_like(x)
    return jnp.concatenate([jnp.where(head_mask(x.shape[0], h), x, zero) for h in range(4)], axis=0)


def unstack_heads(x):
    rows = x.shape[0] // 4
    out = jnp.where(head_mask(rows, 0), x[:rows], 0.0)
    for h in range(1, 4):
        out = out + jnp.where(head_mask(rows, h), x[h * rows : (h + 1) * rows], 0.0)
    return out


def prep_front_kernel(cot, w_down, gact):
    for c in range(4):
        gact[:, c * 512 : (c + 1) * 512] = nt(cot[...], w_down[c * 512 : (c + 1) * 512, :])


def prep_mask_kernel(coord, mask, bias, pt_u, pt_d):
    q = lax.broadcasted_iota(jnp.int32, (QT, KT), 0)
    k = lax.broadcasted_iota(jnp.int32, (QT, KT), 1)
    ki = k // EC
    kc = k % EC
    odd = coord[1] & 1
    near = kc - COLS + odd * (COLS + RIM)
    far = kc - COLS - RIM + (1 - odd) * (COLS + RIM)
    kj = jnp.where(kc < COLS, kc + RIM, jnp.where(kc < COLS + RIM, near, jnp.where(kc < COLS + 2 * RIM, far, -99)))
    da = ki - q // TILE
    db = kj - q % TILE
    slot = jnp.where((da >= 0) & (da < WINDOW) & (db >= 0) & (db < WINDOW), da * WINDOW + db, -1)
    allowed = [jnp.zeros((QT, KT), jnp.int32) for _ in range(TILES)]
    for s in range(WINDOW * WINDOW):
        here = slot == s
        for t in range(TILES):
            allowed[t] = jnp.where(here, mask[t, s], allowed[t])
    gc = coord[1] * COLS + kj - RIM
    for t in range(TILES):
        gr = coord[0] * ROWS + t * TILE + ki - RIM
        ok = (allowed[t] == 1) & (gr >= 0) & (gr < GRID_ROWS) & (gc >= 0) & (gc < GRID_COLS)
        bias[t] = jnp.where(ok, 0.0, -1e30)
    me = coord[2] & 1
    lane = lax.broadcasted_iota(jnp.int32, (512, 512), 1)
    p = lax.broadcasted_iota(jnp.int32, (512, 512), 0)
    co = (p >> 8) ^ me
    k_u = ((p >> 3) & 1) * 128 + ((p >> 4) & 15) * 8 + ((p >> 1) & 3) * 2 + co
    pt_u[...] = jnp.where(lane == k_u * 2 + (p & 1), 1.0, 0.0).astype(BF16)
    k_d = ((p >> 5) & 7) * 8 + ((p >> 3) & 3) * 2 + co
    pt_d[...] = jnp.where(lane == k_d * 8 + (p & 7), 1.0, 0.0).astype(BF16)


def forward_kernel(
    coord, mid, rim_a, rim_b, tok, cot, gains, w_qkv, w_out, w_up, gact, bias, pt_u, pt_d,
    u_keep, u_send, d_keep, d_send, gm_o, q_o, kv_o, p_o, ne_o, no_o, gain_o, text_s, attn_s,
):
    odd = coord[0] & 1
    text_s[pl.ds(odd * (RIM + ROWS), RIM)] = rim_a[...]
    text_s[RIM : RIM + ROWS] = mid[...]
    text_s[pl.ds((1 - odd) * (RIM + ROWS), RIM)] = rim_b[...]
    text_s[ROWS + 2 * RIM :] = jnp.zeros((ER - ROWS - 2 * RIM, EC, D), BF16)
    unit_e, _ = unit_of(text_s[...].reshape(EXT, D).astype(F32))
    ne = (unit_e * gains[0:1, :]).astype(BF16)
    ne_o[...] = ne
    kv_o[...] = nn(ne, w_qkv[:, D:]).astype(BF16)
    xt = tok[...].astype(F32)
    unit_o, _ = unit_of(xt)
    no = (unit_o * gains[0:1, :]).astype(BF16)
    no_o[...] = no
    q_o[...] = nn(no, w_qkv[:, :D]).astype(BF16)
    for t in range(TILES):
        b4 = jnp.concatenate([bias[t]] * 4, axis=0)
        for g in range(2):
            cols = slice(g * 256, (g + 1) * 256)
            vcols = slice(D + g * 256, D + (g + 1) * 256)
            keys = kv_o[t * 128 : t * 128 + KT, cols]
            vals = kv_o[t * 128 : t * 128 + KT, vcols]
            qs = stack_heads(q_o[t * QT : (t + 1) * QT, cols])
            s = nt(qs, keys) * 0.125 + b4
            e = jnp.exp(s - jnp.max(s, axis=-1, keepdims=True))
            prob = e / jnp.sum(e, axis=-1, keepdims=True)
            p_o[t * 2 + g] = prob
            o = nn(prob.astype(BF16), vals)
            attn_s[t * QT : (t + 1) * QT, cols] = unstack_heads(o).astype(BF16)
    attn = attn_s[...]
    mixed = (xt + nn(attn, w_out[...])).astype(BF16)
    um, inv_m = unit_of(mixed.astype(F32))
    nm = (um * gains[1:2, :]).astype(BF16)
    nmt = nt(pt_u[...], nm).astype(BF16)
    gn = jnp.zeros((TOK, D), F32)
    for c in range(4):
        cols = slice(c * 512, (c + 1) * 512)
        pre = nn(nm, w_up[:, cols])
        th = jnp.tanh(GELU_C * (pre + 0.044715 * (pre * pre * pre)))
        half = 0.5 * (1.0 + th)
        act = (pre * half).astype(BF16)
        slope = half + 0.5 * pre * (1.0 - th * th) * (GELU_C * (1.0 + 0.134145 * (pre * pre)))
        gp = (gact[:, cols] * slope).astype(BF16)
        gn = gn + nt(gp, w_up[:, cols])
        gu = nn(nmt, gp).astype(BF16)
        u_keep[:, c] = gu[:256].reshape(16, 16, D)
        u_send[:, c] = gu[256:].reshape(16, 16, D)
        act_t = nt(pt_d[...], act).astype(BF16)
        gd = nn(act_t, cot[...]).astype(BF16)
        for x in range(2):
            lo = (2 * (c & 1) + x) * 4
            d_keep[lo : lo + 4, c >> 1] = gd[x * 128 : x * 128 + 128].reshape(4, 32, D)
            d_send[lo : lo + 4, c >> 1] = gd[256 + x * 128 : 256 + x * 128 + 128].reshape(4, 32, D)
    g = gn * gains[1:2, :]
    gm = (cot[...].astype(F32) + inv_m * (g - um * jnp.mean(g * um, axis=-1, keepdims=True))).astype(BF16)
    gm_o[...] = gm
    gain_o[...] = jnp.sum(gn * um, axis=0, keepdims=True)
    go = nn(nt(pt_u[...], attn).astype(BF16), gm).astype(BF16)
    u_keep[:, 4] = go[:256].reshape(16, 16, D)
    u_send[:, 4] = go[256:].reshape(16, 16, D)


def backward_kernel(
    coord, gm, w_out, w_qkv, q, kv, p_in, ne, no, mid, rim_a, rim_b, tok, gain_mid, pt,
    k_keep, k_send, g_keep, g_send, gne_o, gnq_o, dq_s, dkv_s,
):
    ga = nt(gm[...], w_out[...]).astype(BF16)
    dkv_s[...] = jnp.zeros_like(dkv_s)
    for t in range(TILES):
        for g in range(2):
            cols = slice(g * 256, (g + 1) * 256)
            vcols = slice(D + g * 256, D + (g + 1) * 256)
            rows = slice(t * 128, t * 128 + KT)
            prob = p_in[t * 2 + g]
            gas = stack_heads(ga[t * QT : (t + 1) * QT, cols])
            qs = stack_heads(q[t * QT : (t + 1) * QT, cols])
            gp = nt(gas, kv[rows, vcols])
            inner = jnp.sum(prob * gp, axis=-1, keepdims=True)
            ds = (prob * (gp - inner) * 0.125).astype(BF16)
            dq_s[t * QT : (t + 1) * QT, cols] = unstack_heads(nn(ds, kv[rows, cols])).astype(BF16)
            dkv_s[rows, cols] += tn(ds, qs)
            dkv_s[rows, vcols] += tn(prob.astype(BF16), gas)
    dkv = dkv_s[...].astype(BF16)
    dq = dq_s[...]
    gk = nn(nt(pt[...], ne[...]).astype(BF16), dkv).astype(BF16)
    gq = nn(nt(pt[...], no[...]).astype(BF16), dq).astype(BF16)
    for i, part in enumerate([gq, gk[:, :D], gk[:, D:]]):
        k_keep[:, i] = part[:256].reshape(16, 16, D)
        k_send[:, i] = part[256:].reshape(16, 16, D)
    gne = nt(dkv, w_qkv[:, D:])
    gnq = nt(dq, w_qkv[:, :D])
    gne_o[...] = gne
    gnq_o[...] = gnq
    gain_in = jnp.sum(gnq * unit_of(tok[...].astype(F32))[0], axis=0, keepdims=True)
    odd = coord[0] & 1
    for ref, at in ((rim_a, odd * (RIM + ROWS)), (mid, RIM), (rim_b, (1 - odd) * (RIM + ROWS))):
        size = ref.shape[0] * EC
        unit, _ = unit_of(ref[...].reshape(size, D).astype(F32))
        part = gne_o[pl.ds(pl.multiple_of(at * EC, EC), size), :]
        gain_in = gain_in + jnp.sum(part * unit, axis=0, keepdims=True)
    spread = jnp.concatenate([gain_in, gain_mid[...], jnp.zeros((14, D), F32)], axis=0).astype(BF16)
    g_keep[...] = spread
    g_send[...] = spread


def join_kernel(uk, ur, dk, dr, kk, kr, gk, gr, out):
    at = 0
    for a, b in ((uk, ur), (dk, dr), (kk, kr)):
        n = a.shape[1]
        out[:, at : at + n] = (a[...].astype(F32) + b[...].astype(F32)).astype(BF16)
        at += n
    gain = (gk[...].astype(F32) + gr[...].astype(F32)).astype(BF16)
    for j in range(16):
        out[j, at] = gain


def reduce_xy_kernel(got, out):
    rows = 13 * 16
    acc = got[0].reshape(rows, D).astype(F32)
    for j in range(1, 16):
        acc = acc + got[j].reshape(rows, D).astype(F32)
    acc = acc.astype(BF16)
    i = lax.broadcasted_iota(jnp.int32, (256, rows), 0)
    lane = lax.broadcasted_iota(jnp.int32, (256, rows), 1)
    z = i // 32
    r = i % 32
    up = (r % 4) * 16 + z * 2 + r // 4
    down = 80 + z * 8 + (r - 8)
    o = 64 + z * 2 + (r - 16)
    qkv = 144 + ((r - 18) % 3) * 16 + z * 2 + (r - 18) // 3
    gain = 192 + (r - 24)
    src = jnp.where(r < 8, up, jnp.where(r < 16, down, jnp.where(r < 18, o, jnp.where(r < 24, qkv, gain))))
    pick = jnp.where((lane == src) & (r < 26), 1.0, 0.0).astype(BF16)
    out[...] = nn(pick, acc).astype(BF16).reshape(8, 32, D)


def reduce_z_kernel(got, up, down, o, qkv, gain, acc_s):
    acc = got[0].astype(F32)
    for j in range(1, 8):
        acc = acc + got[j].astype(F32)
    acc_s[...] = acc * (1.0 / math.sqrt(GRID_ROWS * GRID_COLS))
    at = 0
    for ref, rows in ((up, 8), (down, 8), (o, 2), (qkv, 6)):
        for r in range(rows):
            for j in range(4):
                ref[4 * r + j : 4 * r + j + 1, :] = acc_s[at + r : at + r + 1, j * 128 : (j + 1) * 128]
        at += rows
    gain[...] = acc_s[at : at + 2, :]


def call(body, outs, scratch, n_smem, n_in, flops, nbytes, mib):
    smem = pl.BlockSpec(memory_space=pltpu.SMEM)
    vmem = pl.BlockSpec(memory_space=pltpu.VMEM)
    return pl.pallas_call(
        body,
        out_shape=[jax.ShapeDtypeStruct(s, d) for s, d in outs],
        in_specs=[smem] * n_smem + [vmem] * n_in,
        out_specs=[vmem] * len(outs),
        scratch_shapes=scratch,
        compiler_params=pltpu.CompilerParams(vmem_limit_bytes=mib * 1024 * 1024),
        cost_estimate=pl.CostEstimate(flops=flops, bytes_accessed=nbytes, transcendentals=0),
    )


def pairs(stride, count, first):
    out = []
    for k in range(256):
        at = (k // stride) % count
        other = at + 1 if (at - first) % 2 == 0 else at - 1
        if 0 <= other < count:
            out.append((k, k + (other - at) * stride))
    return out


ROW_A, ROW_B = pairs(N_COL, 8, 1), pairs(N_COL, 8, 0)
COL_A, COL_B = pairs(1, N_COL, 1), pairs(1, N_COL, 0)
CORE_SWAP = [(k, k ^ 1) for k in range(256)]
XY_GROUPS = [[zh * 128 + x * 32 + y * 8 + zl * 2 + c for x in range(4) for y in range(4)] for zh in range(2) for zl in range(4) for c in range(2)]
Z_GROUPS = [[zh * 128 + x * 32 + y * 8 + zl * 2 + c for zh in range(2) for zl in range(4)] for x in range(4) for y in range(4) for c in range(2)]


def send(x, perm):
    return lax.ppermute(x, AXES, perm)


def exchange(x, groups):
    return lax.all_to_all(x, AXES, 0, 0, axis_index_groups=groups, tiled=True)


def per_device(tokens, cotangent, gains, w_qkv, w_out, w_up, w_down, tile_mask):
    row = lax.axis_index("row")
    col = lax.axis_index("col")
    coord = jnp.stack([row, col, row * N_COL + col]).astype(jnp.int32)
    tok = tokens.reshape(TOK, D)
    cot = cotangent.reshape(TOK, D)
    mask = tile_mask.reshape(TILES, WINDOW * WINDOW)

    row_odd = (row & 1) == 1
    col_odd = (col & 1) == 1
    first, last = tokens[:, :RIM], tokens[:, COLS - RIM :]
    side_b = send(jnp.where(col_odd, first, last), COL_B)
    side_a = send(jnp.where(col_odd, last, first), COL_A)
    (gact,) = call(
        prep_front_kernel, [((TOK, FF), F32)], [], 0, 2, 2 * TOK * D * FF, 4_000_000, 16,
    )(cot, w_down)
    side_a, side_b, gact, mask = lax.optimization_barrier((side_a, side_b, gact, mask))
    mid = jnp.concatenate([tokens, side_a, side_b, jnp.zeros((ROWS, EC - COLS - 2 * RIM, D), BF16)], axis=1)
    rim_b = send(jnp.where(row_odd, mid[:RIM], mid[ROWS - RIM :]), ROW_B)
    rim_a = send(jnp.where(row_odd, mid[ROWS - RIM :], mid[:RIM]), ROW_A)
    bias, pt_u, pt_d = call(
        prep_mask_kernel, [((TILES, QT, KT), F32), ((D, D), BF16), ((D, D), BF16)],
        [], 2, 0, 2 * TOK * D * FF, 4_000_000, 16,
    )(coord, mask)

    half_u, half_d, half_k = ((16, 5, 16, D), BF16), ((16, 2, 32, D), BF16), ((16, 3, 16, D), BF16)
    u_keep, u_send, d_keep, d_send, gm, q, kv, prob, ne, no, gain_mid = call(
        forward_kernel,
        [
            half_u, half_u, half_d, half_d,
            ((TOK, D), BF16), ((TOK, D), BF16), ((EXT, 2 * D), BF16), ((6, 256, KT), F32),
            ((EXT, D), BF16), ((TOK, D), BF16), ((1, D), F32),
        ],
        [pltpu.VMEM((ER, EC, D), BF16), pltpu.VMEM((TOK, D), BF16)], 1, 13, 5_000_000_000, 20_000_000, 30,
    )(coord, mid, rim_a, rim_b, tok, cot, gains, w_qkv, w_out, w_up, gact, bias, pt_u, pt_d)

    u_got = send(u_send, CORE_SWAP)
    d_got = send(d_send, CORE_SWAP)
    k_keep, k_send, g_keep, g_send, gne, gnq = call(
        backward_kernel,
        [half_k, half_k, ((16, D), BF16), ((16, D), BF16), ((EXT, D), F32), ((TOK, D), F32)],
        [pltpu.VMEM((TOK, D), BF16), pltpu.VMEM((EXT, 2 * D), F32)], 1, 14, 3_000_000_000, 12_000_000, 30,
    )(coord, gm, w_out, w_qkv, q, kv, prob, ne, no, mid, rim_a, rim_b, tok, gain_mid, pt_u)
    u_got, d_got, k_send, g_send = lax.optimization_barrier((u_got, d_got, k_send, g_send))

    k_got = send(k_send, CORE_SWAP)
    g_got = send(g_send, CORE_SWAP)
    (packed,) = call(
        join_kernel, [((16, 13, 16, D), BF16)], [], 0, 8, 4_000_000, 10_000_000, 30,
    )(u_keep, u_got, d_keep.reshape(16, 4, 16, D), d_got.reshape(16, 4, 16, D), k_keep, k_got, g_keep, g_got)
    packed, gne = lax.optimization_barrier((packed, gne))
    got = exchange(packed, XY_GROUPS)
    (spread,) = call(
        reduce_xy_kernel, [((8, 32, D), BF16)], [], 0, 1, 60_000_000, 4_000_000, 16,
    )(got)
    got_z = exchange(spread, Z_GROUPS)
    g_up, g_down, g_out, g_qkv, g_gains = call(
        reduce_z_kernel,
        [((32, 128), F32), ((32, 128), F32), ((8, 128), F32), ((24, 128), F32), ((2, D), F32)],
        [pltpu.VMEM((32, D), F32)], 0, 1, 1_000_000, 400_000, 8,
    )(got_z)

    def place(x, axis, at_end, size):
        gap = size - RIM
        after = [(0, 0)] * 3
        before = [(0, 0)] * 3
        after[axis], before[axis] = (0, gap), (gap, 0)
        x = x.astype(F32)
        return jnp.where(at_end, jnp.pad(x, before), jnp.pad(x, after))

    gne3 = gne.reshape(ER, EC, D)[: ROWS + 2 * RIM]
    back_b = send(gne3[:, COLS + RIM : COLS + 2 * RIM].astype(BF16), COL_B)
    back_a = send(gne3[:, COLS : COLS + RIM].astype(BF16), COL_A)
    own = gne3[:, :COLS] + place(back_a, 1, col_odd, COLS) + place(back_b, 1, ~col_odd, COLS)
    head, tail = own[:RIM].astype(BF16), own[RIM + ROWS :].astype(BF16)
    up_b = send(jnp.where(row_odd, head, tail), ROW_B)
    up_a = send(jnp.where(row_odd, tail, head), ROW_A)
    gn = own[RIM : RIM + ROWS] + place(up_a, 0, row_odd, ROWS) + place(up_b, 0, ~row_odd, ROWS)
    gn = gn + gnq.reshape(ROWS, COLS, D)
    unit, inv = unit_of(tokens.astype(F32))
    g1 = gn * gains[0]
    front = inv * (g1 - unit * jnp.mean(g1 * unit, axis=-1, keepdims=True))
    grad_tokens = (gm.reshape(ROWS, COLS, D).astype(F32) + front).astype(BF16)
    return (grad_tokens, g_qkv.reshape(-1), g_out.reshape(-1), g_up.reshape(-1), g_down.reshape(-1), g_gains)


def solution(mesh):
    block = P("row", "col", None)
    flat = P(("row", "col"))
    return jax.shard_map(
        per_device,
        mesh=mesh,
        in_specs=(block, block, P(), P(), P(), P(), P(), block),
        out_specs=(block, flat, flat, flat, flat, P()),
        check_vma=False,
    )
```

```python
import math

import jax
import jax.numpy as jnp
from jax import lax
from jax.experimental import pallas as pl
from jax.experimental.pallas import tpu as pltpu
from jax.sharding import PartitionSpec as P

D = 512
FF = 2048
HEADS = 8
WINDOW = 7
TILE = 8
RIM = WINDOW // 2
EPS = 1e-06
AXES = ("row", "col")
N_COL = 32
GRID_ROWS = 192
GRID_COLS = 256
ROWS = 24
COLS = 8
TOK = ROWS * COLS
TILES = ROWS // TILE
ER = 32
EC = 16
EXT = ER * EC
QT = TILE * TILE
KT = 256
F32 = jnp.float32
BF16 = jnp.bfloat16
GELU_C = math.sqrt(2.0 / math.pi)


def nn(a, b):
    return lax.dot_general(a, b, (((1,), (0,)), ((), ())), preferred_element_type=F32)


def nt(a, b):
    return lax.dot_general(a, b, (((1,), (1,)), ((), ())), preferred_element_type=F32)


def tn(a, b):
    return lax.dot_general(a, b, (((0,), (0,)), ((), ())), preferred_element_type=F32)


def unit_of(x):
    inv = lax.rsqrt(jnp.mean(x * x, axis=-1, keepdims=True) + EPS)
    return x * inv, inv


def head_mask(rows, h):
    lane = lax.broadcasted_iota(jnp.int32, (rows, 256), 1)
    return (lane // 64) == h


def stack_heads(x):
    zero = jnp.zeros_like(x)
    return jnp.concatenate([jnp.where(head_mask(x.shape[0], h), x, zero) for h in range(4)], axis=0)


def unstack_heads(x):
    rows = x.shape[0] // 4
    out = jnp.where(head_mask(rows, 0), x[:rows], 0.0)
    for h in range(1, 4):
        out = out + jnp.where(head_mask(rows, h), x[h * rows : (h + 1) * rows], 0.0)
    return out


def prep_front_kernel(cot, w_down, gact):
    for c in range(4):
        gact[:, c * 512 : (c + 1) * 512] = nt(cot[...], w_down[c * 512 : (c + 1) * 512, :])


def prep_mask_kernel(coord, mask, bias, pt_u, pt_k, pt_d):
    q = lax.broadcasted_iota(jnp.int32, (QT, KT), 0)
    k = lax.broadcasted_iota(jnp.int32, (QT, KT), 1)
    ki = k // EC
    kc = k % EC
    odd = coord[1] & 1
    near = kc - COLS + odd * (COLS + RIM)
    far = kc - COLS - RIM + (1 - odd) * (COLS + RIM)
    kj = jnp.where(kc < COLS, kc + RIM, jnp.where(kc < COLS + RIM, near, jnp.where(kc < COLS + 2 * RIM, far, -99)))
    da = ki - q // TILE
    db = kj - q % TILE
    slot = jnp.where((da >= 0) & (da < WINDOW) & (db >= 0) & (db < WINDOW), da * WINDOW + db, -1)
    allowed = [jnp.zeros((QT, KT), jnp.int32) for _ in range(TILES)]
    for s in range(WINDOW * WINDOW):
        here = slot == s
        for t in range(TILES):
            allowed[t] = jnp.where(here, mask[t, s], allowed[t])
    gc = coord[1] * COLS + kj - RIM
    for t in range(TILES):
        gr = coord[0] * ROWS + t * TILE + ki - RIM
        ok = (allowed[t] == 1) & (gr >= 0) & (gr < GRID_ROWS) & (gc >= 0) & (gc < GRID_COLS)
        bias[t] = jnp.where(ok, 0.0, -1e30)
    me = coord[2]
    lane = lax.broadcasted_iota(jnp.int32, (512, 512), 1)
    p = lax.broadcasted_iota(jnp.int32, (512, 512), 0)
    core_z = ((p >> 3) & 1) * 128 + ((p >> 1) & 3) * 2 + (p >> 8)
    hi, lo = (p >> 6) & 3, (p >> 4) & 3
    here = me & 121
    pt_u[...] = jnp.where(lane == ((core_z + hi * 32 + lo * 8) ^ here) * 2 + (p & 1), 1.0, 0.0).astype(BF16)
    pt_k[...] = jnp.where(lane == ((core_z + hi * 8 + lo * 32) ^ here) * 2 + (p & 1), 1.0, 0.0).astype(BF16)
    k_d = (((p >> 5) & 1) * 32 + ((p >> 6) & 3) * 8 + ((p >> 3) & 3) * 2 + (p >> 8)) ^ (me & 57)
    pt_d[...] = jnp.where(lane == k_d * 8 + (p & 7), 1.0, 0.0).astype(BF16)


def forward_kernel(
    coord, mid, rim_a, rim_b, tok, cot, gains, w_qkv, w_out, w_up, gact, bias, pt_u, pt_d,
    u_keep, u_send, d_keep, d_send, gm_o, q_o, kv_o, p_o, ne_o, no_o, gain_o, text_s, attn_s,
):
    odd = coord[0] & 1
    text_s[pl.ds(odd * (RIM + ROWS), RIM)] = rim_a[...]
    text_s[RIM : RIM + ROWS] = mid[...]
    text_s[pl.ds((1 - odd) * (RIM + ROWS), RIM)] = rim_b[...]
    text_s[ROWS + 2 * RIM :] = jnp.zeros((ER - ROWS - 2 * RIM, EC, D), BF16)
    unit_e, _ = unit_of(text_s[...].reshape(EXT, D).astype(F32))
    ne = (unit_e * gains[0:1, :]).astype(BF16)
    ne_o[...] = ne
    kv_o[...] = nn(ne, w_qkv[:, D:]).astype(BF16)
    xt = tok[...].astype(F32)
    unit_o, _ = unit_of(xt)
    no = (unit_o * gains[0:1, :]).astype(BF16)
    no_o[...] = no
    q_o[...] = nn(no, w_qkv[:, :D]).astype(BF16)
    for t in range(TILES):
        b4 = jnp.concatenate([bias[t]] * 4, axis=0)
        for g in range(2):
            cols = slice(g * 256, (g + 1) * 256)
            vcols = slice(D + g * 256, D + (g + 1) * 256)
            keys = kv_o[t * 128 : t * 128 + KT, cols]
            vals = kv_o[t * 128 : t * 128 + KT, vcols]
            qs = stack_heads(q_o[t * QT : (t + 1) * QT, cols])
            s = nt(qs, keys) * 0.125 + b4
            e = jnp.exp(s - jnp.max(s, axis=-1, keepdims=True))
            prob = e / jnp.sum(e, axis=-1, keepdims=True)
            p_o[t * 2 + g] = prob
            o = nn(prob.astype(BF16), vals)
            attn_s[t * QT : (t + 1) * QT, cols] = unstack_heads(o).astype(BF16)
    attn = attn_s[...]
    mixed = (xt + nn(attn, w_out[...])).astype(BF16)
    um, inv_m = unit_of(mixed.astype(F32))
    nm = (um * gains[1:2, :]).astype(BF16)
    nmt = nt(pt_u[...], nm).astype(BF16)
    gn = jnp.zeros((TOK, D), F32)
    for c in range(4):
        cols = slice(c * 512, (c + 1) * 512)
        pre = nn(nm, w_up[:, cols])
        th = jnp.tanh(GELU_C * (pre + 0.044715 * (pre * pre * pre)))
        half = 0.5 * (1.0 + th)
        act = (pre * half).astype(BF16)
        slope = half + 0.5 * pre * (1.0 - th * th) * (GELU_C * (1.0 + 0.134145 * (pre * pre)))
        gp = (gact[:, cols] * slope).astype(BF16)
        gn = gn + nt(gp, w_up[:, cols])
        gu = nn(nmt, gp).astype(BF16)
        u_keep[:, c] = gu[:256].reshape(16, 16, D)
        u_send[:, c] = gu[256:].reshape(16, 16, D)
        act_t = nt(pt_d[...], act).astype(BF16)
        gd = nn(act_t, cot[...]).astype(BF16)
        xh = (c & 1) ^ ((coord[2] >> 6) & 1)
        for y in range(4):
            for xl in range(2):
                at = (y * 2 + xl) * 32
                d_keep[y, xh * 2 + xl, c >> 1] = gd[at : at + 32]
                d_send[y, xh * 2 + xl, c >> 1] = gd[256 + at : 256 + at + 32]
    g = gn * gains[1:2, :]
    gm = (cot[...].astype(F32) + inv_m * (g - um * jnp.mean(g * um, axis=-1, keepdims=True))).astype(BF16)
    gm_o[...] = gm
    gain_o[...] = jnp.sum(gn * um, axis=0, keepdims=True)
    go = nn(nt(pt_u[...], attn).astype(BF16), gm).astype(BF16)
    u_keep[:, 4] = go[:256].reshape(16, 16, D)
    u_send[:, 4] = go[256:].reshape(16, 16, D)


def backward_kernel(
    coord, gm, w_out, w_qkv, q, kv, p_in, ne, no, mid, rim_a, rim_b, tok, gain_mid, pt,
    k_keep, k_send, gne_o, gnq_o, dq_s, dkv_s,
):
    ga = nt(gm[...], w_out[...]).astype(BF16)
    dkv_s[...] = jnp.zeros_like(dkv_s)
    for t in range(TILES):
        for g in range(2):
            cols = slice(g * 256, (g + 1) * 256)
            vcols = slice(D + g * 256, D + (g + 1) * 256)
            rows = slice(t * 128, t * 128 + KT)
            prob = p_in[t * 2 + g]
            gas = stack_heads(ga[t * QT : (t + 1) * QT, cols])
            qs = stack_heads(q[t * QT : (t + 1) * QT, cols])
            gp = nt(gas, kv[rows, vcols])
            inner = jnp.sum(prob * gp, axis=-1, keepdims=True)
            ds = (prob * (gp - inner) * 0.125).astype(BF16)
            dq_s[t * QT : (t + 1) * QT, cols] = unstack_heads(nn(ds, kv[rows, cols])).astype(BF16)
            dkv_s[rows, cols] += tn(ds, qs)
            dkv_s[rows, vcols] += tn(prob.astype(BF16), gas)
    dkv = dkv_s[...].astype(BF16)
    dq = dq_s[...]
    gk = nn(nt(pt[...], ne[...]).astype(BF16), dkv).astype(BF16)
    gq = nn(nt(pt[...], no[...]).astype(BF16), dq).astype(BF16)
    for i, part in enumerate([gq, gk[:, :D], gk[:, D:]]):
        for j in range(16):
            k_keep[j * 3 + i] = part[j * 16 : j * 16 + 16]
            k_send[j * 3 + i] = part[256 + j * 16 : 256 + j * 16 + 16]
    gne = nt(dkv, w_qkv[:, D:])
    gnq = nt(dq, w_qkv[:, :D])
    gne_o[...] = gne
    gnq_o[...] = gnq
    gain_in = jnp.sum(gnq * unit_of(tok[...].astype(F32))[0], axis=0, keepdims=True)
    odd = coord[0] & 1
    for ref, at in ((rim_a, odd * (RIM + ROWS)), (mid, RIM), (rim_b, (1 - odd) * (RIM + ROWS))):
        size = ref.shape[0] * EC
        unit, _ = unit_of(ref[...].reshape(size, D).astype(F32))
        part = gne_o[pl.ds(pl.multiple_of(at * EC, EC), size), :]
        gain_in = gain_in + jnp.sum(part * unit, axis=0, keepdims=True)
    spread = jnp.concatenate([gain_in, gain_mid[...], jnp.zeros((14, D), F32)], axis=0).astype(BF16)
    k_keep[48] = spread
    k_send[48] = spread


def add2(a, b):
    return (a.astype(F32) + b.astype(F32)).astype(BF16)


def add4(parts):
    a, b, c, d = [v.astype(F32) for v in parts]
    return ((a + b) + (c + d)).astype(BF16)


def join_pair_kernel(keep, got, *outs):
    n = keep.shape[0] // 4
    for d in range(4):
        outs[d][...] = add2(keep[d * n : (d + 1) * n], got[d * n : (d + 1) * n])


def join_qkv_kernel(keep, got, *outs):
    gain = add2(keep[48], got[48])
    for d in range(4):
        outs[d][:12] = add2(keep[d * 12 : (d + 1) * 12], got[d * 12 : (d + 1) * 12])
        outs[d][12] = gain


def join_four_kernel(*refs):
    parts, outs = refs[:4], refs[4:]
    n = outs[0].shape[0]
    for d in range(4):
        outs[d][...] = add4([r[d * n : (d + 1) * n] for r in parts])


def join_four_qkv_kernel(*refs):
    parts, outs = refs[:4], refs[4:]
    gain = add4([r[12] for r in parts])
    for d in range(4):
        outs[d][:3] = add4([r[d * 3 : (d + 1) * 3] for r in parts])
        outs[d][3] = gain


def reduce_xy_kernel(*refs):
    out = refs[12]
    sums = [add4([r[...] for r in refs[i : i + 4]]).reshape(-1, D) for i in (0, 4, 8)]
    acc = jnp.concatenate(sums, axis=0)
    rows = acc.shape[0]
    i = lax.broadcasted_iota(jnp.int32, (256, rows), 0)
    lane = lax.broadcasted_iota(jnp.int32, (256, rows), 1)
    z = i // 32
    r = i % 32
    up = (r % 4) * 16 + z * 2 + r // 4
    down = 80 + z * 8 + (r - 8)
    o = 64 + z * 2 + (r - 16)
    qkv = 144 + ((r - 18) % 3) * 16 + z * 2 + (r - 18) // 3
    gain = 192 + (r - 24)
    src = jnp.where(r < 8, up, jnp.where(r < 16, down, jnp.where(r < 18, o, jnp.where(r < 24, qkv, gain))))
    pick = jnp.where((lane == src) & (r < 26), 1.0, 0.0).astype(BF16)
    out[...] = nn(pick, acc).astype(BF16).reshape(8, 32, D)


def reduce_z_kernel(got, up, down, o, qkv, gain, acc_s):
    acc = got[0].astype(F32)
    for j in range(1, 8):
        acc = acc + got[j].astype(F32)
    acc_s[...] = acc * (1.0 / math.sqrt(GRID_ROWS * GRID_COLS))
    at = 0
    for ref, rows in ((up, 8), (down, 8), (o, 2), (qkv, 6)):
        for r in range(rows):
            for j in range(4):
                ref[4 * r + j : 4 * r + j + 1, :] = acc_s[at + r : at + r + 1, j * 128 : (j + 1) * 128]
        at += rows
    gain[...] = acc_s[at : at + 2, :]


def call(body, outs, scratch, n_smem, n_in, flops, nbytes, mib):
    smem = pl.BlockSpec(memory_space=pltpu.SMEM)
    vmem = pl.BlockSpec(memory_space=pltpu.VMEM)
    return pl.pallas_call(
        body,
        out_shape=[jax.ShapeDtypeStruct(s, d) for s, d in outs],
        in_specs=[smem] * n_smem + [vmem] * n_in,
        out_specs=[vmem] * len(outs),
        scratch_shapes=scratch,
        compiler_params=pltpu.CompilerParams(vmem_limit_bytes=mib * 1024 * 1024),
        cost_estimate=pl.CostEstimate(flops=flops, bytes_accessed=nbytes, transcendentals=0),
    )


def pairs(stride, count, first):
    out = []
    for k in range(256):
        at = (k // stride) % count
        other = at + 1 if (at - first) % 2 == 0 else at - 1
        if 0 <= other < count:
            out.append((k, k + (other - at) * stride))
    return out


ROW_A, ROW_B = pairs(N_COL, 8, 1), pairs(N_COL, 8, 0)
COL_A, COL_B = pairs(1, N_COL, 1), pairs(1, N_COL, 0)
CORE_SWAP = [(k, k ^ 1) for k in range(256)]
X_BIT = 32
Y_BIT = 8
Z_GROUPS = [[zh * 128 + x * 32 + y * 8 + zl * 2 + c for zh in range(2) for zl in range(4)] for x in range(4) for y in range(4) for c in range(2)]


def send(x, perm):
    return lax.ppermute(x, AXES, perm)


def to_three(chunks, bit):
    return [chunks[0]] + [send(chunks[d], [(k, k ^ (bit * d)) for k in range(256)]) for d in (1, 3, 2)]


def exchange(x, groups):
    return lax.all_to_all(x, AXES, 0, 0, axis_index_groups=groups, tiled=True)


def per_device(tokens, cotangent, gains, w_qkv, w_out, w_up, w_down, tile_mask):
    row = lax.axis_index("row")
    col = lax.axis_index("col")
    coord = jnp.stack([row, col, row * N_COL + col]).astype(jnp.int32)
    tok = tokens.reshape(TOK, D)
    cot = cotangent.reshape(TOK, D)
    mask = tile_mask.reshape(TILES, WINDOW * WINDOW)

    row_odd = (row & 1) == 1
    col_odd = (col & 1) == 1
    first, last = tokens[:, :RIM], tokens[:, COLS - RIM :]
    side_b = send(jnp.where(col_odd, first, last), COL_B)
    side_a = send(jnp.where(col_odd, last, first), COL_A)
    bias, pt_u, pt_k, pt_d = call(
        prep_mask_kernel, [((TILES, QT, KT), F32), ((D, D), BF16), ((D, D), BF16), ((D, D), BF16)],
        [], 2, 0, 2 * TOK * D * FF, 4_000_000, 16,
    )(coord, mask)
    side_a, side_b, cot, bias = lax.optimization_barrier((side_a, side_b, cot, bias))
    mid = jnp.concatenate([tokens, side_a, side_b, jnp.zeros((ROWS, EC - COLS - 2 * RIM, D), BF16)], axis=1)
    rim_b = send(jnp.where(row_odd, mid[:RIM], mid[ROWS - RIM :]), ROW_B)
    rim_a = send(jnp.where(row_odd, mid[ROWS - RIM :], mid[:RIM]), ROW_A)
    (gact,) = call(
        prep_front_kernel, [((TOK, FF), F32)], [], 0, 2, 2 * TOK * D * FF, 4_000_000, 16,
    )(cot, w_down)

    half_u, half_d, half_k = ((16, 5, 16, D), BF16), ((4, 4, 2, 32, D), BF16), ((49, 16, D), BF16)
    u_keep, u_send, d_keep, d_send, gm, q, kv, prob, ne, no, gain_mid = call(
        forward_kernel,
        [
            half_u, half_u, half_d, half_d,
            ((TOK, D), BF16), ((TOK, D), BF16), ((EXT, 2 * D), BF16), ((6, 256, KT), F32),
            ((EXT, D), BF16), ((TOK, D), BF16), ((1, D), F32),
        ],
        [pltpu.VMEM((ER, EC, D), BF16), pltpu.VMEM((TOK, D), BF16)], 1, 13, 5_000_000_000, 20_000_000, 30,
    )(coord, mid, rim_a, rim_b, tok, cot, gains, w_qkv, w_out, w_up, gact, bias, pt_u, pt_d)

    u_got = send(u_send, CORE_SWAP)
    d_got = send(d_send, CORE_SWAP)
    k_keep, k_send, gne, gnq = call(
        backward_kernel,
        [half_k, half_k, ((EXT, D), F32), ((TOK, D), F32)],
        [pltpu.VMEM((TOK, D), BF16), pltpu.VMEM((EXT, 2 * D), F32)], 1, 14, 3_000_000_000, 12_000_000, 30,
    )(coord, gm, w_out, w_qkv, q, kv, prob, ne, no, mid, rim_a, rim_b, tok, gain_mid, pt_k)
    u_got, d_got, k_send = lax.optimization_barrier((u_got, d_got, k_send))

    def join(body, ins, blocks):
        outs = [((blocks, 16, D), BF16)] * 4
        return list(call(body, outs, [], 0, len(ins), 1_000_000, 4_000_000, 12)(*ins))

    k_got = send(k_send, CORE_SWAP)
    u = join(join_pair_kernel, [u_keep.reshape(80, 16, D), u_got.reshape(80, 16, D)], 20)
    d = join(join_pair_kernel, [d_keep.reshape(64, 16, D), d_got.reshape(64, 16, D)], 16)
    u1 = to_three(u, X_BIT)
    d1 = to_three(d, Y_BIT)
    k_got, u[0], d[0] = lax.optimization_barrier((k_got, u[0], d[0]))
    kc = join(join_qkv_kernel, [k_keep, k_got], 13)
    kc[0], gne = lax.optimization_barrier((kc[0], gne))
    k1 = to_three(kc, Y_BIT)
    u1[0], d1[0] = u[0], d[0]
    u = join(join_four_kernel, u1, 5)
    d = join(join_four_kernel, d1, 4)
    u2 = to_three(u, Y_BIT)
    d2 = to_three(d, X_BIT)
    k1[0], u2[0], d2[0] = lax.optimization_barrier((k1[0], u2[0], d2[0]))
    kc = join(join_four_qkv_kernel, k1, 4)
    k2 = to_three(kc, X_BIT)
    (spread,) = call(
        reduce_xy_kernel, [((8, 32, D), BF16)], [], 0, 12, 60_000_000, 4_000_000, 12,
    )(*u2, *d2, *k2)
    got_z = exchange(spread, Z_GROUPS)
    g_up, g_down, g_out, g_qkv, g_gains = call(
        reduce_z_kernel,
        [((32, 128), F32), ((32, 128), F32), ((8, 128), F32), ((24, 128), F32), ((2, D), F32)],
        [pltpu.VMEM((32, D), F32)], 0, 1, 1_000_000, 400_000, 8,
    )(got_z)

    def place(x, axis, at_end, size):
        gap = size - RIM
        after = [(0, 0)] * 3
        before = [(0, 0)] * 3
        after[axis], before[axis] = (0, gap), (gap, 0)
        x = x.astype(F32)
        return jnp.where(at_end, jnp.pad(x, before), jnp.pad(x, after))

    gne3 = gne.reshape(ER, EC, D)[: ROWS + 2 * RIM]
    back_b = send(gne3[:, COLS + RIM : COLS + 2 * RIM].astype(BF16), COL_B)
    back_a = send(gne3[:, COLS : COLS + RIM].astype(BF16), COL_A)
    own = gne3[:, :COLS] + place(back_a, 1, col_odd, COLS) + place(back_b, 1, ~col_odd, COLS)
    head, tail = own[:RIM].astype(BF16), own[RIM + ROWS :].astype(BF16)
    up_b = send(jnp.where(row_odd, head, tail), ROW_B)
    up_a = send(jnp.where(row_odd, tail, head), ROW_A)
    gn = own[RIM : RIM + ROWS] + place(up_a, 0, row_odd, ROWS) + place(up_b, 0, ~row_odd, ROWS)
    gn = gn + gnq.reshape(ROWS, COLS, D)
    unit, inv = unit_of(tokens.astype(F32))
    g1 = gn * gains[0]
    front = inv * (g1 - unit * jnp.mean(g1 * unit, axis=-1, keepdims=True))
    grad_tokens = (gm.reshape(ROWS, COLS, D).astype(F32) + front).astype(BF16)
    return (grad_tokens, g_qkv.reshape(-1), g_out.reshape(-1), g_up.reshape(-1), g_down.reshape(-1), g_gains)


def solution(mesh):
    block = P("row", "col", None)
    flat = P(("row", "col"))
    return jax.shard_map(
        per_device,
        mesh=mesh,
        in_specs=(block, block, P(), P(), P(), P(), P(), block),
        out_specs=(block, flat, flat, flat, flat, P()),
        check_vma=False,
    )
```

```python
import math

import jax
import jax.numpy as jnp
from jax import lax
from jax.experimental import pallas as pl
from jax.experimental.pallas import tpu as pltpu
from jax.sharding import PartitionSpec as P

D = 512
FF = 2048
HEADS = 8
WINDOW = 7
TILE = 8
RIM = WINDOW // 2
EPS = 1e-06
AXES = ("row", "col")
N_COL = 32
GRID_ROWS = 192
GRID_COLS = 256
ROWS = 24
COLS = 8
TOK = ROWS * COLS
TILES = ROWS // TILE
ER = 32
EC = 16
EXT = ER * EC
QT = TILE * TILE
KT = 256
F32 = jnp.float32
BF16 = jnp.bfloat16
GELU_C = math.sqrt(2.0 / math.pi)


def nn(a, b):
    return lax.dot_general(a, b, (((1,), (0,)), ((), ())), preferred_element_type=F32)


def nt(a, b):
    return lax.dot_general(a, b, (((1,), (1,)), ((), ())), preferred_element_type=F32)


def tn(a, b):
    return lax.dot_general(a, b, (((0,), (0,)), ((), ())), preferred_element_type=F32)


def unit_of(x):
    inv = lax.rsqrt(jnp.mean(x * x, axis=-1, keepdims=True) + EPS)
    return x * inv, inv


def head_mask(rows, h):
    lane = lax.broadcasted_iota(jnp.int32, (rows, 256), 1)
    return (lane // 64) == h


def stack_heads(x):
    zero = jnp.zeros_like(x)
    return jnp.concatenate([jnp.where(head_mask(x.shape[0], h), x, zero) for h in range(4)], axis=0)


def unstack_heads(x):
    rows = x.shape[0] // 4
    out = jnp.where(head_mask(rows, 0), x[:rows], 0.0)
    for h in range(1, 4):
        out = out + jnp.where(head_mask(rows, h), x[h * rows : (h + 1) * rows], 0.0)
    return out


def prep_front_kernel(cot, w_down, gact):
    for c in range(4):
        gact[:, c * 512 : (c + 1) * 512] = nt(cot[...], w_down[c * 512 : (c + 1) * 512, :])


def prep_mask_kernel(coord, mask, bias, pt_u, pt_k, pt_d):
    q = lax.broadcasted_iota(jnp.int32, (QT, KT), 0)
    k = lax.broadcasted_iota(jnp.int32, (QT, KT), 1)
    ki = k // EC
    kc = k % EC
    odd = coord[1] & 1
    near = kc - COLS + odd * (COLS + RIM)
    far = kc - COLS - RIM + (1 - odd) * (COLS + RIM)
    kj = jnp.where(kc < COLS, kc + RIM, jnp.where(kc < COLS + RIM, near, jnp.where(kc < COLS + 2 * RIM, far, -99)))
    da = ki - q // TILE
    db = kj - q % TILE
    slot = jnp.where((da >= 0) & (da < WINDOW) & (db >= 0) & (db < WINDOW), da * WINDOW + db, -1)
    allowed = [jnp.zeros((QT, KT), jnp.int32) for _ in range(TILES)]
    for s in range(WINDOW * WINDOW):
        here = slot == s
        for t in range(TILES):
            allowed[t] = jnp.where(here, mask[t, s], allowed[t])
    gc = coord[1] * COLS + kj - RIM
    for t in range(TILES):
        gr = coord[0] * ROWS + t * TILE + ki - RIM
        ok = (allowed[t] == 1) & (gr >= 0) & (gr < GRID_ROWS) & (gc >= 0) & (gc < GRID_COLS)
        bias[t] = jnp.where(ok, 0.0, -1e30)
    me = coord[2]
    lane = lax.broadcasted_iota(jnp.int32, (512, 512), 1)
    p = lax.broadcasted_iota(jnp.int32, (512, 512), 0)
    core_z = ((p >> 3) & 1) * 128 + ((p >> 1) & 3) * 2 + (p >> 8)
    hi, lo = (p >> 6) & 3, (p >> 4) & 3
    here = me & 121
    pt_u[...] = jnp.where(lane == ((core_z + hi * 32 + lo * 8) ^ (me & 1)) * 2 + (p & 1), 1.0, 0.0).astype(BF16)
    pt_k[...] = jnp.where(lane == ((core_z + hi * 8 + lo * 32) ^ here) * 2 + (p & 1), 1.0, 0.0).astype(BF16)
    k_d = (((p >> 5) & 1) * 32 + ((p >> 6) & 3) * 8 + ((p >> 3) & 3) * 2 + (p >> 8)) ^ (me & 57)
    pt_d[...] = jnp.where(lane == k_d * 8 + (p & 7), 1.0, 0.0).astype(BF16)


def forward_kernel(
    coord, mid, rim_a, rim_b, tok, cot, gains, w_qkv, w_out, w_up, gact, bias, pt_u, pt_d,
    u_keep, u_send, d_keep, d_send, gm_o, q_o, kv_o, p_o, ne_o, no_o, gain_o, text_s, attn_s,
):
    odd = coord[0] & 1
    text_s[pl.ds(odd * (RIM + ROWS), RIM)] = rim_a[...]
    text_s[RIM : RIM + ROWS] = mid[...]
    text_s[pl.ds((1 - odd) * (RIM + ROWS), RIM)] = rim_b[...]
    text_s[ROWS + 2 * RIM :] = jnp.zeros((ER - ROWS - 2 * RIM, EC, D), BF16)
    unit_e, _ = unit_of(text_s[...].reshape(EXT, D).astype(F32))
    ne = (unit_e * gains[0:1, :]).astype(BF16)
    ne_o[...] = ne
    kv_o[...] = nn(ne, w_qkv[:, D:]).astype(BF16)
    xt = tok[...].astype(F32)
    unit_o, _ = unit_of(xt)
    no = (unit_o * gains[0:1, :]).astype(BF16)
    no_o[...] = no
    q_o[...] = nn(no, w_qkv[:, :D]).astype(BF16)
    for t in range(TILES):
        b4 = jnp.concatenate([bias[t]] * 4, axis=0)
        for g in range(2):
            cols = slice(g * 256, (g + 1) * 256)
            vcols = slice(D + g * 256, D + (g + 1) * 256)
            keys = kv_o[t * 128 : t * 128 + KT, cols]
            vals = kv_o[t * 128 : t * 128 + KT, vcols]
            qs = stack_heads(q_o[t * QT : (t + 1) * QT, cols])
            s = nt(qs, keys) * 0.125 + b4
            e = jnp.exp(s - jnp.max(s, axis=-1, keepdims=True))
            prob = e / jnp.sum(e, axis=-1, keepdims=True)
            p_o[t * 2 + g] = prob
            o = nn(prob.astype(BF16), vals)
            attn_s[t * QT : (t + 1) * QT, cols] = unstack_heads(o).astype(BF16)
    attn = attn_s[...]
    mixed = (xt + nn(attn, w_out[...])).astype(BF16)
    um, inv_m = unit_of(mixed.astype(F32))
    nm = (um * gains[1:2, :]).astype(BF16)
    nmt = nt(pt_u[...], nm).astype(BF16)
    gn = jnp.zeros((TOK, D), F32)
    for c in range(4):
        cols = slice(c * 512, (c + 1) * 512)
        pre = nn(nm, w_up[:, cols])
        th = jnp.tanh(GELU_C * (pre + 0.044715 * (pre * pre * pre)))
        half = 0.5 * (1.0 + th)
        act = (pre * half).astype(BF16)
        slope = half + 0.5 * pre * (1.0 - th * th) * (GELU_C * (1.0 + 0.134145 * (pre * pre)))
        gp = (gact[:, cols] * slope).astype(BF16)
        gn = gn + nt(gp, w_up[:, cols])
        gu = nn(nmt, gp).astype(BF16)
        u_keep[:, c] = gu[:256].reshape(16, 16, D)
        u_send[:, c] = gu[256:].reshape(16, 16, D)
        act_t = nt(pt_d[...], act).astype(BF16)
        gd = nn(act_t, cot[...]).astype(BF16)
        xh = (c & 1) ^ ((coord[2] >> 6) & 1)
        for y in range(4):
            for xl in range(2):
                at = (y * 2 + xl) * 32
                d_keep[y, xh * 2 + xl, c >> 1] = gd[at : at + 32]
                d_send[y, xh * 2 + xl, c >> 1] = gd[256 + at : 256 + at + 32]
    g = gn * gains[1:2, :]
    gm = (cot[...].astype(F32) + inv_m * (g - um * jnp.mean(g * um, axis=-1, keepdims=True))).astype(BF16)
    gm_o[...] = gm
    gain_o[...] = jnp.sum(gn * um, axis=0, keepdims=True)
    go = nn(nt(pt_u[...], attn).astype(BF16), gm).astype(BF16)
    u_keep[:, 4] = go[:256].reshape(16, 16, D)
    u_send[:, 4] = go[256:].reshape(16, 16, D)


def backward_kernel(
    coord, gm, w_out, w_qkv, q, kv, p_in, ne, no, mid, rim_a, rim_b, tok, gain_mid, pt,
    k_keep, k_send, gne_o, gnq_o, dq_s, dkv_s,
):
    ga = nt(gm[...], w_out[...]).astype(BF16)
    dkv_s[...] = jnp.zeros_like(dkv_s)
    for t in range(TILES):
        for g in range(2):
            cols = slice(g * 256, (g + 1) * 256)
            vcols = slice(D + g * 256, D + (g + 1) * 256)
            rows = slice(t * 128, t * 128 + KT)
            prob = p_in[t * 2 + g]
            gas = stack_heads(ga[t * QT : (t + 1) * QT, cols])
            qs = stack_heads(q[t * QT : (t + 1) * QT, cols])
            gp = nt(gas, kv[rows, vcols])
            inner = jnp.sum(prob * gp, axis=-1, keepdims=True)
            ds = (prob * (gp - inner) * 0.125).astype(BF16)
            dq_s[t * QT : (t + 1) * QT, cols] = unstack_heads(nn(ds, kv[rows, cols])).astype(BF16)
            dkv_s[rows, cols] += tn(ds, qs)
            dkv_s[rows, vcols] += tn(prob.astype(BF16), gas)
    dkv = dkv_s[...].astype(BF16)
    dq = dq_s[...]
    gk = nn(nt(pt[...], ne[...]).astype(BF16), dkv).astype(BF16)
    gq = nn(nt(pt[...], no[...]).astype(BF16), dq).astype(BF16)
    for i, part in enumerate([gq, gk[:, :D], gk[:, D:]]):
        for j in range(16):
            k_keep[j * 3 + i] = part[j * 16 : j * 16 + 16]
            k_send[j * 3 + i] = part[256 + j * 16 : 256 + j * 16 + 16]
    gne = nt(dkv, w_qkv[:, D:])
    gnq = nt(dq, w_qkv[:, :D])
    gne_o[...] = gne
    gnq_o[...] = gnq
    gain_in = jnp.sum(gnq * unit_of(tok[...].astype(F32))[0], axis=0, keepdims=True)
    odd = coord[0] & 1
    for ref, at in ((rim_a, odd * (RIM + ROWS)), (mid, RIM), (rim_b, (1 - odd) * (RIM + ROWS))):
        size = ref.shape[0] * EC
        unit, _ = unit_of(ref[...].reshape(size, D).astype(F32))
        part = gne_o[pl.ds(pl.multiple_of(at * EC, EC), size), :]
        gain_in = gain_in + jnp.sum(part * unit, axis=0, keepdims=True)
    spread = jnp.concatenate([gain_in, gain_mid[...], jnp.zeros((14, D), F32)], axis=0).astype(BF16)
    k_keep[48] = spread
    k_send[48] = spread


def add2(a, b):
    return (a.astype(F32) + b.astype(F32)).astype(BF16)


def add4(parts):
    a, b, c, d = [v.astype(F32) for v in parts]
    return ((a + b) + (c + d)).astype(BF16)


def join_pair_kernel(keep, got, out):
    out[...] = add2(keep[...], got[...])


def join_down_qkv_kernel(dk, dg, kk, kg, *outs):
    gain = add2(kk[48], kg[48])
    for d in range(4):
        outs[d][:16] = add2(dk[d * 16 : (d + 1) * 16], dg[d * 16 : (d + 1) * 16])
        outs[d][16:28] = add2(kk[d * 12 : (d + 1) * 12], kg[d * 12 : (d + 1) * 12])
        outs[d][28] = gain


def sum_up_kernel(got, out):
    out[...] = add4([got[d] for d in range(4)])


def sum_down_qkv_kernel(*refs):
    parts, outs = refs[:4], refs[4:]
    gain = add4([r[28] for r in parts])
    for d in range(4):
        outs[d][:4] = add4([r[d * 4 : (d + 1) * 4] for r in parts])
        outs[d][4:7] = add4([r[16 + d * 3 : 16 + (d + 1) * 3] for r in parts])
        outs[d][7] = gain


def reduce_xy_kernel(*refs):
    u_got, out = refs[0], refs[5]
    sums = [add4([u_got[d] for d in range(4)]).reshape(-1, D), add4([r[...] for r in refs[1:5]]).reshape(-1, D)]
    acc = jnp.concatenate(sums, axis=0)
    rows = acc.shape[0]
    i = lax.broadcasted_iota(jnp.int32, (256, rows), 0)
    lane = lax.broadcasted_iota(jnp.int32, (256, rows), 1)
    z = i // 32
    r = i % 32
    up = (r % 4) * 16 + z * 2 + r // 4
    down = 80 + z * 8 + (r - 8)
    o = 64 + z * 2 + (r - 16)
    qkv = 144 + ((r - 18) % 3) * 16 + z * 2 + (r - 18) // 3
    gain = 192 + (r - 24)
    src = jnp.where(r < 8, up, jnp.where(r < 16, down, jnp.where(r < 18, o, jnp.where(r < 24, qkv, gain))))
    pick = jnp.where((lane == src) & (r < 26), 1.0, 0.0).astype(BF16)
    out[...] = nn(pick, acc).astype(BF16).reshape(8, 32, D)


def reduce_z_kernel(got, up, down, o, qkv, gain, acc_s):
    acc = got[0].astype(F32)
    for j in range(1, 8):
        acc = acc + got[j].astype(F32)
    acc_s[...] = acc * (1.0 / math.sqrt(GRID_ROWS * GRID_COLS))
    at = 0
    for ref, rows in ((up, 8), (down, 8), (o, 2), (qkv, 6)):
        for r in range(rows):
            for j in range(4):
                ref[4 * r + j : 4 * r + j + 1, :] = acc_s[at + r : at + r + 1, j * 128 : (j + 1) * 128]
        at += rows
    gain[...] = acc_s[at : at + 2, :]


def call(body, outs, scratch, n_smem, n_in, flops, nbytes, mib):
    smem = pl.BlockSpec(memory_space=pltpu.SMEM)
    vmem = pl.BlockSpec(memory_space=pltpu.VMEM)
    return pl.pallas_call(
        body,
        out_shape=[jax.ShapeDtypeStruct(s, d) for s, d in outs],
        in_specs=[smem] * n_smem + [vmem] * n_in,
        out_specs=[vmem] * len(outs),
        scratch_shapes=scratch,
        compiler_params=pltpu.CompilerParams(vmem_limit_bytes=mib * 1024 * 1024),
        cost_estimate=pl.CostEstimate(flops=flops, bytes_accessed=nbytes, transcendentals=0),
    )


def pairs(stride, count, first):
    out = []
    for k in range(256):
        at = (k // stride) % count
        other = at + 1 if (at - first) % 2 == 0 else at - 1
        if 0 <= other < count:
            out.append((k, k + (other - at) * stride))
    return out


ROW_A, ROW_B = pairs(N_COL, 8, 1), pairs(N_COL, 8, 0)
COL_A, COL_B = pairs(1, N_COL, 1), pairs(1, N_COL, 0)
CORE_SWAP = [(k, k ^ 1) for k in range(256)]
X_BIT = 32
Y_BIT = 8
X_GROUPS = [[zh * 128 + x * 32 + c for x in range(4)] for zh in range(2) for c in range(32)]
Y_GROUPS = [[r * 32 + y * 8 + c for y in range(4)] for r in range(8) for c in range(8)]
Z_GROUPS = [[zh * 128 + x * 32 + y * 8 + zl * 2 + c for zh in range(2) for zl in range(4)] for x in range(4) for y in range(4) for c in range(2)]


def send(x, perm):
    return lax.ppermute(x, AXES, perm)


def to_three(chunks, bit):
    return [chunks[0]] + [send(chunks[d], [(k, k ^ (bit * d)) for k in range(256)]) for d in (1, 3, 2)]


def exchange(x, groups):
    return lax.all_to_all(x, AXES, 0, 0, axis_index_groups=groups, tiled=True)


def per_device(tokens, cotangent, gains, w_qkv, w_out, w_up, w_down, tile_mask):
    row = lax.axis_index("row")
    col = lax.axis_index("col")
    coord = jnp.stack([row, col, row * N_COL + col]).astype(jnp.int32)
    tok = tokens.reshape(TOK, D)
    cot = cotangent.reshape(TOK, D)
    mask = tile_mask.reshape(TILES, WINDOW * WINDOW)

    row_odd = (row & 1) == 1
    col_odd = (col & 1) == 1
    first, last = tokens[:, :RIM], tokens[:, COLS - RIM :]
    side_b = send(jnp.where(col_odd, first, last), COL_B)
    side_a = send(jnp.where(col_odd, last, first), COL_A)
    bias, pt_u, pt_k, pt_d = call(
        prep_mask_kernel, [((TILES, QT, KT), F32), ((D, D), BF16), ((D, D), BF16), ((D, D), BF16)],
        [], 2, 0, 2 * TOK * D * FF, 4_000_000, 8,
    )(coord, mask)
    side_a, side_b, cot, bias = lax.optimization_barrier((side_a, side_b, cot, bias))
    mid = jnp.concatenate([tokens, side_a, side_b, jnp.zeros((ROWS, EC - COLS - 2 * RIM, D), BF16)], axis=1)
    rim_b = send(jnp.where(row_odd, mid[:RIM], mid[ROWS - RIM :]), ROW_B)
    rim_a = send(jnp.where(row_odd, mid[ROWS - RIM :], mid[:RIM]), ROW_A)
    (gact,) = call(
        prep_front_kernel, [((TOK, FF), F32)], [], 0, 2, 2 * TOK * D * FF, 4_000_000, 8,
    )(cot, w_down)

    half_u, half_d, half_k = ((16, 5, 16, D), BF16), ((4, 4, 2, 32, D), BF16), ((49, 16, D), BF16)
    u_keep, u_send, d_keep, d_send, gm, q, kv, prob, ne, no, gain_mid = call(
        forward_kernel,
        [
            half_u, half_u, half_d, half_d,
            ((TOK, D), BF16), ((TOK, D), BF16), ((EXT, 2 * D), BF16), ((6, 256, KT), F32),
            ((EXT, D), BF16), ((TOK, D), BF16), ((1, D), F32),
        ],
        [pltpu.VMEM((ER, EC, D), BF16), pltpu.VMEM((TOK, D), BF16)], 1, 13, 5_000_000_000, 20_000_000, 24,
    )(coord, mid, rim_a, rim_b, tok, cot, gains, w_qkv, w_out, w_up, gact, bias, pt_u, pt_d)

    u_got = send(u_send, CORE_SWAP)
    d_got = send(d_send, CORE_SWAP)
    k_keep, k_send, gne, gnq = call(
        backward_kernel,
        [half_k, half_k, ((EXT, D), F32), ((TOK, D), F32)],
        [pltpu.VMEM((TOK, D), BF16), pltpu.VMEM((EXT, 2 * D), F32)], 1, 14, 3_000_000_000, 12_000_000, 20,
    )(coord, gm, w_out, w_qkv, q, kv, prob, ne, no, mid, rim_a, rim_b, tok, gain_mid, pt_k)
    u_got, d_got, k_send = lax.optimization_barrier((u_got, d_got, k_send))

    def place(x, axis, at_end, size):
        gap = size - RIM
        after = [(0, 0)] * 3
        before = [(0, 0)] * 3
        after[axis], before[axis] = (0, gap), (gap, 0)
        x = x.astype(F32)
        return jnp.where(at_end, jnp.pad(x, before), jnp.pad(x, after))

    gne3 = gne.reshape(ER, EC, D)[: ROWS + 2 * RIM]
    back_b = send(gne3[:, COLS + RIM : COLS + 2 * RIM].astype(BF16), COL_B)
    back_a = send(gne3[:, COLS : COLS + RIM].astype(BF16), COL_A)
    own = gne3[:, :COLS] + place(back_a, 1, col_odd, COLS) + place(back_b, 1, ~col_odd, COLS)

    def join(body, ins, outs):
        return list(call(body, [(o, BF16) for o in outs], [], 0, len(ins), 1_000_000, 4_000_000, 12)(*ins))

    k_got = send(k_send, CORE_SWAP)
    (u,) = join(join_pair_kernel, [u_keep.reshape(80, 16, D), u_got.reshape(80, 16, D)], [(80, 16, D)])
    u, k_got = lax.optimization_barrier((u, k_got))
    u_x = exchange(u.reshape(4, 20, 16, D), X_GROUPS)
    b = join(
        join_down_qkv_kernel, [d_keep.reshape(64, 16, D), d_got.reshape(64, 16, D), k_keep, k_got], [(29, 16, D)] * 4,
    )
    b = to_three(b, Y_BIT)
    u_x, *b = lax.optimization_barrier((u_x, *b))
    (u,) = join(sum_up_kernel, [u_x], [(20, 16, D)])
    b = join(sum_down_qkv_kernel, b, [(8, 16, D)] * 4)
    u, own, *b = lax.optimization_barrier((u, own, *b))
    u_y = exchange(u.reshape(4, 5, 16, D), Y_GROUPS)
    b = to_three(b, X_BIT)
    (spread,) = call(
        reduce_xy_kernel, [((8, 32, D), BF16)], [], 0, 5, 60_000_000, 4_000_000, 12,
    )(u_y, *b)
    got_z = exchange(spread, Z_GROUPS)
    g_up, g_down, g_out, g_qkv, g_gains = call(
        reduce_z_kernel,
        [((32, 128), F32), ((32, 128), F32), ((8, 128), F32), ((24, 128), F32), ((2, D), F32)],
        [pltpu.VMEM((32, D), F32)], 0, 1, 1_000_000, 400_000, 8,
    )(got_z)

    head, tail = own[:RIM].astype(BF16), own[RIM + ROWS :].astype(BF16)
    up_b = send(jnp.where(row_odd, head, tail), ROW_B)
    up_a = send(jnp.where(row_odd, tail, head), ROW_A)
    gn = own[RIM : RIM + ROWS] + place(up_a, 0, row_odd, ROWS) + place(up_b, 0, ~row_odd, ROWS)
    gn = gn + gnq.reshape(ROWS, COLS, D)
    unit, inv = unit_of(tokens.astype(F32))
    g1 = gn * gains[0]
    front = inv * (g1 - unit * jnp.mean(g1 * unit, axis=-1, keepdims=True))
    grad_tokens = (gm.reshape(ROWS, COLS, D).astype(F32) + front).astype(BF16)
    return (grad_tokens, g_qkv.reshape(-1), g_out.reshape(-1), g_up.reshape(-1), g_down.reshape(-1), g_gains)


def solution(mesh):
    block = P("row", "col", None)
    flat = P(("row", "col"))
    return jax.shard_map(
        per_device,
        mesh=mesh,
        in_specs=(block, block, P(), P(), P(), P(), P(), block),
        out_specs=(block, flat, flat, flat, flat, P()),
        check_vma=False,
    )
```

```python
import math

import jax
import jax.numpy as jnp
from jax import lax
from jax.experimental import pallas as pl
from jax.experimental.pallas import tpu as pltpu
from jax.sharding import PartitionSpec as P

D = 512
FF = 2048
HEADS = 8
WINDOW = 7
TILE = 8
RIM = WINDOW // 2
EPS = 1e-06
AXES = ("row", "col")
N_COL = 32
GRID_ROWS = 192
GRID_COLS = 256
ROWS = 24
COLS = 8
TOK = ROWS * COLS
TILES = ROWS // TILE
ER = 32
EC = 16
EXT = ER * EC
QT = TILE * TILE
KT = 256
F32 = jnp.float32
BF16 = jnp.bfloat16
GELU_C = math.sqrt(2.0 / math.pi)


def nn(a, b):
    return lax.dot_general(a, b, (((1,), (0,)), ((), ())), preferred_element_type=F32)


def nt(a, b):
    return lax.dot_general(a, b, (((1,), (1,)), ((), ())), preferred_element_type=F32)


def tn(a, b):
    return lax.dot_general(a, b, (((0,), (0,)), ((), ())), preferred_element_type=F32)


def unit_of(x):
    inv = lax.rsqrt(jnp.mean(x * x, axis=-1, keepdims=True) + EPS)
    return x * inv, inv


def head_mask(rows, h):
    lane = lax.broadcasted_iota(jnp.int32, (rows, 256), 1)
    return (lane // 64) == h


def stack_heads(x):
    zero = jnp.zeros_like(x)
    return jnp.concatenate([jnp.where(head_mask(x.shape[0], h), x, zero) for h in range(4)], axis=0)


def unstack_heads(x):
    rows = x.shape[0] // 4
    out = jnp.where(head_mask(rows, 0), x[:rows], 0.0)
    for h in range(1, 4):
        out = out + jnp.where(head_mask(rows, h), x[h * rows : (h + 1) * rows], 0.0)
    return out


def prep_front_kernel(cot, w_down, gact):
    for c in range(4):
        gact[:, c * 512 : (c + 1) * 512] = nt(cot[...], w_down[c * 512 : (c + 1) * 512, :])


def prep_mask_kernel(coord, mask, bias, pt_u, pt_k, pt_d):
    q = lax.broadcasted_iota(jnp.int32, (QT, KT), 0)
    k = lax.broadcasted_iota(jnp.int32, (QT, KT), 1)
    ki = k // EC
    kc = k % EC
    odd = coord[1] & 1
    near = kc - COLS + odd * (COLS + RIM)
    far = kc - COLS - RIM + (1 - odd) * (COLS + RIM)
    kj = jnp.where(kc < COLS, kc + RIM, jnp.where(kc < COLS + RIM, near, jnp.where(kc < COLS + 2 * RIM, far, -99)))
    da = ki - q // TILE
    db = kj - q % TILE
    slot = jnp.where((da >= 0) & (da < WINDOW) & (db >= 0) & (db < WINDOW), da * WINDOW + db, -1)
    allowed = [jnp.zeros((QT, KT), jnp.int32) for _ in range(TILES)]
    for s in range(WINDOW * WINDOW):
        here = slot == s
        for t in range(TILES):
            allowed[t] = jnp.where(here, mask[t, s], allowed[t])
    gc = coord[1] * COLS + kj - RIM
    for t in range(TILES):
        gr = coord[0] * ROWS + t * TILE + ki - RIM
        ok = (allowed[t] == 1) & (gr >= 0) & (gr < GRID_ROWS) & (gc >= 0) & (gc < GRID_COLS)
        bias[t] = jnp.where(ok, 0.0, -1e30)
    me = coord[2]
    lane = lax.broadcasted_iota(jnp.int32, (512, 512), 1)
    p = lax.broadcasted_iota(jnp.int32, (512, 512), 0)
    core_z = ((p >> 3) & 1) * 128 + ((p >> 1) & 3) * 2 + (p >> 8)
    hi, lo = (p >> 6) & 3, (p >> 4) & 3
    here = me & 121
    pt_u[...] = jnp.where(lane == ((core_z + hi * 32 + lo * 8) ^ here) * 2 + (p & 1), 1.0, 0.0).astype(BF16)
    pt_k[...] = jnp.where(lane == ((core_z + hi * 8 + lo * 32) ^ here) * 2 + (p & 1), 1.0, 0.0).astype(BF16)
    k_d = (((p >> 5) & 1) * 32 + ((p >> 6) & 3) * 8 + ((p >> 3) & 3) * 2 + (p >> 8)) ^ (me & 57)
    pt_d[...] = jnp.where(lane == k_d * 8 + (p & 7), 1.0, 0.0).astype(BF16)


def attend(qt, keys, vals, bias_t):
    s = nt(stack_heads(qt), keys) * 0.125 + jnp.concatenate([bias_t] * 4, axis=0)
    e = jnp.exp(s - jnp.max(s, axis=-1, keepdims=True))
    prob = e / jnp.sum(e, axis=-1, keepdims=True)
    return prob, unstack_heads(nn(prob.astype(BF16), vals)).astype(BF16)


def middle_kernel(mid, tok, gains, w_qkv, bias, q_o, no_o, ne_o, kv_o, p_o, attn_o):
    unit_e, _ = unit_of(mid[...].reshape(ROWS * EC, D).astype(F32))
    ne = (unit_e * gains[0:1, :]).astype(BF16)
    ne_o[...] = ne
    kv_o[...] = nn(ne, w_qkv[:, D:]).astype(BF16)
    unit_o, _ = unit_of(tok[...].astype(F32))
    no = (unit_o * gains[0:1, :]).astype(BF16)
    no_o[...] = no
    q_o[...] = nn(no, w_qkv[:, :D]).astype(BF16)
    at = 128 - RIM * EC
    for g in range(2):
        cols = slice(g * 256, (g + 1) * 256)
        vcols = slice(D + g * 256, D + (g + 1) * 256)
        prob, o = attend(q_o[QT : 2 * QT, cols], kv_o[at : at + KT, cols], kv_o[at : at + KT, vcols], bias[1])
        p_o[g] = prob
        attn_o[:, cols] = o


def forward_kernel(
    coord, rim_a, rim_b, tok, cot, gains, w_qkv, w_out, w_up, gact, bias, pt_u, pt_d, q_i, ne_i, kv_i, attn_i,
    u_keep, u_send, d_keep, d_send, gm_o, kv_o, p_o, ne_o, gain_o, attn_s,
):
    odd = coord[0] & 1
    edge = RIM * EC
    at_a = pl.multiple_of(odd * (RIM + ROWS) * EC, EC)
    at_b = pl.multiple_of((1 - odd) * (RIM + ROWS) * EC, EC)
    end = (RIM + ROWS) * EC
    both = jnp.concatenate([rim_a[...].reshape(edge, D), rim_b[...].reshape(edge, D)], axis=0)
    unit_r, _ = unit_of(both.astype(F32))
    ne_r = (unit_r * gains[0:1, :]).astype(BF16)
    kv_r = nn(ne_r, w_qkv[:, D:]).astype(BF16)
    for ref, mid, rims in ((ne_o, ne_i, ne_r), (kv_o, kv_i, kv_r)):
        ref[edge:end, :] = mid[...]
        ref[pl.ds(at_a, edge), :] = rims[:edge]
        ref[pl.ds(at_b, edge), :] = rims[edge:]
        ref[end + edge :, :] = jnp.zeros((EXT - end - edge, ref.shape[1]), BF16)
    xt = tok[...].astype(F32)
    attn_s[QT : 2 * QT, :] = attn_i[...]
    for i, t in enumerate((0, 2)):
        rows = slice(t * 128, t * 128 + KT)
        for g in range(2):
            cols = slice(g * 256, (g + 1) * 256)
            vcols = slice(D + g * 256, D + (g + 1) * 256)
            prob, o = attend(q_i[t * QT : (t + 1) * QT, cols], kv_o[rows, cols], kv_o[rows, vcols], bias[t])
            p_o[i * 2 + g] = prob
            attn_s[t * QT : (t + 1) * QT, cols] = o
    attn = attn_s[...]
    mixed = (xt + nn(attn, w_out[...])).astype(BF16)
    um, inv_m = unit_of(mixed.astype(F32))
    nm = (um * gains[1:2, :]).astype(BF16)
    nmt = nt(pt_u[...], nm).astype(BF16)
    gn = jnp.zeros((TOK, D), F32)
    for c in range(4):
        cols = slice(c * 512, (c + 1) * 512)
        pre = nn(nm, w_up[:, cols])
        th = jnp.tanh(GELU_C * (pre + 0.044715 * (pre * pre * pre)))
        half = 0.5 * (1.0 + th)
        act = (pre * half).astype(BF16)
        slope = half + 0.5 * pre * (1.0 - th * th) * (GELU_C * (1.0 + 0.134145 * (pre * pre)))
        gp = (gact[:, cols] * slope).astype(BF16)
        gn = gn + nt(gp, w_up[:, cols])
        gu = nn(nmt, gp).astype(BF16)
        u_keep[:, c] = gu[:256].reshape(16, 16, D)
        u_send[:, c] = gu[256:].reshape(16, 16, D)
        act_t = nt(pt_d[...], act).astype(BF16)
        gd = nn(act_t, cot[...]).astype(BF16)
        xh = (c & 1) ^ ((coord[2] >> 6) & 1)
        for y in range(4):
            for xl in range(2):
                at = (y * 2 + xl) * 32
                d_keep[y, xh * 2 + xl, c >> 1] = gd[at : at + 32]
                d_send[y, xh * 2 + xl, c >> 1] = gd[256 + at : 256 + at + 32]
    g = gn * gains[1:2, :]
    gm = (cot[...].astype(F32) + inv_m * (g - um * jnp.mean(g * um, axis=-1, keepdims=True))).astype(BF16)
    gm_o[...] = gm
    gain_o[...] = jnp.sum(gn * um, axis=0, keepdims=True)
    go = nn(nt(pt_u[...], attn).astype(BF16), gm).astype(BF16)
    u_keep[:, 4] = go[:256].reshape(16, 16, D)
    u_send[:, 4] = go[256:].reshape(16, 16, D)


def backward_kernel(
    coord, gm, w_out, w_qkv, q, kv, p_mid, p_out, ne, no, mid, rim_a, rim_b, tok, gain_mid, pt,
    k_keep, k_send, gne_o, gnq_o, dq_s, dkv_s,
):
    ga = nt(gm[...], w_out[...]).astype(BF16)
    dkv_s[...] = jnp.zeros_like(dkv_s)
    for t in range(TILES):
        for g in range(2):
            cols = slice(g * 256, (g + 1) * 256)
            vcols = slice(D + g * 256, D + (g + 1) * 256)
            rows = slice(t * 128, t * 128 + KT)
            prob = p_mid[g] if t == 1 else p_out[t + g]
            gas = stack_heads(ga[t * QT : (t + 1) * QT, cols])
            qs = stack_heads(q[t * QT : (t + 1) * QT, cols])
            gp = nt(gas, kv[rows, vcols])
            inner = jnp.sum(prob * gp, axis=-1, keepdims=True)
            ds = (prob * (gp - inner) * 0.125).astype(BF16)
            dq_s[t * QT : (t + 1) * QT, cols] = unstack_heads(nn(ds, kv[rows, cols])).astype(BF16)
            dkv_s[rows, cols] += tn(ds, qs)
            dkv_s[rows, vcols] += tn(prob.astype(BF16), gas)
    dkv = dkv_s[...].astype(BF16)
    dq = dq_s[...]
    gk = nn(nt(pt[...], ne[...]).astype(BF16), dkv).astype(BF16)
    gq = nn(nt(pt[...], no[...]).astype(BF16), dq).astype(BF16)
    for i, part in enumerate([gq, gk[:, :D], gk[:, D:]]):
        for j in range(16):
            k_keep[j * 3 + i] = part[j * 16 : j * 16 + 16]
            k_send[j * 3 + i] = part[256 + j * 16 : 256 + j * 16 + 16]
    gne = nt(dkv, w_qkv[:, D:])
    gnq = nt(dq, w_qkv[:, :D])
    gne_o[...] = gne[: (ROWS + 2 * RIM) * EC]
    sides = gne.reshape(ER, EC, D)[: ROWS + 2 * RIM, COLS:]
    k_send[49:] = sides.reshape((ROWS + 2 * RIM) * COLS, D).astype(BF16).reshape(15, 16, D)
    gnq_o[...] = gnq
    gain_in = jnp.sum(gnq * unit_of(tok[...].astype(F32))[0], axis=0, keepdims=True)
    odd = coord[0] & 1
    for ref, at in ((rim_a, odd * (RIM + ROWS)), (mid, RIM), (rim_b, (1 - odd) * (RIM + ROWS))):
        size = ref.shape[0] * EC
        unit, _ = unit_of(ref[...].reshape(size, D).astype(F32))
        part = gne_o[pl.ds(pl.multiple_of(at * EC, EC), size), :]
        gain_in = gain_in + jnp.sum(part * unit, axis=0, keepdims=True)
    spread = jnp.concatenate([gain_in, gain_mid[...], jnp.zeros((14, D), F32)], axis=0).astype(BF16)
    k_keep[48] = spread
    k_send[48] = spread


def add2(a, b):
    return (a.astype(F32) + b.astype(F32)).astype(BF16)


def add4(parts):
    a, b, c, d = [v.astype(F32) for v in parts]
    return ((a + b) + (c + d)).astype(BF16)


def join_down_qkv_kernel(dk, dg, kk, kg, *outs):
    gain = add2(kk[48], kg[48])
    for d in range(4):
        outs[d][:16] = add2(dk[d * 16 : (d + 1) * 16], dg[d * 16 : (d + 1) * 16])
        outs[d][16:28] = add2(kk[d * 12 : (d + 1) * 12], kg[d * 12 : (d + 1) * 12])
        outs[d][28] = gain


def join_up_kernel(keep, got, *outs):
    for d in range(4):
        outs[d][...] = add2(keep[d * 20 : (d + 1) * 20], got[d * 20 : (d + 1) * 20])


def sum_up_kernel(*refs):
    parts, outs = refs[:4], refs[4:]
    for d in range(4):
        outs[d][...] = add4([r[d * 5 : (d + 1) * 5] for r in parts])


def sum_down_qkv_kernel(*refs):
    parts, ride, outs = refs[:4], refs[4], refs[5:]
    gain = add4([r[28] for r in parts])
    for d in range(4):
        outs[d][:4] = add4([r[d * 4 : (d + 1) * 4] for r in parts])
        outs[d][4:7] = add4([r[16 + d * 3 : 16 + (d + 1) * 3] for r in parts])
        outs[d][7] = gain
    outs[1][8:10] = ride[...]


def reduce_xy_kernel(*refs):
    out = refs[8]
    sums = [add4([r[...] for r in refs[:4]]).reshape(-1, D), add4([r[:8] for r in refs[4:8]]).reshape(-1, D)]
    acc = jnp.concatenate(sums, axis=0)
    rows = acc.shape[0]
    i = lax.broadcasted_iota(jnp.int32, (256, rows), 0)
    lane = lax.broadcasted_iota(jnp.int32, (256, rows), 1)
    z = i // 32
    r = i % 32
    up = (r % 4) * 16 + z * 2 + r // 4
    down = 80 + z * 8 + (r - 8)
    o = 64 + z * 2 + (r - 16)
    qkv = 144 + ((r - 18) % 3) * 16 + z * 2 + (r - 18) // 3
    gain = 192 + (r - 24)
    src = jnp.where(r < 8, up, jnp.where(r < 16, down, jnp.where(r < 18, o, jnp.where(r < 24, qkv, gain))))
    pick = jnp.where((lane == src) & (r < 26), 1.0, 0.0).astype(BF16)
    out[...] = nn(pick, acc).astype(BF16).reshape(8, 32, D)


def reduce_z_kernel(got, up, down, o, qkv, gain, acc_s):
    acc = got[0].astype(F32)
    for j in range(1, 8):
        acc = acc + got[j].astype(F32)
    acc_s[...] = acc * (1.0 / math.sqrt(GRID_ROWS * GRID_COLS))
    at = 0
    for ref, rows in ((up, 8), (down, 8), (o, 2), (qkv, 6)):
        for r in range(rows):
            for j in range(4):
                ref[4 * r + j : 4 * r + j + 1, :] = acc_s[at + r : at + r + 1, j * 128 : (j + 1) * 128]
        at += rows
    gain[...] = acc_s[at : at + 2, :]


def call(body, outs, scratch, n_smem, n_in, flops, nbytes, mib):
    smem = pl.BlockSpec(memory_space=pltpu.SMEM)
    vmem = pl.BlockSpec(memory_space=pltpu.VMEM)
    return pl.pallas_call(
        body,
        out_shape=[jax.ShapeDtypeStruct(s, d) for s, d in outs],
        in_specs=[smem] * n_smem + [vmem] * n_in,
        out_specs=[vmem] * len(outs),
        scratch_shapes=scratch,
        compiler_params=pltpu.CompilerParams(vmem_limit_bytes=mib * 1024 * 1024),
        cost_estimate=pl.CostEstimate(flops=flops, bytes_accessed=nbytes, transcendentals=0),
    )


def pairs(stride, count, first):
    out = []
    for k in range(256):
        at = (k // stride) % count
        other = at + 1 if (at - first) % 2 == 0 else at - 1
        if 0 <= other < count:
            out.append((k, k + (other - at) * stride))
    return out


ROW_A, ROW_B = pairs(N_COL, 8, 1), pairs(N_COL, 8, 0)
COL_A, COL_B = pairs(1, N_COL, 1), pairs(1, N_COL, 0)
CORE_SWAP = [(k, k ^ 1) for k in range(256)]
X_BIT = 32
Y_BIT = 8
Z_GROUPS = [[zh * 128 + x * 32 + y * 8 + zl * 2 + c for zh in range(2) for zl in range(4)] for x in range(4) for y in range(4) for c in range(2)]


def send(x, perm):
    return lax.ppermute(x, AXES, perm)


def to_three(chunks, bit):
    return [chunks[0]] + [send(chunks[d], [(k, k ^ (bit * d)) for k in range(256)]) for d in (1, 3, 2)]


def exchange(x, groups):
    return lax.all_to_all(x, AXES, 0, 0, axis_index_groups=groups, tiled=True)


def per_device(tokens, cotangent, gains, w_qkv, w_out, w_up, w_down, tile_mask):
    row = lax.axis_index("row")
    col = lax.axis_index("col")
    coord = jnp.stack([row, col, row * N_COL + col]).astype(jnp.int32)
    tok = tokens.reshape(TOK, D)
    cot = cotangent.reshape(TOK, D)
    mask = tile_mask.reshape(TILES, WINDOW * WINDOW)

    row_odd = (row & 1) == 1
    col_odd = (col & 1) == 1
    first, last = tokens[:, :RIM], tokens[:, COLS - RIM :]
    side_b = send(jnp.where(col_odd, first, last), COL_B)
    side_a = send(jnp.where(col_odd, last, first), COL_A)
    bias, pt_u, pt_k, pt_d = call(
        prep_mask_kernel, [((TILES, QT, KT), F32), ((D, D), BF16), ((D, D), BF16), ((D, D), BF16)],
        [], 2, 0, 2 * TOK * D * FF, 4_000_000, 8,
    )(coord, mask)
    side_a, side_b, cot, bias = lax.optimization_barrier((side_a, side_b, cot, bias))
    mid = jnp.concatenate([tokens, side_a, side_b, jnp.zeros((ROWS, EC - COLS - 2 * RIM, D), BF16)], axis=1)
    rim_b = send(jnp.where(row_odd, mid[:RIM], mid[ROWS - RIM :]), ROW_B)
    rim_a = send(jnp.where(row_odd, mid[ROWS - RIM :], mid[:RIM]), ROW_A)
    (gact,) = call(
        prep_front_kernel, [((TOK, FF), F32)], [], 0, 2, 2 * TOK * D * FF, 4_000_000, 8,
    )(cot, w_down)

    q, no, ne_mid, kv_mid, p_mid, attn_mid = call(
        middle_kernel,
        [
            ((TOK, D), BF16), ((TOK, D), BF16), ((ROWS * EC, D), BF16), ((ROWS * EC, 2 * D), BF16),
            ((2, 256, KT), F32), ((QT, D), BF16),
        ],
        [], 0, 5, 600_000_000, 5_000_000, 16,
    )(mid, tok, gains, w_qkv, bias)

    half_u, half_d, half_k = ((16, 5, 16, D), BF16), ((4, 4, 2, 32, D), BF16), ((49, 16, D), BF16)
    u_keep, u_send, d_keep, d_send, gm, kv, p_out, ne, gain_mid = call(
        forward_kernel,
        [
            half_u, half_u, half_d, half_d, ((TOK, D), BF16), ((EXT, 2 * D), BF16), ((4, 256, KT), F32),
            ((EXT, D), BF16), ((1, D), F32),
        ],
        [pltpu.VMEM((TOK, D), BF16)], 1, 16, 4_000_000_000, 20_000_000, 24,
    )(coord, rim_a, rim_b, tok, cot, gains, w_qkv, w_out, w_up, gact, bias, pt_u, pt_d, q, ne_mid, kv_mid, attn_mid)

    u_got = send(u_send, CORE_SWAP)
    d_got = send(d_send, CORE_SWAP)
    k_keep, k_send, gne, gnq = call(
        backward_kernel,
        [half_k, ((64, 16, D), BF16), (((ROWS + 2 * RIM) * EC, D), F32), ((TOK, D), F32)],
        [pltpu.VMEM((TOK, D), BF16), pltpu.VMEM((EXT, 2 * D), F32)], 1, 15, 3_000_000_000, 12_000_000, 20,
    )(coord, gm, w_out, w_qkv, q, kv, p_mid, p_out, ne, no, mid, rim_a, rim_b, tok, gain_mid, pt_k)
    u_got, d_got, k_send = lax.optimization_barrier((u_got, d_got, k_send))

    def place(x, axis, at_end, size):
        gap = size - RIM
        after = [(0, 0)] * 3
        before = [(0, 0)] * 3
        after[axis], before[axis] = (0, gap), (gap, 0)
        x = x.astype(F32)
        return jnp.where(at_end, jnp.pad(x, before), jnp.pad(x, after))

    def join(body, ins, outs):
        return list(call(body, [(o, BF16) for o in outs], [], 0, len(ins), 1_000_000, 4_000_000, 12)(*ins))

    k_got = send(k_send, CORE_SWAP)
    gne3 = gne.reshape(ROWS + 2 * RIM, EC, D)
    back_a = send(gne3[:, COLS : COLS + RIM].astype(BF16), COL_A)
    b = join(
        join_down_qkv_kernel, [d_keep.reshape(64, 16, D), d_got.reshape(64, 16, D), k_keep, k_got], [(29, 16, D)] * 4,
    )
    u_got, *b = lax.optimization_barrier((u_got, *b))
    b = to_three(b, Y_BIT)
    u = join(join_up_kernel, [u_keep.reshape(80, 16, D), u_got.reshape(80, 16, D)], [(20, 16, D)] * 4)
    u = to_three(u, X_BIT)
    back_b = k_got[49:].reshape(ROWS + 2 * RIM, COLS, D)[:, RIM : 2 * RIM]
    own = gne3[:, :COLS] + place(back_a, 1, col_odd, COLS) + place(back_b, 1, ~col_odd, COLS)
    head, tail = own[:RIM].astype(BF16), own[RIM + ROWS :].astype(BF16)
    ride = jnp.pad(jnp.where(row_odd, head, tail), ((0, 1), (0, 0), (0, 0))).reshape(2, 16, D)
    u, b, ride = lax.optimization_barrier((u, b, ride))
    b = join(sum_down_qkv_kernel, [*b, ride], [(8, 16, D), (10, 16, D), (8, 16, D), (8, 16, D)])
    b = to_three(b, X_BIT)
    u = join(sum_up_kernel, u, [(5, 16, D)] * 4)
    u = to_three(u, Y_BIT)
    up_b = b[1][8:].reshape(4, COLS, D)[:RIM]
    (spread,) = call(
        reduce_xy_kernel, [((8, 32, D), BF16)], [], 0, 8, 60_000_000, 4_000_000, 12,
    )(*u, *b)
    got_z = exchange(spread, Z_GROUPS)
    g_up, g_down, g_out, g_qkv, g_gains = call(
        reduce_z_kernel,
        [((32, 128), F32), ((32, 128), F32), ((8, 128), F32), ((24, 128), F32), ((2, D), F32)],
        [pltpu.VMEM((32, D), F32)], 0, 1, 1_000_000, 400_000, 8,
    )(got_z)

    up_a = send(jnp.where(row_odd, tail, head), ROW_A)
    gn = own[RIM : RIM + ROWS] + place(up_a, 0, row_odd, ROWS) + place(up_b, 0, ~row_odd, ROWS)
    gn = gn + gnq.reshape(ROWS, COLS, D)
    unit, inv = unit_of(tokens.astype(F32))
    g1 = gn * gains[0]
    front = inv * (g1 - unit * jnp.mean(g1 * unit, axis=-1, keepdims=True))
    grad_tokens = (gm.reshape(ROWS, COLS, D).astype(F32) + front).astype(BF16)
    return (grad_tokens, g_qkv.reshape(-1), g_out.reshape(-1), g_up.reshape(-1), g_down.reshape(-1), g_gains)


def solution(mesh):
    block = P("row", "col", None)
    flat = P(("row", "col"))
    return jax.shard_map(
        per_device,
        mesh=mesh,
        in_specs=(block, block, P(), P(), P(), P(), P(), block),
        out_specs=(block, flat, flat, flat, flat, P()),
        check_vma=False,
    )
```

```python
import functools
import math

import jax
import jax.numpy as jnp
from jax import lax
from jax.experimental import pallas as pl
from jax.experimental.pallas import tpu as pltpu
from jax.sharding import PartitionSpec as P

D = 512
FF = 2048
HEADS = 8
WINDOW = 7
TILE = 8
RIM = WINDOW // 2
EPS = 1e-06
AXES = ("row", "col")
N_COL = 32
GRID_ROWS = 192
GRID_COLS = 256
ROWS = 24
COLS = 8
TOK = ROWS * COLS
TILES = ROWS // TILE
ER = 32
EC = 16
EXT = ER * EC
QT = TILE * TILE
KT = 256
F32 = jnp.float32
BF16 = jnp.bfloat16
GELU_C = math.sqrt(2.0 / math.pi)


def nn(a, b):
    return lax.dot_general(a, b, (((1,), (0,)), ((), ())), preferred_element_type=F32)


def nt(a, b):
    return lax.dot_general(a, b, (((1,), (1,)), ((), ())), preferred_element_type=F32)


def tn(a, b):
    return lax.dot_general(a, b, (((0,), (0,)), ((), ())), preferred_element_type=F32)


def unit_of(x):
    inv = lax.rsqrt(jnp.mean(x * x, axis=-1, keepdims=True) + EPS)
    return x * inv, inv


def head_mask(rows, h):
    lane = lax.broadcasted_iota(jnp.int32, (rows, 256), 1)
    return (lane // 64) == h


def stack_heads(x):
    zero = jnp.zeros_like(x)
    return jnp.concatenate([jnp.where(head_mask(x.shape[0], h), x, zero) for h in range(4)], axis=0)


def unstack_heads(x):
    rows = x.shape[0] // 4
    out = jnp.where(head_mask(rows, 0), x[:rows], 0.0)
    for h in range(1, 4):
        out = out + jnp.where(head_mask(rows, h), x[h * rows : (h + 1) * rows], 0.0)
    return out


def prep_front_kernel(cot, w_down, gact):
    for c in range(4):
        gact[:, c * 512 : (c + 1) * 512] = nt(cot[...], w_down[c * 512 : (c + 1) * 512, :])


def prep_mask_kernel(coord, mask, bias):
    q = lax.broadcasted_iota(jnp.int32, (QT, KT), 0)
    k = lax.broadcasted_iota(jnp.int32, (QT, KT), 1)
    ki = k // EC
    kc = k % EC
    odd = coord[1] & 1
    near = kc - COLS + odd * (COLS + RIM)
    far = kc - COLS - RIM + (1 - odd) * (COLS + RIM)
    kj = jnp.where(kc < COLS, kc + RIM, jnp.where(kc < COLS + RIM, near, jnp.where(kc < COLS + 2 * RIM, far, -99)))
    da = ki - q // TILE
    db = kj - q % TILE
    slot = jnp.where((da >= 0) & (da < WINDOW) & (db >= 0) & (db < WINDOW), da * WINDOW + db, -1)
    allowed = [jnp.zeros((QT, KT), jnp.int32) for _ in range(TILES)]
    for s in range(WINDOW * WINDOW):
        here = slot == s
        for t in range(TILES):
            allowed[t] = jnp.where(here, mask[t, 0, s], allowed[t])
    gc = coord[1] * COLS + kj - RIM
    for t in range(TILES):
        gr = coord[0] * ROWS + t * TILE + ki - RIM
        ok = (allowed[t] == 1) & (gr >= 0) & (gr < GRID_ROWS) & (gc >= 0) & (gc < GRID_COLS)
        bias[t] = jnp.where(ok, 0.0, -1e30)


def prep_order_kernel(coord, pt_u, pt_k, pt_d):
    me = coord[2]
    lane = lax.broadcasted_iota(jnp.int32, (512, 512), 1)
    p = lax.broadcasted_iota(jnp.int32, (512, 512), 0)
    core_z = ((p >> 3) & 1) * 128 + ((p >> 1) & 3) * 2 + (p >> 8)
    hi, lo = (p >> 6) & 3, (p >> 4) & 3
    here = me & 121
    pt_u[...] = jnp.where(lane == ((core_z + hi * 32 + lo * 8) ^ here) * 2 + (p & 1), 1.0, 0.0).astype(BF16)
    pt_k[...] = jnp.where(lane == ((core_z + hi * 8 + lo * 32) ^ here) * 2 + (p & 1), 1.0, 0.0).astype(BF16)
    k_d = (((p >> 5) & 1) * 32 + ((p >> 6) & 3) * 8 + ((p >> 3) & 3) * 2 + (p >> 8)) ^ (me & 57)
    pt_d[...] = jnp.where(lane == k_d * 8 + (p & 7), 1.0, 0.0).astype(BF16)


def attend(qt, keys, vals, bias_t):
    s = nt(stack_heads(qt), keys) * 0.125 + jnp.concatenate([bias_t] * 4, axis=0)
    e = jnp.exp(s - jnp.max(s, axis=-1, keepdims=True))
    prob = e / jnp.sum(e, axis=-1, keepdims=True)
    return prob, unstack_heads(nn(prob.astype(BF16), vals)).astype(BF16)


def middle_kernel(mid, tok, gains, w_qkv, bias, q_o, no_o, ne_o, kv_o, p_o, attn_o):
    unit_e, _ = unit_of(mid[...].reshape(ROWS * EC, D).astype(F32))
    ne = (unit_e * gains[0:1, :]).astype(BF16)
    ne_o[...] = ne
    kv_o[...] = nn(ne, w_qkv[:, D:]).astype(BF16)
    unit_o, _ = unit_of(tok[...].astype(F32))
    no = (unit_o * gains[0:1, :]).astype(BF16)
    no_o[...] = no
    q_o[...] = nn(no, w_qkv[:, :D]).astype(BF16)
    at = 128 - RIM * EC
    for g in range(2):
        cols = slice(g * 256, (g + 1) * 256)
        vcols = slice(D + g * 256, D + (g + 1) * 256)
        prob, o = attend(q_o[QT : 2 * QT, cols], kv_o[at : at + KT, cols], kv_o[at : at + KT, vcols], bias[1])
        p_o[g] = prob
        attn_o[:, cols] = o


def forward_kernel(
    coord, rim_a, rim_b, tok, cot, gains, w_qkv, w_out, w_up, gact, bias, pt_u, pt_d, q_i, ne_i, kv_i, attn_i,
    u_keep, u_send, d_keep, d_send, gm_o, kv_o, p_o, ne_o, gain_o, attn_s,
):
    odd = coord[0] & 1
    edge = RIM * EC
    at_a = pl.multiple_of(odd * (RIM + ROWS) * EC, EC)
    at_b = pl.multiple_of((1 - odd) * (RIM + ROWS) * EC, EC)
    end = (RIM + ROWS) * EC
    both = jnp.concatenate([rim_a[...].reshape(edge, D), rim_b[...].reshape(edge, D)], axis=0)
    unit_r, _ = unit_of(both.astype(F32))
    ne_r = (unit_r * gains[0:1, :]).astype(BF16)
    kv_r = nn(ne_r, w_qkv[:, D:]).astype(BF16)
    for ref, mid, rims in ((ne_o, ne_i, ne_r), (kv_o, kv_i, kv_r)):
        ref[edge:end, :] = mid[...]
        ref[pl.ds(at_a, edge), :] = rims[:edge]
        ref[pl.ds(at_b, edge), :] = rims[edge:]
        ref[end + edge :, :] = jnp.zeros((EXT - end - edge, ref.shape[1]), BF16)
    xt = tok[...].astype(F32)
    attn_s[QT : 2 * QT, :] = attn_i[...]
    for i, t in enumerate((0, 2)):
        rows = slice(t * 128, t * 128 + KT)
        for g in range(2):
            cols = slice(g * 256, (g + 1) * 256)
            vcols = slice(D + g * 256, D + (g + 1) * 256)
            prob, o = attend(q_i[t * QT : (t + 1) * QT, cols], kv_o[rows, cols], kv_o[rows, vcols], bias[t])
            p_o[i * 2 + g] = prob
            attn_s[t * QT : (t + 1) * QT, cols] = o
    attn = attn_s[...]
    mixed = (xt + nn(attn, w_out[...])).astype(BF16)
    um, inv_m = unit_of(mixed.astype(F32))
    nm = (um * gains[1:2, :]).astype(BF16)
    nmt = nt(pt_u[...], nm).astype(BF16)
    gn = jnp.zeros((TOK, D), F32)
    for c in range(4):
        cols = slice(c * 512, (c + 1) * 512)
        pre = nn(nm, w_up[:, cols])
        th = jnp.tanh(GELU_C * (pre + 0.044715 * (pre * pre * pre)))
        half = 0.5 * (1.0 + th)
        act = (pre * half).astype(BF16)
        slope = half + 0.5 * pre * (1.0 - th * th) * (GELU_C * (1.0 + 0.134145 * (pre * pre)))
        gp = (gact[:, cols] * slope).astype(BF16)
        gn = gn + nt(gp, w_up[:, cols])
        gu = nn(nmt, gp).astype(BF16)
        u_keep[:, c] = gu[:256].reshape(16, 16, D)
        u_send[:, c] = gu[256:].reshape(16, 16, D)
        act_t = nt(pt_d[...], act).astype(BF16)
        gd = nn(act_t, cot[...]).astype(BF16)
        xh = (c & 1) ^ ((coord[2] >> 6) & 1)
        for y in range(4):
            for xl in range(2):
                at = (y * 2 + xl) * 32
                d_keep[y, xh * 2 + xl, c >> 1] = gd[at : at + 32]
                d_send[y, xh * 2 + xl, c >> 1] = gd[256 + at : 256 + at + 32]
    g = gn * gains[1:2, :]
    gm = (cot[...].astype(F32) + inv_m * (g - um * jnp.mean(g * um, axis=-1, keepdims=True))).astype(BF16)
    gm_o[...] = gm
    gain_o[...] = jnp.sum(gn * um, axis=0, keepdims=True)
    go = nn(nt(pt_u[...], attn).astype(BF16), gm).astype(BF16)
    u_keep[:, 4] = go[:256].reshape(16, 16, D)
    u_send[:, 4] = go[256:].reshape(16, 16, D)


def backward_kernel(
    gm, w_out, q, kv, p_mid, p_out, ne, no, pt_u, pt_k,
    k_keep, k_send, dq_s, dkv_o, dkv_s,
):
    ga = nt(gm[...], w_out[...]).astype(BF16)
    dkv_s[...] = jnp.zeros_like(dkv_s)
    for t in range(TILES):
        for g in range(2):
            cols = slice(g * 256, (g + 1) * 256)
            vcols = slice(D + g * 256, D + (g + 1) * 256)
            rows = slice(t * 128, t * 128 + KT)
            prob = p_mid[g] if t == 1 else p_out[t + g]
            gas = stack_heads(ga[t * QT : (t + 1) * QT, cols])
            qs = stack_heads(q[t * QT : (t + 1) * QT, cols])
            gp = nt(gas, kv[rows, vcols])
            inner = jnp.sum(prob * gp, axis=-1, keepdims=True)
            ds = (prob * (gp - inner) * 0.125).astype(BF16)
            dq_s[t * QT : (t + 1) * QT, cols] = unstack_heads(nn(ds, kv[rows, cols])).astype(BF16)
            dkv_s[rows, cols] += tn(ds, qs)
            dkv_s[rows, vcols] += tn(prob.astype(BF16), gas)
    dkv = dkv_s[...].astype(BF16)
    dkv_o[...] = dkv
    gk = nn(nt(pt_k[...], ne[...]).astype(BF16), dkv).astype(BF16)
    gq = nn(nt(pt_u[...], no[...]).astype(BF16), dq_s[...]).astype(BF16)
    for at, out in ((0, k_keep), (256, k_send)):
        out[:16] = gq[at : at + 256].reshape(16, 16, D)
        for i in range(2):
            for j in range(16):
                out[16 + j * 2 + i] = gk[at + j * 16 : at + j * 16 + 16, i * D : (i + 1) * D]


def inputs_kernel(coord, dq, dkv, w_qkv, mid, rim_a, rim_b, tok, gain_mid, gne_o, gnq_o, gain_o, send_o):
    gne = nt(dkv[...], w_qkv[:, D:])
    gnq = nt(dq[...], w_qkv[:, :D])
    gne_o[...] = gne[: (ROWS + 2 * RIM) * EC]
    sides = gne.reshape(ER, EC, D)[: ROWS + 2 * RIM, COLS:]
    send_o[:15] = sides.reshape((ROWS + 2 * RIM) * COLS, D).astype(BF16).reshape(15, 16, D)
    gnq_o[...] = gnq
    gain_in = jnp.sum(gnq * unit_of(tok[...].astype(F32))[0], axis=0, keepdims=True)
    odd = coord[0] & 1
    for ref, at in ((rim_a, odd * (RIM + ROWS)), (mid, RIM), (rim_b, (1 - odd) * (RIM + ROWS))):
        size = ref.shape[0] * EC
        unit, _ = unit_of(ref[...].reshape(size, D).astype(F32))
        part = gne_o[pl.ds(pl.multiple_of(at * EC, EC), size), :]
        gain_in = gain_in + jnp.sum(part * unit, axis=0, keepdims=True)
    spread = jnp.concatenate([gain_in, gain_mid[...], jnp.zeros((14, D), F32)], axis=0).astype(BF16)
    gain_o[...] = spread
    send_o[15] = spread


def add2(a, b):
    return (a.astype(F32) + b.astype(F32)).astype(BF16)


def add4(parts):
    a, b, c, d = [v.astype(F32) for v in parts]
    return ((a + b) + (c + d)).astype(BF16)


def join_down_kv_kernel(dk, dg, kk, kg, gk, gg, *outs):
    gain = add2(gk[...], gg[15])
    for d in range(4):
        outs[d][:16] = add2(dk[d * 16 : (d + 1) * 16], dg[d * 16 : (d + 1) * 16])
        outs[d][16:24] = add2(kk[16 + d * 8 : 24 + d * 8], kg[16 + d * 8 : 24 + d * 8])
        outs[d][24] = gain


def join_up_q_kernel(which, uk, ug, kk, kg, *outs):
    for out, d in zip(outs, which):
        out[:20] = add2(uk[d * 20 : (d + 1) * 20], ug[d * 20 : (d + 1) * 20])
        out[20:] = add2(kk[d * 4 : (d + 1) * 4], kg[d * 4 : (d + 1) * 4])


def sum_up_q_kernel(*refs):
    parts, outs = refs[:4], refs[4:]
    for d in range(4):
        outs[d][:5] = add4([r[d * 5 : (d + 1) * 5] for r in parts])
        outs[d][5] = add4([r[20 + d] for r in parts])


def sum_down_kv_kernel(*refs):
    parts, ride, outs = refs[:4], refs[4], refs[5:]
    gain = add4([r[24] for r in parts])
    for d in range(4):
        outs[d][:4] = add4([r[d * 4 : (d + 1) * 4] for r in parts])
        outs[d][4:6] = add4([r[16 + d * 2 : 18 + d * 2] for r in parts])
        outs[d][6] = gain
    outs[1][7:9] = ride[...]


def reduce_xy_kernel(*refs):
    out = refs[8]
    sums = [add4([r[...] for r in refs[:4]]).reshape(-1, D), add4([r[:7] for r in refs[4:8]]).reshape(-1, D)]
    acc = jnp.concatenate(sums, axis=0)
    rows = acc.shape[0]
    i = lax.broadcasted_iota(jnp.int32, (256, rows), 0)
    lane = lax.broadcasted_iota(jnp.int32, (256, rows), 1)
    z = i // 32
    r = i % 32
    up = (r % 4) * 16 + z * 2 + r // 4
    down = 96 + z * 8 + (r - 8)
    o = 64 + z * 2 + (r - 16)
    part = (r - 18) % 3
    qkv = jnp.where(part == 0, 80, 144 + part * 16) + z * 2 + (r - 18) // 3
    gain = 192 + (r - 24)
    src = jnp.where(r < 8, up, jnp.where(r < 16, down, jnp.where(r < 18, o, jnp.where(r < 24, qkv, gain))))
    pick = jnp.where((lane == src) & (r < 26), 1.0, 0.0).astype(BF16)
    out[...] = nn(pick, acc).astype(BF16).reshape(8, 32, D)


def reduce_z_kernel(got, up, down, o, qkv, gain, acc_s):
    acc = got[0].astype(F32)
    for j in range(1, 8):
        acc = acc + got[j].astype(F32)
    acc_s[...] = acc * (1.0 / math.sqrt(GRID_ROWS * GRID_COLS))
    at = 0
    for ref, rows in ((up, 8), (down, 8), (o, 2), (qkv, 6)):
        for r in range(rows):
            for j in range(4):
                ref[4 * r + j : 4 * r + j + 1, :] = acc_s[at + r : at + r + 1, j * 128 : (j + 1) * 128]
        at += rows
    gain[...] = acc_s[at : at + 2, :]


def call(body, outs, scratch, n_smem, n_in, flops, nbytes, mib):
    smem = pl.BlockSpec(memory_space=pltpu.SMEM)
    vmem = pl.BlockSpec(memory_space=pltpu.VMEM)
    return pl.pallas_call(
        body,
        out_shape=[jax.ShapeDtypeStruct(s, d) for s, d in outs],
        in_specs=[smem] * n_smem + [vmem] * n_in,
        out_specs=[vmem] * len(outs),
        scratch_shapes=scratch,
        compiler_params=pltpu.CompilerParams(vmem_limit_bytes=mib * 1024 * 1024),
        cost_estimate=pl.CostEstimate(flops=flops, bytes_accessed=nbytes, transcendentals=0),
    )


def pairs(stride, count, first):
    out = []
    for k in range(256):
        at = (k // stride) % count
        other = at + 1 if (at - first) % 2 == 0 else at - 1
        if 0 <= other < count:
            out.append((k, k + (other - at) * stride))
    return out


ROW_A, ROW_B = pairs(N_COL, 8, 1), pairs(N_COL, 8, 0)
COL_A, COL_B = pairs(1, N_COL, 1), pairs(1, N_COL, 0)
CORE_SWAP = [(k, k ^ 1) for k in range(256)]
X_BIT = 32
Y_BIT = 8
Z_GROUPS = [[zh * 128 + x * 32 + y * 8 + zl * 2 + c for zh in range(2) for zl in range(4)] for x in range(4) for y in range(4) for c in range(2)]


def send(x, perm):
    return lax.ppermute(x, AXES, perm)


def by(bits):
    return [(k, k ^ bits) for k in range(256)]


def to_three(chunks, bit):
    return [chunks[0]] + [send(chunks[d], by(bit * d)) for d in (1, 3, 2)]


def exchange(x, groups):
    return lax.all_to_all(x, AXES, 0, 0, axis_index_groups=groups, tiled=True)


def per_device(tokens, cotangent, gains, w_qkv, w_out, w_up, w_down, tile_mask):
    row = lax.axis_index("row")
    col = lax.axis_index("col")
    coord = jnp.stack([row, col, row * N_COL + col]).astype(jnp.int32)
    tok = tokens.reshape(TOK, D)
    cot = cotangent.reshape(TOK, D)

    row_odd = (row & 1) == 1
    col_odd = (col & 1) == 1
    first, last = tokens[:, :RIM], tokens[:, COLS - RIM :]
    side_b = send(jnp.where(col_odd, first, last), COL_B)
    side_a = send(jnp.where(col_odd, last, first), COL_A)
    (bias,) = call(
        prep_mask_kernel, [((TILES, QT, KT), F32)], [], 2, 0, 2 * TOK * D * FF, 4_000_000, 8,
    )(coord, tile_mask)
    side_a, side_b, cot, bias, coord = lax.optimization_barrier((side_a, side_b, cot, bias, coord))
    mid = jnp.concatenate([tokens, side_a, side_b, jnp.zeros((ROWS, EC - COLS - 2 * RIM, D), BF16)], axis=1)
    rim_b = send(jnp.where(row_odd, mid[:RIM], mid[ROWS - RIM :]), ROW_B)
    rim_a = send(jnp.where(row_odd, mid[ROWS - RIM :], mid[:RIM]), ROW_A)
    pt_u, pt_k, pt_d = call(
        prep_order_kernel, [((D, D), BF16)] * 3, [], 1, 0, 2 * TOK * D * FF, 4_000_000, 8,
    )(coord)
    (gact,) = call(
        prep_front_kernel, [((TOK, FF), F32)], [], 0, 2, 2 * TOK * D * FF, 4_000_000, 8,
    )(cot, w_down)

    q, no, ne_mid, kv_mid, p_mid, attn_mid = call(
        middle_kernel,
        [
            ((TOK, D), BF16), ((TOK, D), BF16), ((ROWS * EC, D), BF16), ((ROWS * EC, 2 * D), BF16),
            ((2, 256, KT), F32), ((QT, D), BF16),
        ],
        [], 0, 5, 600_000_000, 5_000_000, 10,
    )(mid, tok, gains, w_qkv, bias)

    half_u, half_d = ((16, 5, 16, D), BF16), ((4, 4, 2, 32, D), BF16)
    half_q, half_k = ((16, 16, D), BF16), ((48, 16, D), BF16)
    u_keep, u_send, d_keep, d_send, gm, kv, p_out, ne, gain_mid = call(
        forward_kernel,
        [
            half_u, half_u, half_d, half_d, ((TOK, D), BF16), ((EXT, 2 * D), BF16), ((4, 256, KT), F32),
            ((EXT, D), BF16), ((1, D), F32),
        ],
        [pltpu.VMEM((TOK, D), BF16)], 1, 16, 4_000_000_000, 20_000_000, 16,
    )(coord, rim_a, rim_b, tok, cot, gains, w_qkv, w_out, w_up, gact, bias, pt_u, pt_d, q, ne_mid, kv_mid, attn_mid)

    u_got = send(u_send, CORE_SWAP)
    d_got = send(d_send, CORE_SWAP)
    k_keep, k_send, dq, dkv = call(
        backward_kernel,
        [half_k, half_k, ((TOK, D), BF16), ((EXT, 2 * D), BF16)],
        [pltpu.VMEM((EXT, 2 * D), F32)], 0, 10, 2_500_000_000, 10_000_000, 12,
    )(gm, w_out, q, kv, p_mid, p_out, ne, no, pt_u, pt_k)
    u_got, d_got, k_send = lax.optimization_barrier((u_got, d_got, k_send))
    k_got = send(k_send, CORE_SWAP)
    gne, gnq, g_keep, g_send = call(
        inputs_kernel,
        [(((ROWS + 2 * RIM) * EC, D), F32), ((TOK, D), F32), ((16, D), BF16), half_q],
        [], 1, 8, 600_000_000, 4_000_000, 6,
    )(coord, dq, dkv, w_qkv, mid, rim_a, rim_b, tok, gain_mid)
    g_got = send(g_send, CORE_SWAP)

    def place(x, axis, odd, end_if_odd, size):
        gap = size - RIM
        after = [(0, 0)] * 3
        before = [(0, 0)] * 3
        after[axis], before[axis] = (0, gap), (gap, 0)
        x = x.astype(F32)
        x_odd, x_even = (before, after) if end_if_odd else (after, before)
        return jnp.where(odd, jnp.pad(x, x_odd), jnp.pad(x, x_even))

    def join(body, ins, outs):
        return list(call(body, [(o, BF16) for o in outs], [], 0, len(ins), 1_000_000, 4_000_000, 6)(*ins))

    def join_up(which, got):
        ins = [u_keep.reshape(80, 16, D), got.reshape(80, 16, D), k_keep, k_got]
        return join(functools.partial(join_up_q_kernel, which), ins, [(24, 16, D)] * len(which))

    u0, u1, u2, u3 = join_up((0, 1, 2, 3), u_got)
    d_got, u0, u1, u2, u3 = lax.optimization_barrier((d_got, u0, u1, u2, u3))
    b = join(
        join_down_kv_kernel, [d_keep.reshape(64, 16, D), d_got.reshape(64, 16, D), k_keep, k_got, g_keep, g_got],
        [(25, 16, D)] * 4,
    )
    gne3 = gne.reshape(ROWS + 2 * RIM, EC, D)
    back_a = send(gne3[:, COLS : COLS + RIM].astype(BF16), COL_A)
    u1, u3 = send(u1, by(X_BIT)), send(u3, by(3 * X_BIT))
    b = to_three(b, Y_BIT)
    u1, u2, back_a, g_got = lax.optimization_barrier((u1, u2, back_a, g_got))
    u = [u0, u1, u3, send(u2, by(2 * X_BIT))]
    back_b = g_got[:15].reshape(ROWS + 2 * RIM, COLS, D)[:, RIM : 2 * RIM]
    own = gne3[:, :COLS] + place(back_a, 1, col_odd, True, COLS) + place(back_b, 1, col_odd, False, COLS)
    head, tail = own[:RIM].astype(BF16), own[RIM + ROWS :].astype(BF16)
    ride = jnp.pad(jnp.where(row_odd, head, tail), ((0, 1), (0, 0), (0, 0))).reshape(2, 16, D)
    u, b, ride = lax.optimization_barrier((u, b, ride))
    b = join(sum_down_kv_kernel, [*b, ride], [(7, 16, D), (9, 16, D), (7, 16, D), (7, 16, D)])
    b = to_three(b, X_BIT)
    u = join(sum_up_q_kernel, u, [(6, 16, D)] * 4)
    u = to_three(u, Y_BIT)
    up_b = b[1][7:].reshape(4, COLS, D)[:RIM]
    (spread,) = call(
        reduce_xy_kernel, [((8, 32, D), BF16)], [], 0, 8, 60_000_000, 4_000_000, 5,
    )(*u, *b)
    got_z = exchange(spread, Z_GROUPS)
    g_up, g_down, g_out, g_qkv, g_gains = call(
        reduce_z_kernel,
        [((32, 128), F32), ((32, 128), F32), ((8, 128), F32), ((24, 128), F32), ((2, D), F32)],
        [pltpu.VMEM((32, D), F32)], 0, 1, 1_000_000, 400_000, 8,
    )(got_z)

    up_a = send(jnp.where(row_odd, tail, head), ROW_A)
    gn = own[RIM : RIM + ROWS] + place(up_a, 0, row_odd, True, ROWS) + place(up_b, 0, row_odd, False, ROWS)
    gn = gn + gnq.reshape(ROWS, COLS, D)
    unit, inv = unit_of(tokens.astype(F32))
    g1 = gn * gains[0]
    front = inv * (g1 - unit * jnp.mean(g1 * unit, axis=-1, keepdims=True))
    grad_tokens = (gm.reshape(ROWS, COLS, D).astype(F32) + front).astype(BF16)
    return (grad_tokens, g_qkv.reshape(-1), g_out.reshape(-1), g_up.reshape(-1), g_down.reshape(-1), g_gains)


def solution(mesh):
    block = P("row", "col", None)
    flat = P(("row", "col"))
    return jax.shard_map(
        per_device,
        mesh=mesh,
        in_specs=(block, block, P(), P(), P(), P(), P(), block),
        out_specs=(block, flat, flat, flat, flat, P()),
        check_vma=False,
    )
```

```python
import math

import jax
import jax.numpy as jnp
from jax import lax
from jax.experimental import pallas as pl
from jax.experimental.pallas import tpu as pltpu
from jax.sharding import PartitionSpec as P

D = 512
FF = 2048
HEADS = 8
WINDOW = 7
TILE = 8
RIM = WINDOW // 2
EPS = 1e-06
AXES = ("row", "col")
N_COL = 32
GRID_ROWS = 192
GRID_COLS = 256
ROWS = 24
COLS = 8
TOK = ROWS * COLS
TILES = ROWS // TILE
ER = 32
EC = 16
EXT = ER * EC
QT = TILE * TILE
ZROWS = 112
KT = 256
F32 = jnp.float32
BF16 = jnp.bfloat16
GELU_C = math.sqrt(2.0 / math.pi)


def nn(a, b):
    return lax.dot_general(a, b, (((1,), (0,)), ((), ())), preferred_element_type=F32)


def nt(a, b):
    return lax.dot_general(a, b, (((1,), (1,)), ((), ())), preferred_element_type=F32)


def tn(a, b):
    return lax.dot_general(a, b, (((0,), (0,)), ((), ())), preferred_element_type=F32)


def unit_of(x):
    inv = lax.rsqrt(jnp.mean(x * x, axis=-1, keepdims=True) + EPS)
    return x * inv, inv


def head_mask(rows, h):
    lane = lax.broadcasted_iota(jnp.int32, (rows, 256), 1)
    return (lane // 64) == h


def stack_heads(x):
    zero = jnp.zeros_like(x)
    return jnp.concatenate([jnp.where(head_mask(x.shape[0], h), x, zero) for h in range(4)], axis=0)


def unstack_heads(x):
    rows = x.shape[0] // 4
    out = jnp.where(head_mask(rows, 0), x[:rows], 0.0)
    for h in range(1, 4):
        out = out + jnp.where(head_mask(rows, h), x[h * rows : (h + 1) * rows], 0.0)
    return out


def prep_front_kernel(cot, w_down, gact):
    for c in range(4):
        gact[:, c * 512 : (c + 1) * 512] = nt(cot[...], w_down[c * 512 : (c + 1) * 512, :])


def prep_mask_kernel(coord, mask, bias):
    q = lax.broadcasted_iota(jnp.int32, (QT, KT), 0)
    k = lax.broadcasted_iota(jnp.int32, (QT, KT), 1)
    ki = k // EC
    kc = k % EC
    odd = coord[1] & 1
    near = kc - COLS + odd * (COLS + RIM)
    far = kc - COLS - RIM + (1 - odd) * (COLS + RIM)
    kj = jnp.where(kc < COLS, kc + RIM, jnp.where(kc < COLS + RIM, near, jnp.where(kc < COLS + 2 * RIM, far, -99)))
    da = ki - q // TILE
    db = kj - q % TILE
    slot = jnp.where((da >= 0) & (da < WINDOW) & (db >= 0) & (db < WINDOW), da * WINDOW + db, -1)
    allowed = [jnp.zeros((QT, KT), jnp.int32) for _ in range(TILES)]
    for s in range(WINDOW * WINDOW):
        here = slot == s
        for t in range(TILES):
            allowed[t] = jnp.where(here, mask[t, 0, s], allowed[t])
    gc = coord[1] * COLS + kj - RIM
    for t in range(TILES):
        gr = coord[0] * ROWS + t * TILE + ki - RIM
        ok = (allowed[t] == 1) & (gr >= 0) & (gr < GRID_ROWS) & (gc >= 0) & (gc < GRID_COLS)
        bias[t] = jnp.where(ok, 0.0, -1e30)


def prep_order_kernel(coord, pt_u, pt_k, pt_d):
    me = coord[2]
    lane = lax.broadcasted_iota(jnp.int32, (512, 512), 1)
    p = lax.broadcasted_iota(jnp.int32, (512, 512), 0)
    core_z = ((p >> 3) & 1) * 128 + ((p >> 1) & 3) * 2 + (p >> 8)
    hi, lo = (p >> 6) & 3, (p >> 4) & 3
    here = me & 121
    pt_u[...] = jnp.where(lane == ((core_z + hi * 32 + lo * 8) ^ here) * 2 + (p & 1), 1.0, 0.0).astype(BF16)
    pt_k[...] = jnp.where(lane == ((core_z + hi * 8 + lo * 32) ^ here) * 2 + (p & 1), 1.0, 0.0).astype(BF16)
    k_d = (((p >> 5) & 1) * 32 + ((p >> 6) & 3) * 8 + ((p >> 3) & 3) * 2 + (p >> 8)) ^ (me & 57)
    pt_d[...] = jnp.where(lane == k_d * 8 + (p & 7), 1.0, 0.0).astype(BF16)


def attend(qt, keys, vals, bias_t):
    s = nt(stack_heads(qt), keys) * 0.125 + jnp.concatenate([bias_t] * 4, axis=0)
    e = jnp.exp(s - jnp.max(s, axis=-1, keepdims=True))
    prob = e / jnp.sum(e, axis=-1, keepdims=True)
    return prob, unstack_heads(nn(prob.astype(BF16), vals)).astype(BF16)


def middle_kernel(mid, tok, gains, w_qkv, bias, q_o, no_o, ne_o, kv_o, p_o, attn_o):
    unit_e, _ = unit_of(mid[...].reshape(ROWS * EC, D).astype(F32))
    ne = (unit_e * gains[0:1, :]).astype(BF16)
    ne_o[...] = ne
    kv_o[...] = nn(ne, w_qkv[:, D:]).astype(BF16)
    unit_o, _ = unit_of(tok[...].astype(F32))
    no = (unit_o * gains[0:1, :]).astype(BF16)
    no_o[...] = no
    q_o[...] = nn(no, w_qkv[:, :D]).astype(BF16)
    at = 128 - RIM * EC
    for g in range(2):
        cols = slice(g * 256, (g + 1) * 256)
        vcols = slice(D + g * 256, D + (g + 1) * 256)
        prob, o = attend(q_o[QT : 2 * QT, cols], kv_o[at : at + KT, cols], kv_o[at : at + KT, vcols], bias[1])
        p_o[g] = prob
        attn_o[:, cols] = o


def forward_kernel(
    coord, rim_a, rim_b, tok, cot, gains, w_qkv, w_out, w_up, gact, bias, pt_u, pt_d, q_i, ne_i, kv_i, attn_i,
    u_keep, u_send, d_keep, d_send, gm_o, kv_o, p_o, ne_o, gain_o, attn_s,
):
    odd = coord[0] & 1
    edge = RIM * EC
    at_a = pl.multiple_of(odd * (RIM + ROWS) * EC, EC)
    at_b = pl.multiple_of((1 - odd) * (RIM + ROWS) * EC, EC)
    end = (RIM + ROWS) * EC
    both = jnp.concatenate([rim_a[...].reshape(edge, D), rim_b[...].reshape(edge, D)], axis=0)
    unit_r, _ = unit_of(both.astype(F32))
    ne_r = (unit_r * gains[0:1, :]).astype(BF16)
    kv_r = nn(ne_r, w_qkv[:, D:]).astype(BF16)
    for ref, mid, rims in ((ne_o, ne_i, ne_r), (kv_o, kv_i, kv_r)):
        ref[edge:end, :] = mid[...]
        ref[pl.ds(at_a, edge), :] = rims[:edge]
        ref[pl.ds(at_b, edge), :] = rims[edge:]
        ref[end + edge :, :] = jnp.zeros((EXT - end - edge, ref.shape[1]), BF16)
    xt = tok[...].astype(F32)
    attn_s[QT : 2 * QT, :] = attn_i[...]
    for i, t in enumerate((0, 2)):
        rows = slice(t * 128, t * 128 + KT)
        for g in range(2):
            cols = slice(g * 256, (g + 1) * 256)
            vcols = slice(D + g * 256, D + (g + 1) * 256)
            prob, o = attend(q_i[t * QT : (t + 1) * QT, cols], kv_o[rows, cols], kv_o[rows, vcols], bias[t])
            p_o[i * 2 + g] = prob
            attn_s[t * QT : (t + 1) * QT, cols] = o
    attn = attn_s[...]
    mixed = (xt + nn(attn, w_out[...])).astype(BF16)
    um, inv_m = unit_of(mixed.astype(F32))
    nm = (um * gains[1:2, :]).astype(BF16)
    nmt = nt(pt_u[...], nm).astype(BF16)
    gn = jnp.zeros((TOK, D), F32)
    for c in range(4):
        cols = slice(c * 512, (c + 1) * 512)
        pre = nn(nm, w_up[:, cols])
        th = jnp.tanh(GELU_C * (pre + 0.044715 * (pre * pre * pre)))
        half = 0.5 * (1.0 + th)
        act = (pre * half).astype(BF16)
        slope = half + 0.5 * pre * (1.0 - th * th) * (GELU_C * (1.0 + 0.134145 * (pre * pre)))
        gp = (gact[:, cols] * slope).astype(BF16)
        gn = gn + nt(gp, w_up[:, cols])
        gu = nn(nmt, gp).astype(BF16)
        u_keep[:, c] = gu[:256].reshape(16, 16, D)
        u_send[:, c] = gu[256:].reshape(16, 16, D)
        act_t = nt(pt_d[...], act).astype(BF16)
        gd = nn(act_t, cot[...]).astype(BF16)
        xh = (c & 1) ^ ((coord[2] >> 6) & 1)
        for y in range(4):
            for xl in range(2):
                at = (y * 2 + xl) * 32
                d_keep[y, xh * 2 + xl, c >> 1] = gd[at : at + 32]
                d_send[y, xh * 2 + xl, c >> 1] = gd[256 + at : 256 + at + 32]
    g = gn * gains[1:2, :]
    gm = (cot[...].astype(F32) + inv_m * (g - um * jnp.mean(g * um, axis=-1, keepdims=True))).astype(BF16)
    gm_o[...] = gm
    gain_o[...] = jnp.sum(gn * um, axis=0, keepdims=True)
    go = nn(nt(pt_u[...], attn).astype(BF16), gm).astype(BF16)
    u_keep[:, 4] = go[:256].reshape(16, 16, D)
    u_send[:, 4] = go[256:].reshape(16, 16, D)


def backward_kernel(
    gm, w_out, q, kv, p_mid, p_out, ne, no, pt_u, pt_k,
    k_keep, k_send, dq_s, dkv_o, dkv_s,
):
    ga = nt(gm[...], w_out[...]).astype(BF16)
    dkv_s[...] = jnp.zeros_like(dkv_s)
    for t in range(TILES):
        for g in range(2):
            cols = slice(g * 256, (g + 1) * 256)
            vcols = slice(D + g * 256, D + (g + 1) * 256)
            rows = slice(t * 128, t * 128 + KT)
            prob = p_mid[g] if t == 1 else p_out[t + g]
            gas = stack_heads(ga[t * QT : (t + 1) * QT, cols])
            qs = stack_heads(q[t * QT : (t + 1) * QT, cols])
            gp = nt(gas, kv[rows, vcols])
            inner = jnp.sum(prob * gp, axis=-1, keepdims=True)
            ds = (prob * (gp - inner) * 0.125).astype(BF16)
            dq_s[t * QT : (t + 1) * QT, cols] = unstack_heads(nn(ds, kv[rows, cols])).astype(BF16)
            dkv_s[rows, cols] += tn(ds, qs)
            dkv_s[rows, vcols] += tn(prob.astype(BF16), gas)
    dkv = dkv_s[...].astype(BF16)
    dkv_o[...] = dkv
    gk = nn(nt(pt_k[...], ne[...]).astype(BF16), dkv).astype(BF16)
    gq = nn(nt(pt_u[...], no[...]).astype(BF16), dq_s[...]).astype(BF16)
    for at, out in ((0, k_keep), (256, k_send)):
        out[:16] = gq[at : at + 256].reshape(16, 16, D)
        for i in range(2):
            for j in range(16):
                out[16 + j * 2 + i] = gk[at + j * 16 : at + j * 16 + 16, i * D : (i + 1) * D]


def inputs_kernel(coord, dq, dkv, w_qkv, mid, rim_a, rim_b, tok, gain_mid, gne_o, gnq_o, gain_o, send_o):
    gne = nt(dkv[...], w_qkv[:, D:])
    gnq = nt(dq[...], w_qkv[:, :D])
    gne_o[...] = gne[: (ROWS + 2 * RIM) * EC]
    sides = gne.reshape(ER, EC, D)[: ROWS + 2 * RIM, COLS:]
    send_o[:15] = sides.reshape((ROWS + 2 * RIM) * COLS, D).astype(BF16).reshape(15, 16, D)
    gnq_o[...] = gnq
    gain_in = jnp.sum(gnq * unit_of(tok[...].astype(F32))[0], axis=0, keepdims=True)
    odd = coord[0] & 1
    for ref, at in ((rim_a, odd * (RIM + ROWS)), (mid, RIM), (rim_b, (1 - odd) * (RIM + ROWS))):
        size = ref.shape[0] * EC
        unit, _ = unit_of(ref[...].reshape(size, D).astype(F32))
        part = gne_o[pl.ds(pl.multiple_of(at * EC, EC), size), :]
        gain_in = gain_in + jnp.sum(part * unit, axis=0, keepdims=True)
    spread = jnp.concatenate([gain_in, gain_mid[...], jnp.zeros((14, D), F32)], axis=0).astype(BF16)
    gain_o[...] = spread
    send_o[15] = spread


def add2(a, b):
    return (a.astype(F32) + b.astype(F32)).astype(BF16)


def add4(parts):
    a, b, c, d = [v.astype(F32) for v in parts]
    return ((a + b) + (c + d)).astype(BF16)


def halves():
    return ((0, (1, 2), (0, 3)), (1, (3, 2), (0, 1)))


def join_down_kv_kernel(dk, dg, kk, kg, gk, gg, *outs):
    gain = add2(gk[...], gg[15])
    for h, away, stay in halves():
        for out, chunks in ((outs[h], away), (outs[2 + h], stay)):
            for i, d in enumerate(chunks):
                lo, at = d * 16 + h * 8, i * 12
                out[at : at + 8] = add2(dk[lo : lo + 8], dg[lo : lo + 8])
                lo = 16 + d * 8 + h * 4
                out[at + 8 : at + 12] = add2(kk[lo : lo + 4], kg[lo : lo + 4])
    outs[0][24] = gain
    outs[2][24] = gain


def join_up_q_kernel(uk, ug, kk, kg, *outs):
    for h, away, stay in halves():
        for out, chunks in ((outs[h], away), (outs[2 + h], stay)):
            for i, d in enumerate(chunks):
                lo, at = d * 20 + h * 10, i * 12
                out[at : at + 10] = add2(uk[lo : lo + 10], ug[lo : lo + 10])
                lo = d * 4 + h * 2
                out[at + 10 : at + 12] = add2(kk[lo : lo + 2], kg[lo : lo + 2])


def second_kernel(p_got, q_got, p_keep, q_keep, p_send, q_send, p_own, q_own):
    p_own[:12] = add2(p_keep[:12], p_got[:12])
    p_send[:12] = add2(p_keep[12:24], p_got[12:24])
    q_own[...] = add2(q_keep[:12], q_got[:12])
    q_send[...] = add2(q_keep[12:], q_got[12:])
    if p_keep.shape[0] == 25:
        gain = add2(p_keep[24], p_got[24])
        p_own[12] = gain
        p_send[12] = gain


def sum_up_q_kernel(p_got, q_got, p_own, q_own, *outs):
    for h, got, own in ((0, p_got, p_own), (1, q_got, q_own)):
        for i in range(2):
            outs[2 * h + i][:5] = add2(got[i * 5 : i * 5 + 5], own[i * 5 : i * 5 + 5])
            outs[2 * h + i][5] = add2(got[10 + i], own[10 + i])


def sum_down_kv_kernel(p_got, q_got, p_own, q_own, ride, *outs):
    gain = add2(p_got[12], p_own[12])
    for h, got, own in ((0, p_got, p_own), (1, q_got, q_own)):
        for i in range(2):
            out = outs[2 * h + i]
            out[:4] = add2(got[i * 4 : i * 4 + 4], own[i * 4 : i * 4 + 4])
            out[4:6] = add2(got[8 + i * 2 : 10 + i * 2], own[8 + i * 2 : 10 + i * 2])
            out[6] = gain
    outs[1][7:9] = ride[...]


def reduce_xy_kernel(*refs):
    out = refs[8]
    sums = [add4([r[...] for r in refs[:4]]).reshape(-1, D), add4([r[:7] for r in refs[4:8]]).reshape(-1, D)]
    acc = jnp.concatenate(sums, axis=0)
    rows = acc.shape[0]
    i = lax.broadcasted_iota(jnp.int32, (8 * ZROWS, rows), 0)
    lane = lax.broadcasted_iota(jnp.int32, (8 * ZROWS, rows), 1)
    z = i // ZROWS
    r = (i % ZROWS) // 4
    up = (r % 4) * 16 + z * 2 + r // 4
    down = 96 + z * 8 + (r - 8)
    o = 64 + z * 2 + (r - 16)
    part = (r - 18) % 3
    qkv = jnp.where(part == 0, 80, 144 + part * 16) + z * 2 + (r - 18) // 3
    gain = 192 + (r - 24)
    src = jnp.where(r < 8, up, jnp.where(r < 16, down, jnp.where(r < 18, o, jnp.where(r < 24, qkv, gain))))
    hit = (lane == src) & (r < 26)
    picked = jnp.zeros((8 * ZROWS, 128), F32)
    for j in range(4):
        pick = jnp.where(hit & (i % 4 == j), 1.0, 0.0).astype(BF16)
        picked = picked + nn(pick, acc[:, j * 128 : (j + 1) * 128])
    out[...] = picked.astype(BF16).reshape(8, ZROWS, 128)


def reduce_z_kernel(got, up, down, o, qkv, gain):
    acc = got[0].astype(F32)
    for j in range(1, 8):
        acc = acc + got[j].astype(F32)
    acc = acc * (1.0 / math.sqrt(GRID_ROWS * GRID_COLS))
    at = 0
    for ref in (up, down, o, qkv):
        ref[...] = acc[at : at + ref.shape[0]]
        at += ref.shape[0]
    for r in range(2):
        for j in range(4):
            gain[r : r + 1, j * 128 : (j + 1) * 128] = acc[at + 4 * r + j : at + 4 * r + j + 1]


def call(body, outs, scratch, n_smem, n_in, flops, nbytes, mib):
    smem = pl.BlockSpec(memory_space=pltpu.SMEM)
    vmem = pl.BlockSpec(memory_space=pltpu.VMEM)
    return pl.pallas_call(
        body,
        out_shape=[jax.ShapeDtypeStruct(s, d) for s, d in outs],
        in_specs=[smem] * n_smem + [vmem] * n_in,
        out_specs=[vmem] * len(outs),
        scratch_shapes=scratch,
        compiler_params=pltpu.CompilerParams(vmem_limit_bytes=mib * 1024 * 1024),
        cost_estimate=pl.CostEstimate(flops=flops, bytes_accessed=nbytes, transcendentals=0),
    )


def pairs(stride, count, first):
    out = []
    for k in range(256):
        at = (k // stride) % count
        other = at + 1 if (at - first) % 2 == 0 else at - 1
        if 0 <= other < count:
            out.append((k, k + (other - at) * stride))
    return out


ROW_A, ROW_B = pairs(N_COL, 8, 1), pairs(N_COL, 8, 0)
COL_A, COL_B = pairs(1, N_COL, 1), pairs(1, N_COL, 0)
CORE_SWAP = [(k, k ^ 1) for k in range(256)]
X_BIT = 32
Y_BIT = 8
Z_GROUPS = [[zh * 128 + x * 32 + y * 8 + zl * 2 + c for zh in range(2) for zl in range(4)] for x in range(4) for y in range(4) for c in range(2)]


def send(x, perm):
    return lax.ppermute(x, AXES, perm)


def by(bits):
    return [(k, k ^ bits) for k in range(256)]


def to_three(chunks, bit):
    return [chunks[0]] + [send(chunks[d], by(bit * d)) for d in (1, 3, 2)]


def exchange(x, groups):
    return lax.all_to_all(x, AXES, 0, 0, axis_index_groups=groups, tiled=True)


def per_device(tokens, cotangent, gains, w_qkv, w_out, w_up, w_down, tile_mask):
    row = lax.axis_index("row")
    col = lax.axis_index("col")
    coord = jnp.stack([row, col, row * N_COL + col]).astype(jnp.int32)
    tok = tokens.reshape(TOK, D)
    cot = cotangent.reshape(TOK, D)

    row_odd = (row & 1) == 1
    col_odd = (col & 1) == 1
    first, last = tokens[:, :RIM], tokens[:, COLS - RIM :]
    side_b = send(jnp.where(col_odd, first, last), COL_B)
    side_a = send(jnp.where(col_odd, last, first), COL_A)
    (bias,) = call(
        prep_mask_kernel, [((TILES, QT, KT), F32)], [], 2, 0, 2 * TOK * D * FF, 4_000_000, 8,
    )(coord, tile_mask)
    side_a, side_b, cot, bias, coord = lax.optimization_barrier((side_a, side_b, cot, bias, coord))
    mid = jnp.concatenate([tokens, side_a, side_b, jnp.zeros((ROWS, EC - COLS - 2 * RIM, D), BF16)], axis=1)
    rim_b = send(jnp.where(row_odd, mid[:RIM], mid[ROWS - RIM :]), ROW_B)
    rim_a = send(jnp.where(row_odd, mid[ROWS - RIM :], mid[:RIM]), ROW_A)
    pt_u, pt_k, pt_d = call(
        prep_order_kernel, [((D, D), BF16)] * 3, [], 1, 0, 2 * TOK * D * FF, 4_000_000, 8,
    )(coord)
    (gact,) = call(
        prep_front_kernel, [((TOK, FF), F32)], [], 0, 2, 2 * TOK * D * FF, 4_000_000, 8,
    )(cot, w_down)

    q, no, ne_mid, kv_mid, p_mid, attn_mid = call(
        middle_kernel,
        [
            ((TOK, D), BF16), ((TOK, D), BF16), ((ROWS * EC, D), BF16), ((ROWS * EC, 2 * D), BF16),
            ((2, 256, KT), F32), ((QT, D), BF16),
        ],
        [], 0, 5, 600_000_000, 5_000_000, 10,
    )(mid, tok, gains, w_qkv, bias)

    half_u, half_d = ((16, 5, 16, D), BF16), ((4, 4, 2, 32, D), BF16)
    half_q, half_k = ((16, 16, D), BF16), ((48, 16, D), BF16)
    u_keep, u_send, d_keep, d_send, gm, kv, p_out, ne, gain_mid = call(
        forward_kernel,
        [
            half_u, half_u, half_d, half_d, ((TOK, D), BF16), ((EXT, 2 * D), BF16), ((4, 256, KT), F32),
            ((EXT, D), BF16), ((1, D), F32),
        ],
        [pltpu.VMEM((TOK, D), BF16)], 1, 16, 4_000_000_000, 20_000_000, 16,
    )(coord, rim_a, rim_b, tok, cot, gains, w_qkv, w_out, w_up, gact, bias, pt_u, pt_d, q, ne_mid, kv_mid, attn_mid)

    u_got = send(u_send, CORE_SWAP)
    d_got = send(d_send, CORE_SWAP)
    k_keep, k_send, dq, dkv = call(
        backward_kernel,
        [half_k, half_k, ((TOK, D), BF16), ((EXT, 2 * D), BF16)],
        [pltpu.VMEM((EXT, 2 * D), F32)], 0, 10, 2_500_000_000, 10_000_000, 12,
    )(gm, w_out, q, kv, p_mid, p_out, ne, no, pt_u, pt_k)
    u_got, d_got, k_send = lax.optimization_barrier((u_got, d_got, k_send))
    k_got = send(k_send, CORE_SWAP)
    gne, gnq, g_keep, g_send = call(
        inputs_kernel,
        [(((ROWS + 2 * RIM) * EC, D), F32), ((TOK, D), F32), ((16, D), BF16), half_q],
        [], 1, 8, 600_000_000, 4_000_000, 6,
    )(coord, dq, dkv, w_qkv, mid, rim_a, rim_b, tok, gain_mid)
    g_got = send(g_send, CORE_SWAP)

    def place(x, axis, odd, end_if_odd, size):
        gap = size - RIM
        after = [(0, 0)] * 3
        before = [(0, 0)] * 3
        after[axis], before[axis] = (0, gap), (gap, 0)
        x = x.astype(F32)
        x_odd, x_even = (before, after) if end_if_odd else (after, before)
        return jnp.where(odd, jnp.pad(x, x_odd), jnp.pad(x, x_even))

    def join(body, ins, outs):
        return list(call(body, [(o, BF16) for o in outs], [], 0, len(ins), 1_000_000, 4_000_000, 6)(*ins))

    def first(sent, bit):
        return send(sent[0], by(bit)), send(sent[1], by(3 * bit))

    def second(sent, bit):
        return send(sent[0], by(3 * bit)), send(sent[1], by(bit))

    k_got, gnq = lax.optimization_barrier((k_got, gnq))
    u_p, u_q, *u_stay = join(
        join_up_q_kernel, [u_keep.reshape(80, 16, D), u_got.reshape(80, 16, D), k_keep, k_got], [(24, 16, D)] * 4,
    )
    u_first = first((u_p, u_q), X_BIT)
    b_p, b_q, *b_stay = join(
        join_down_kv_kernel, [d_keep.reshape(64, 16, D), d_got.reshape(64, 16, D), k_keep, k_got, g_keep, g_got],
        [(25, 16, D), (24, 16, D)] * 2,
    )
    gne3 = gne.reshape(ROWS + 2 * RIM, EC, D)
    side = gne3[:, COLS : COLS + RIM].astype(BF16)
    b_first = first((b_p, b_q), Y_BIT)
    u_first, side = lax.optimization_barrier((u_first, side))
    back_a = send(side, COL_A)
    u_p, u_q, *u_own = join(second_kernel, [*u_first, *u_stay], [(12, 16, D)] * 4)
    u_second = second((u_p, u_q), X_BIT)
    b_p, b_q, *b_own = join(second_kernel, [*b_first, *b_stay], [(13, 16, D), (12, 16, D)] * 2)
    b_second = second((b_p, b_q), Y_BIT)
    back_b = g_got[:15].reshape(ROWS + 2 * RIM, COLS, D)[:, RIM : 2 * RIM]
    own = gne3[:, :COLS] + place(back_a, 1, col_odd, True, COLS) + place(back_b, 1, col_odd, False, COLS)
    head, tail = own[:RIM].astype(BF16), own[RIM + ROWS :].astype(BF16)
    ride = jnp.pad(jnp.where(row_odd, head, tail), ((0, 1), (0, 0), (0, 0))).reshape(2, 16, D)
    u = join(sum_up_q_kernel, [*u_second, *u_own], [(6, 16, D)] * 4)
    u = to_three(u, Y_BIT)
    b = join(sum_down_kv_kernel, [*b_second, *b_own, ride], [(7, 16, D), (9, 16, D), (7, 16, D), (7, 16, D)])
    b = to_three(b, X_BIT)
    up_b = b[1][7:].reshape(4, COLS, D)[:RIM]
    (spread,) = call(
        reduce_xy_kernel, [((8, ZROWS, 128), BF16)], [], 0, 8, 60_000_000, 4_000_000, 5,
    )(*u, *b)
    up_a = send(jnp.where(row_odd, tail, head), ROW_A)
    got_z = exchange(spread, Z_GROUPS)
    g_up, g_down, g_out, g_qkv, g_gains = call(
        reduce_z_kernel,
        [((32, 128), F32), ((32, 128), F32), ((8, 128), F32), ((24, 128), F32), ((2, D), F32)],
        [], 0, 1, 100_000_000_000, 400_000, 4,
    )(got_z)

    gn = own[RIM : RIM + ROWS] + place(up_a, 0, row_odd, True, ROWS) + place(up_b, 0, row_odd, False, ROWS)
    gn = gn + gnq.reshape(ROWS, COLS, D)
    unit, inv = unit_of(tokens.astype(F32))
    g1 = gn * gains[0]
    front = inv * (g1 - unit * jnp.mean(g1 * unit, axis=-1, keepdims=True))
    grad_tokens = (gm.reshape(ROWS, COLS, D).astype(F32) + front).astype(BF16)
    return (grad_tokens, g_qkv.reshape(-1), g_out.reshape(-1), g_up.reshape(-1), g_down.reshape(-1), g_gains)


def solution(mesh):
    block = P("row", "col", None)
    flat = P(("row", "col"))
    return jax.shard_map(
        per_device,
        mesh=mesh,
        in_specs=(block, block, P(), P(), P(), P(), P(), block),
        out_specs=(block, flat, flat, flat, flat, P()),
        check_vma=False,
    )
```

```python
import math

import jax
import jax.numpy as jnp
from jax import lax
from jax.experimental import pallas as pl
from jax.experimental.pallas import tpu as pltpu
from jax.sharding import PartitionSpec as P

D = 512
FF = 2048
HEADS = 8
WINDOW = 7
TILE = 8
RIM = WINDOW // 2
EPS = 1e-06
AXES = ("row", "col")
N_COL = 32
GRID_ROWS = 192
GRID_COLS = 256
ROWS = 24
COLS = 8
TOK = ROWS * COLS
TILES = ROWS // TILE
ER = 32
EC = 16
EXT = ER * EC
QT = TILE * TILE
ZROWS = 112
KT = 256
F32 = jnp.float32
BF16 = jnp.bfloat16
GELU_C = math.sqrt(2.0 / math.pi)


def nn(a, b):
    return lax.dot_general(a, b, (((1,), (0,)), ((), ())), preferred_element_type=F32)


def nt(a, b):
    return lax.dot_general(a, b, (((1,), (1,)), ((), ())), preferred_element_type=F32)


def tn(a, b):
    return lax.dot_general(a, b, (((0,), (0,)), ((), ())), preferred_element_type=F32)


def unit_of(x):
    inv = lax.rsqrt(jnp.mean(x * x, axis=-1, keepdims=True) + EPS)
    return x * inv, inv


def head_mask(rows, h):
    lane = lax.broadcasted_iota(jnp.int32, (rows, 256), 1)
    return (lane // 64) == h


def stack_heads(x):
    zero = jnp.zeros_like(x)
    return jnp.concatenate([jnp.where(head_mask(x.shape[0], h), x, zero) for h in range(4)], axis=0)


def unstack_heads(x):
    rows = x.shape[0] // 4
    out = jnp.where(head_mask(rows, 0), x[:rows], 0.0)
    for h in range(1, 4):
        out = out + jnp.where(head_mask(rows, h), x[h * rows : (h + 1) * rows], 0.0)
    return out


def prep_front_kernel(cot, w_down, gact):
    for c in range(4):
        gact[:, c * 512 : (c + 1) * 512] = nt(cot[...], w_down[c * 512 : (c + 1) * 512, :])


def prep_mask_kernel(coord, mask, bias):
    q = lax.broadcasted_iota(jnp.int32, (QT, KT), 0)
    k = lax.broadcasted_iota(jnp.int32, (QT, KT), 1)
    ki = k // EC
    kc = k % EC
    odd = coord[1] & 1
    near = kc - COLS + odd * (COLS + RIM)
    far = kc - COLS - RIM + (1 - odd) * (COLS + RIM)
    kj = jnp.where(kc < COLS, kc + RIM, jnp.where(kc < COLS + RIM, near, jnp.where(kc < COLS + 2 * RIM, far, -99)))
    da = ki - q // TILE
    db = kj - q % TILE
    slot = jnp.where((da >= 0) & (da < WINDOW) & (db >= 0) & (db < WINDOW), da * WINDOW + db, -1)
    allowed = [jnp.zeros((QT, KT), jnp.int32) for _ in range(TILES)]
    for s in range(WINDOW * WINDOW):
        here = slot == s
        for t in range(TILES):
            allowed[t] = jnp.where(here, mask[t, 0, s], allowed[t])
    gc = coord[1] * COLS + kj - RIM
    for t in range(TILES):
        gr = coord[0] * ROWS + t * TILE + ki - RIM
        ok = (allowed[t] == 1) & (gr >= 0) & (gr < GRID_ROWS) & (gc >= 0) & (gc < GRID_COLS)
        bias[t] = jnp.where(ok, 0.0, -1e30)


def prep_order_kernel(coord, pt_u, pt_k, pt_d):
    me = coord[2]
    lane = lax.broadcasted_iota(jnp.int32, (512, 512), 1)
    p = lax.broadcasted_iota(jnp.int32, (512, 512), 0)
    core_z = ((p >> 3) & 1) * 128 + ((p >> 1) & 3) * 2 + (p >> 8)
    hi, lo = (p >> 6) & 3, (p >> 4) & 3
    here = me & 121
    pt_u[...] = jnp.where(lane == ((core_z + hi * 32 + lo * 8) ^ here) * 2 + (p & 1), 1.0, 0.0).astype(BF16)
    pt_k[...] = jnp.where(lane == ((core_z + hi * 8 + lo * 32) ^ here) * 2 + (p & 1), 1.0, 0.0).astype(BF16)
    k_d = (((p >> 5) & 1) * 32 + ((p >> 6) & 3) * 8 + ((p >> 3) & 3) * 2 + (p >> 8)) ^ (me & 57)
    pt_d[...] = jnp.where(lane == k_d * 8 + (p & 7), 1.0, 0.0).astype(BF16)


def attend(qt, keys, vals, bias_t):
    s = nt(stack_heads(qt), keys) * 0.125 + jnp.concatenate([bias_t] * 4, axis=0)
    e = jnp.exp(s - jnp.max(s, axis=-1, keepdims=True))
    prob = e / jnp.sum(e, axis=-1, keepdims=True)
    return prob, unstack_heads(nn(prob.astype(BF16), vals)).astype(BF16)


def middle_kernel(mid, tok, gains, w_qkv, bias, q_o, no_o, ne_o, kv_o, p_o, attn_o):
    unit_e, _ = unit_of(mid[...].reshape(ROWS * EC, D).astype(F32))
    ne = (unit_e * gains[0:1, :]).astype(BF16)
    ne_o[...] = ne
    kv_o[...] = nn(ne, w_qkv[:, D:]).astype(BF16)
    unit_o, _ = unit_of(tok[...].astype(F32))
    no = (unit_o * gains[0:1, :]).astype(BF16)
    no_o[...] = no
    q_o[...] = nn(no, w_qkv[:, :D]).astype(BF16)
    at = 128 - RIM * EC
    for g in range(2):
        cols = slice(g * 256, (g + 1) * 256)
        vcols = slice(D + g * 256, D + (g + 1) * 256)
        prob, o = attend(q_o[QT : 2 * QT, cols], kv_o[at : at + KT, cols], kv_o[at : at + KT, vcols], bias[1])
        p_o[g] = prob
        attn_o[:, cols] = o


def forward_kernel(
    coord, rim_a, rim_b, tok, cot, gains, w_qkv, w_out, w_up, gact, bias, pt_u, pt_d, q_i, ne_i, kv_i, attn_i,
    u_keep, u_send, d_keep, d_send, gm_o, kv_o, p_o, ne_o, gain_o, attn_s,
):
    odd = coord[0] & 1
    edge = RIM * EC
    at_a = pl.multiple_of(odd * (RIM + ROWS) * EC, EC)
    at_b = pl.multiple_of((1 - odd) * (RIM + ROWS) * EC, EC)
    end = (RIM + ROWS) * EC
    both = jnp.concatenate([rim_a[...].reshape(edge, D), rim_b[...].reshape(edge, D)], axis=0)
    unit_r, _ = unit_of(both.astype(F32))
    ne_r = (unit_r * gains[0:1, :]).astype(BF16)
    kv_r = nn(ne_r, w_qkv[:, D:]).astype(BF16)
    for ref, mid, rims in ((ne_o, ne_i, ne_r), (kv_o, kv_i, kv_r)):
        ref[edge:end, :] = mid[...]
        ref[pl.ds(at_a, edge), :] = rims[:edge]
        ref[pl.ds(at_b, edge), :] = rims[edge:]
        ref[end + edge :, :] = jnp.zeros((EXT - end - edge, ref.shape[1]), BF16)
    xt = tok[...].astype(F32)
    attn_s[QT : 2 * QT, :] = attn_i[...]
    for i, t in enumerate((0, 2)):
        rows = slice(t * 128, t * 128 + KT)
        for g in range(2):
            cols = slice(g * 256, (g + 1) * 256)
            vcols = slice(D + g * 256, D + (g + 1) * 256)
            prob, o = attend(q_i[t * QT : (t + 1) * QT, cols], kv_o[rows, cols], kv_o[rows, vcols], bias[t])
            p_o[i * 2 + g] = prob
            attn_s[t * QT : (t + 1) * QT, cols] = o
    attn = attn_s[...]
    mixed = (xt + nn(attn, w_out[...])).astype(BF16)
    um, inv_m = unit_of(mixed.astype(F32))
    nm = (um * gains[1:2, :]).astype(BF16)
    nmt = nt(pt_u[...], nm).astype(BF16)
    gn = jnp.zeros((TOK, D), F32)
    for c in range(4):
        cols = slice(c * 512, (c + 1) * 512)
        pre = nn(nm, w_up[:, cols])
        th = jnp.tanh(GELU_C * (pre + 0.044715 * (pre * pre * pre)))
        half = 0.5 * (1.0 + th)
        act = (pre * half).astype(BF16)
        slope = half + 0.5 * pre * (1.0 - th * th) * (GELU_C * (1.0 + 0.134145 * (pre * pre)))
        gp = (gact[:, cols] * slope).astype(BF16)
        gn = gn + nt(gp, w_up[:, cols])
        gu = nn(nmt, gp).astype(BF16)
        u_keep[:, c] = gu[:256].reshape(16, 16, D)
        u_send[:, c] = gu[256:].reshape(16, 16, D)
        act_t = nt(pt_d[...], act).astype(BF16)
        gd = nn(act_t, cot[...]).astype(BF16)
        xh = (c & 1) ^ ((coord[2] >> 6) & 1)
        for y in range(4):
            for xl in range(2):
                at = (y * 2 + xl) * 32
                d_keep[y, xh * 2 + xl, c >> 1] = gd[at : at + 32]
                d_send[y, xh * 2 + xl, c >> 1] = gd[256 + at : 256 + at + 32]
    g = gn * gains[1:2, :]
    gm = (cot[...].astype(F32) + inv_m * (g - um * jnp.mean(g * um, axis=-1, keepdims=True))).astype(BF16)
    gm_o[...] = gm
    gain_o[...] = jnp.sum(gn * um, axis=0, keepdims=True)
    go = nn(nt(pt_u[...], attn).astype(BF16), gm).astype(BF16)
    u_keep[:, 4] = go[:256].reshape(16, 16, D)
    u_send[:, 4] = go[256:].reshape(16, 16, D)


def backward_kernel(
    gm, w_out, q, kv, p_mid, p_out, ne, no, pt_u, pt_k,
    k_keep, k_send, dq_s, dkv_o, dkv_s,
):
    ga = nt(gm[...], w_out[...]).astype(BF16)
    dkv_s[...] = jnp.zeros_like(dkv_s)
    for t in range(TILES):
        for g in range(2):
            cols = slice(g * 256, (g + 1) * 256)
            vcols = slice(D + g * 256, D + (g + 1) * 256)
            rows = slice(t * 128, t * 128 + KT)
            prob = p_mid[g] if t == 1 else p_out[t + g]
            gas = stack_heads(ga[t * QT : (t + 1) * QT, cols])
            qs = stack_heads(q[t * QT : (t + 1) * QT, cols])
            gp = nt(gas, kv[rows, vcols])
            inner = jnp.sum(prob * gp, axis=-1, keepdims=True)
            ds = (prob * (gp - inner) * 0.125).astype(BF16)
            dq_s[t * QT : (t + 1) * QT, cols] = unstack_heads(nn(ds, kv[rows, cols])).astype(BF16)
            dkv_s[rows, cols] += tn(ds, qs)
            dkv_s[rows, vcols] += tn(prob.astype(BF16), gas)
    dkv = dkv_s[...].astype(BF16)
    dkv_o[...] = dkv
    gk = nn(nt(pt_k[...], ne[...]).astype(BF16), dkv).astype(BF16)
    gq = nn(nt(pt_u[...], no[...]).astype(BF16), dq_s[...]).astype(BF16)
    for at, out in ((0, k_keep), (256, k_send)):
        out[:16] = gq[at : at + 256].reshape(16, 16, D)
        for i in range(2):
            for j in range(16):
                out[16 + j * 2 + i] = gk[at + j * 16 : at + j * 16 + 16, i * D : (i + 1) * D]


def inputs_kernel(coord, dq, dkv, w_qkv, mid, rim_a, rim_b, tok, gain_mid, gne_o, gnq_o, gain_o, send_o):
    gne = nt(dkv[...], w_qkv[:, D:])
    gnq = nt(dq[...], w_qkv[:, :D])
    gne_o[...] = gne[: (ROWS + 2 * RIM) * EC]
    sides = gne.reshape(ER, EC, D)[: ROWS + 2 * RIM, COLS:]
    send_o[:15] = sides.reshape((ROWS + 2 * RIM) * COLS, D).astype(BF16).reshape(15, 16, D)
    gnq_o[...] = gnq
    gain_in = jnp.sum(gnq * unit_of(tok[...].astype(F32))[0], axis=0, keepdims=True)
    odd = coord[0] & 1
    for ref, at in ((rim_a, odd * (RIM + ROWS)), (mid, RIM), (rim_b, (1 - odd) * (RIM + ROWS))):
        size = ref.shape[0] * EC
        unit, _ = unit_of(ref[...].reshape(size, D).astype(F32))
        part = gne_o[pl.ds(pl.multiple_of(at * EC, EC), size), :]
        gain_in = gain_in + jnp.sum(part * unit, axis=0, keepdims=True)
    spread = jnp.concatenate([gain_in, gain_mid[...], jnp.zeros((14, D), F32)], axis=0).astype(BF16)
    gain_o[...] = spread
    send_o[15] = spread


def add2(a, b):
    return (a.astype(F32) + b.astype(F32)).astype(BF16)


def add4(parts):
    a, b, c, d = [v.astype(F32) for v in parts]
    return ((a + b) + (c + d)).astype(BF16)


def halves():
    return ((0, (1, 2), (0, 3)), (1, (3, 2), (0, 1)))


def join_down_kv_kernel(dk, dg, kk, kg, gk, gg, *outs):
    gain = add2(gk[...], gg[15])
    for h, away, stay in halves():
        for out, chunks in ((outs[h], away), (outs[2 + h], stay)):
            for i, d in enumerate(chunks):
                lo, at = d * 16 + h * 8, i * 12
                out[at : at + 8] = add2(dk[lo : lo + 8], dg[lo : lo + 8])
                lo = 16 + d * 8 + h * 4
                out[at + 8 : at + 12] = add2(kk[lo : lo + 4], kg[lo : lo + 4])
    outs[0][24] = gain
    outs[2][24] = gain


def join_up_q_kernel(uk, ug, kk, kg, *outs):
    for h, away, stay in halves():
        for out, chunks in ((outs[h], away), (outs[2 + h], stay)):
            for i, d in enumerate(chunks):
                lo, at = d * 20 + h * 10, i * 12
                out[at : at + 10] = add2(uk[lo : lo + 10], ug[lo : lo + 10])
                lo = d * 4 + h * 2
                out[at + 10 : at + 12] = add2(kk[lo : lo + 2], kg[lo : lo + 2])


def second_kernel(p_got, q_got, p_keep, q_keep, p_send, q_send, p_own, q_own):
    p_own[:12] = add2(p_keep[:12], p_got[:12])
    p_send[:12] = add2(p_keep[12:24], p_got[12:24])
    q_own[...] = add2(q_keep[:12], q_got[:12])
    q_send[...] = add2(q_keep[12:], q_got[12:])
    if p_keep.shape[0] == 25:
        gain = add2(p_keep[24], p_got[24])
        p_own[12] = gain
        p_send[12] = gain


def sum_up_q_kernel(p_got, q_got, p_own, q_own, *outs):
    for h, got, own in ((0, p_got, p_own), (1, q_got, q_own)):
        for i in range(2):
            outs[2 * h + i][:5] = add2(got[i * 5 : i * 5 + 5], own[i * 5 : i * 5 + 5])
            outs[2 * h + i][5] = add2(got[10 + i], own[10 + i])


def sum_down_kv_kernel(p_got, q_got, p_own, q_own, ride, *outs):
    gain = add2(p_got[12], p_own[12])
    for h, got, own in ((0, p_got, p_own), (1, q_got, q_own)):
        for i in range(2):
            out = outs[2 * h + i]
            out[:4] = add2(got[i * 4 : i * 4 + 4], own[i * 4 : i * 4 + 4])
            out[4:6] = add2(got[8 + i * 2 : 10 + i * 2], own[8 + i * 2 : 10 + i * 2])
            out[6] = gain
    outs[1][7:9] = ride[...]


def reduce_xy_kernel(*refs):
    out, flat_s = refs[8:]
    sums = [add4([r[...] for r in refs[:4]]).reshape(-1, D), add4([r[:7] for r in refs[4:8]]).reshape(-1, D)]
    acc = jnp.concatenate(sums, axis=0)
    rows = acc.shape[0]
    per = ZROWS // 4
    i = lax.broadcasted_iota(jnp.int32, (8 * per, rows), 0)
    lane = lax.broadcasted_iota(jnp.int32, (8 * per, rows), 1)
    z = i // per
    r = i % per
    up = (r % 4) * 16 + z * 2 + r // 4
    down = 96 + z * 8 + (r - 8)
    o = 64 + z * 2 + (r - 16)
    part = (r - 18) % 3
    qkv = jnp.where(part == 0, 80, 144 + part * 16) + z * 2 + (r - 18) // 3
    gain = 192 + (r - 24)
    src = jnp.where(r < 8, up, jnp.where(r < 16, down, jnp.where(r < 18, o, jnp.where(r < 24, qkv, gain))))
    picked = nn(jnp.where((lane == src) & (r < 26), 1.0, 0.0).astype(BF16), acc)
    for j in range(4):
        flat_s[pl.ds(j, 8 * per, stride=4), :] = picked[:, j * 128 : (j + 1) * 128]
    out[...] = flat_s[...].astype(BF16).reshape(8, ZROWS, 128)


def reduce_z_kernel(got, up, down, o, qkv, gain):
    acc = got[0].astype(F32)
    for j in range(1, 8):
        acc = acc + got[j].astype(F32)
    acc = acc * (1.0 / math.sqrt(GRID_ROWS * GRID_COLS))
    at = 0
    for ref in (up, down, o, qkv):
        ref[...] = acc[at : at + ref.shape[0]]
        at += ref.shape[0]
    for r in range(2):
        for j in range(4):
            gain[r : r + 1, j * 128 : (j + 1) * 128] = acc[at + 4 * r + j : at + 4 * r + j + 1]


def call(body, outs, scratch, n_smem, n_in, flops, nbytes, mib):
    smem = pl.BlockSpec(memory_space=pltpu.SMEM)
    vmem = pl.BlockSpec(memory_space=pltpu.VMEM)
    return pl.pallas_call(
        body,
        out_shape=[jax.ShapeDtypeStruct(s, d) for s, d in outs],
        in_specs=[smem] * n_smem + [vmem] * n_in,
        out_specs=[vmem] * len(outs),
        scratch_shapes=scratch,
        compiler_params=pltpu.CompilerParams(vmem_limit_bytes=mib * 1024 * 1024),
        cost_estimate=pl.CostEstimate(flops=flops, bytes_accessed=nbytes, transcendentals=0),
    )


def pairs(stride, count, first):
    out = []
    for k in range(256):
        at = (k // stride) % count
        other = at + 1 if (at - first) % 2 == 0 else at - 1
        if 0 <= other < count:
            out.append((k, k + (other - at) * stride))
    return out


ROW_A, ROW_B = pairs(N_COL, 8, 1), pairs(N_COL, 8, 0)
COL_A, COL_B = pairs(1, N_COL, 1), pairs(1, N_COL, 0)
CORE_SWAP = [(k, k ^ 1) for k in range(256)]
X_BIT = 32
Y_BIT = 8
Z_GROUPS = [[zh * 128 + x * 32 + y * 8 + zl * 2 + c for zh in range(2) for zl in range(4)] for x in range(4) for y in range(4) for c in range(2)]


def send(x, perm):
    return lax.ppermute(x, AXES, perm)


def by(bits):
    return [(k, k ^ bits) for k in range(256)]


def to_three(chunks, bit):
    return [chunks[0]] + [send(chunks[d], by(bit * d)) for d in (1, 3, 2)]


def exchange(x, groups):
    return lax.all_to_all(x, AXES, 0, 0, axis_index_groups=groups, tiled=True)


def per_device(tokens, cotangent, gains, w_qkv, w_out, w_up, w_down, tile_mask):
    row = lax.axis_index("row")
    col = lax.axis_index("col")
    coord = jnp.stack([row, col, row * N_COL + col]).astype(jnp.int32)
    tok = tokens.reshape(TOK, D)
    cot = cotangent.reshape(TOK, D)

    row_odd = (row & 1) == 1
    col_odd = (col & 1) == 1
    first, last = tokens[:, :RIM], tokens[:, COLS - RIM :]
    side_b = send(jnp.where(col_odd, first, last), COL_B)
    side_a = send(jnp.where(col_odd, last, first), COL_A)
    (bias,) = call(
        prep_mask_kernel, [((TILES, QT, KT), F32)], [], 2, 0, 2 * TOK * D * FF, 4_000_000, 8,
    )(coord, tile_mask)
    side_a, side_b, cot, bias, coord = lax.optimization_barrier((side_a, side_b, cot, bias, coord))
    mid = jnp.concatenate([tokens, side_a, side_b, jnp.zeros((ROWS, EC - COLS - 2 * RIM, D), BF16)], axis=1)
    rim_b = send(jnp.where(row_odd, mid[:RIM], mid[ROWS - RIM :]), ROW_B)
    rim_a = send(jnp.where(row_odd, mid[ROWS - RIM :], mid[:RIM]), ROW_A)
    pt_u, pt_k, pt_d = call(
        prep_order_kernel, [((D, D), BF16)] * 3, [], 1, 0, 2 * TOK * D * FF, 4_000_000, 8,
    )(coord)
    (gact,) = call(
        prep_front_kernel, [((TOK, FF), F32)], [], 0, 2, 2 * TOK * D * FF, 4_000_000, 8,
    )(cot, w_down)

    q, no, ne_mid, kv_mid, p_mid, attn_mid = call(
        middle_kernel,
        [
            ((TOK, D), BF16), ((TOK, D), BF16), ((ROWS * EC, D), BF16), ((ROWS * EC, 2 * D), BF16),
            ((2, 256, KT), F32), ((QT, D), BF16),
        ],
        [], 0, 5, 600_000_000, 5_000_000, 10,
    )(mid, tok, gains, w_qkv, bias)

    half_u, half_d = ((16, 5, 16, D), BF16), ((4, 4, 2, 32, D), BF16)
    half_q, half_k = ((16, 16, D), BF16), ((48, 16, D), BF16)
    u_keep, u_send, d_keep, d_send, gm, kv, p_out, ne, gain_mid = call(
        forward_kernel,
        [
            half_u, half_u, half_d, half_d, ((TOK, D), BF16), ((EXT, 2 * D), BF16), ((4, 256, KT), F32),
            ((EXT, D), BF16), ((1, D), F32),
        ],
        [pltpu.VMEM((TOK, D), BF16)], 1, 16, 4_000_000_000, 20_000_000, 16,
    )(coord, rim_a, rim_b, tok, cot, gains, w_qkv, w_out, w_up, gact, bias, pt_u, pt_d, q, ne_mid, kv_mid, attn_mid)

    u_got = send(u_send, CORE_SWAP)
    d_got = send(d_send, CORE_SWAP)
    k_keep, k_send, dq, dkv = call(
        backward_kernel,
        [half_k, half_k, ((TOK, D), BF16), ((EXT, 2 * D), BF16)],
        [pltpu.VMEM((EXT, 2 * D), F32)], 0, 10, 2_500_000_000, 10_000_000, 12,
    )(gm, w_out, q, kv, p_mid, p_out, ne, no, pt_u, pt_k)
    u_got, d_got, k_send = lax.optimization_barrier((u_got, d_got, k_send))
    k_got = send(k_send, CORE_SWAP)
    gne, gnq, g_keep, g_send = call(
        inputs_kernel,
        [(((ROWS + 2 * RIM) * EC, D), F32), ((TOK, D), F32), ((16, D), BF16), half_q],
        [], 1, 8, 600_000_000, 4_000_000, 6,
    )(coord, dq, dkv, w_qkv, mid, rim_a, rim_b, tok, gain_mid)
    g_got = send(g_send, CORE_SWAP)

    def place(x, axis, odd, end_if_odd, size):
        gap = size - RIM
        after = [(0, 0)] * 3
        before = [(0, 0)] * 3
        after[axis], before[axis] = (0, gap), (gap, 0)
        x = x.astype(F32)
        x_odd, x_even = (before, after) if end_if_odd else (after, before)
        return jnp.where(odd, jnp.pad(x, x_odd), jnp.pad(x, x_even))

    def join(body, ins, outs):
        return list(call(body, [(o, BF16) for o in outs], [], 0, len(ins), 1_000_000, 4_000_000, 6)(*ins))

    def first(sent, bit):
        return send(sent[0], by(bit)), send(sent[1], by(3 * bit))

    def second(sent, bit):
        return send(sent[0], by(3 * bit)), send(sent[1], by(bit))

    k_got, gnq = lax.optimization_barrier((k_got, gnq))
    u_p, u_q, *u_stay = join(
        join_up_q_kernel, [u_keep.reshape(80, 16, D), u_got.reshape(80, 16, D), k_keep, k_got], [(24, 16, D)] * 4,
    )
    u_first = first((u_p, u_q), X_BIT)
    b_p, b_q, *b_stay = join(
        join_down_kv_kernel, [d_keep.reshape(64, 16, D), d_got.reshape(64, 16, D), k_keep, k_got, g_keep, g_got],
        [(25, 16, D), (24, 16, D)] * 2,
    )
    gne3 = gne.reshape(ROWS + 2 * RIM, EC, D)
    side = gne3[:, COLS : COLS + RIM].astype(BF16)
    b_first = first((b_p, b_q), Y_BIT)
    back_a = send(side, COL_A)
    b_first, back_a, g_got = lax.optimization_barrier((b_first, back_a, g_got))
    u_p, u_q, *u_own = join(second_kernel, [*u_first, *u_stay], [(12, 16, D)] * 4)
    u_second = second((u_p, u_q), X_BIT)
    b_p, b_q, *b_own = join(second_kernel, [*b_first, *b_stay], [(13, 16, D), (12, 16, D)] * 2)
    b_second = second((b_p, b_q), Y_BIT)
    back_b = g_got[:15].reshape(ROWS + 2 * RIM, COLS, D)[:, RIM : 2 * RIM]
    own = gne3[:, :COLS] + place(back_a, 1, col_odd, True, COLS) + place(back_b, 1, col_odd, False, COLS)
    head, tail = own[:RIM].astype(BF16), own[RIM + ROWS :].astype(BF16)
    ride = jnp.pad(jnp.where(row_odd, head, tail), ((0, 1), (0, 0), (0, 0))).reshape(2, 16, D)
    u = join(sum_up_q_kernel, [*u_second, *u_own], [(6, 16, D)] * 4)
    u = to_three(u, Y_BIT)
    b = join(sum_down_kv_kernel, [*b_second, *b_own, ride], [(7, 16, D), (9, 16, D), (7, 16, D), (7, 16, D)])
    b = to_three(b, X_BIT)
    up_b = b[1][7:].reshape(4, COLS, D)[:RIM]
    (spread,) = call(
        reduce_xy_kernel, [((8, ZROWS, 128), BF16)], [pltpu.VMEM((8 * ZROWS, 128), F32)], 0, 8, 60_000_000, 4_000_000, 5,
    )(*u, *b)
    up_a = send(jnp.where(row_odd, tail, head), ROW_A)
    got_z = exchange(spread, Z_GROUPS)
    got_z, up_a = lax.optimization_barrier((got_z, up_a))
    g_up, g_down, g_out, g_qkv, g_gains = call(
        reduce_z_kernel,
        [((32, 128), F32), ((32, 128), F32), ((8, 128), F32), ((24, 128), F32), ((2, D), F32)],
        [], 0, 1, 100_000_000_000, 400_000, 4,
    )(got_z)

    gn = own[RIM : RIM + ROWS] + place(up_a, 0, row_odd, True, ROWS) + place(up_b, 0, row_odd, False, ROWS)
    gn = gn + gnq.reshape(ROWS, COLS, D)
    unit, inv = unit_of(tokens.astype(F32))
    g1 = gn * gains[0]
    front = inv * (g1 - unit * jnp.mean(g1 * unit, axis=-1, keepdims=True))
    grad_tokens = (gm.reshape(ROWS, COLS, D).astype(F32) + front).astype(BF16)
    return (grad_tokens, g_qkv.reshape(-1), g_out.reshape(-1), g_up.reshape(-1), g_down.reshape(-1), g_gains)


def solution(mesh):
    block = P("row", "col", None)
    flat = P(("row", "col"))
    return jax.shard_map(
        per_device,
        mesh=mesh,
        in_specs=(block, block, P(), P(), P(), P(), P(), block),
        out_specs=(block, flat, flat, flat, flat, P()),
        check_vma=False,
    )
```

```python
import math

import jax
import jax.numpy as jnp
from jax import lax
from jax.experimental import pallas as pl
from jax.experimental.pallas import tpu as pltpu
from jax.sharding import PartitionSpec as P

D = 512
FF = 2048
HEADS = 8
WINDOW = 7
TILE = 8
RIM = WINDOW // 2
EPS = 1e-06
AXES = ("row", "col")
N_COL = 32
GRID_ROWS = 192
GRID_COLS = 256
ROWS = 24
COLS = 8
TOK = ROWS * COLS
TILES = ROWS // TILE
ER = 32
EC = 16
EXT = ER * EC
QT = TILE * TILE
ZROWS = 112
KT = 256
F32 = jnp.float32
BF16 = jnp.bfloat16
GELU_C = math.sqrt(2.0 / math.pi)


def nn(a, b):
    return lax.dot_general(a, b, (((1,), (0,)), ((), ())), preferred_element_type=F32)


def nt(a, b):
    return lax.dot_general(a, b, (((1,), (1,)), ((), ())), preferred_element_type=F32)


def tn(a, b):
    return lax.dot_general(a, b, (((0,), (0,)), ((), ())), preferred_element_type=F32)


def unit_of(x):
    inv = lax.rsqrt(jnp.mean(x * x, axis=-1, keepdims=True) + EPS)
    return x * inv, inv


def head_mask(rows, h):
    lane = lax.broadcasted_iota(jnp.int32, (rows, 256), 1)
    return (lane // 64) == h


def stack_heads(x):
    zero = jnp.zeros_like(x)
    return jnp.concatenate([jnp.where(head_mask(x.shape[0], h), x, zero) for h in range(4)], axis=0)


def unstack_heads(x):
    rows = x.shape[0] // 4
    out = jnp.where(head_mask(rows, 0), x[:rows], 0.0)
    for h in range(1, 4):
        out = out + jnp.where(head_mask(rows, h), x[h * rows : (h + 1) * rows], 0.0)
    return out


def prep_front_kernel(cot, w_down, gact):
    for c in range(4):
        gact[:, c * 512 : (c + 1) * 512] = nt(cot[...], w_down[c * 512 : (c + 1) * 512, :])


def prep_mask_kernel(coord, mask, bias):
    q = lax.broadcasted_iota(jnp.int32, (QT, KT), 0)
    k = lax.broadcasted_iota(jnp.int32, (QT, KT), 1)
    ki = k // EC
    kc = k % EC
    odd = coord[1] & 1
    near = kc - COLS + odd * (COLS + RIM)
    far = kc - COLS - RIM + (1 - odd) * (COLS + RIM)
    kj = jnp.where(kc < COLS, kc + RIM, jnp.where(kc < COLS + RIM, near, jnp.where(kc < COLS + 2 * RIM, far, -99)))
    da = ki - q // TILE
    db = kj - q % TILE
    slot = jnp.where((da >= 0) & (da < WINDOW) & (db >= 0) & (db < WINDOW), da * WINDOW + db, -1)
    allowed = [jnp.zeros((QT, KT), jnp.int32) for _ in range(TILES)]
    for s in range(WINDOW * WINDOW):
        here = slot == s
        for t in range(TILES):
            allowed[t] = jnp.where(here, mask[t, 0, s], allowed[t])
    gc = coord[1] * COLS + kj - RIM
    for t in range(TILES):
        gr = coord[0] * ROWS + t * TILE + ki - RIM
        ok = (allowed[t] == 1) & (gr >= 0) & (gr < GRID_ROWS) & (gc >= 0) & (gc < GRID_COLS)
        bias[t] = jnp.where(ok, 0.0, -1e30)


def prep_order_kernel(coord, pt_u, pt_k, pt_d):
    me = coord[2]
    lane = lax.broadcasted_iota(jnp.int32, (512, 512), 1)
    p = lax.broadcasted_iota(jnp.int32, (512, 512), 0)
    core_z = ((p >> 3) & 1) * 128 + ((p >> 1) & 3) * 2 + (p >> 8)
    hi, lo = (p >> 6) & 3, (p >> 4) & 3
    here = me & 121
    pt_u[...] = jnp.where(lane == ((core_z + hi * 32 + lo * 8) ^ here) * 2 + (p & 1), 1.0, 0.0).astype(BF16)
    pt_k[...] = jnp.where(lane == ((core_z + hi * 8 + lo * 32) ^ here) * 2 + (p & 1), 1.0, 0.0).astype(BF16)
    k_d = (((p >> 5) & 1) * 32 + ((p >> 6) & 3) * 8 + ((p >> 3) & 3) * 2 + (p >> 8)) ^ (me & 57)
    pt_d[...] = jnp.where(lane == k_d * 8 + (p & 7), 1.0, 0.0).astype(BF16)


def attend(qt, keys, vals, bias_t):
    s = nt(stack_heads(qt), keys) * 0.125 + jnp.concatenate([bias_t] * 4, axis=0)
    e = jnp.exp(s - jnp.max(s, axis=-1, keepdims=True))
    prob = e / jnp.sum(e, axis=-1, keepdims=True)
    return prob, unstack_heads(nn(prob.astype(BF16), vals)).astype(BF16)


def middle_kernel(mid, tok, gains, w_qkv, bias, q_o, no_o, ne_o, kv_o, p_o, attn_o):
    unit_e, _ = unit_of(mid[...].reshape(ROWS * EC, D).astype(F32))
    ne = (unit_e * gains[0:1, :]).astype(BF16)
    ne_o[...] = ne
    kv_o[...] = nn(ne, w_qkv[:, D:]).astype(BF16)
    unit_o, _ = unit_of(tok[...].astype(F32))
    no = (unit_o * gains[0:1, :]).astype(BF16)
    no_o[...] = no
    q_o[...] = nn(no, w_qkv[:, :D]).astype(BF16)
    at = 128 - RIM * EC
    for g in range(2):
        cols = slice(g * 256, (g + 1) * 256)
        vcols = slice(D + g * 256, D + (g + 1) * 256)
        prob, o = attend(q_o[QT : 2 * QT, cols], kv_o[at : at + KT, cols], kv_o[at : at + KT, vcols], bias[1])
        p_o[g] = prob
        attn_o[:, cols] = o


def forward_kernel(
    coord, rim_a, rim_b, tok, cot, gains, w_qkv, w_out, w_up, gact, bias, pt_u, pt_d, q_i, ne_i, kv_i, attn_i,
    u_keep, u_send, d_keep, d_send, gm_o, kv_o, p_o, ne_o, gain_o, attn_s,
):
    odd = coord[0] & 1
    edge = RIM * EC
    at_a = pl.multiple_of(odd * (RIM + ROWS) * EC, EC)
    at_b = pl.multiple_of((1 - odd) * (RIM + ROWS) * EC, EC)
    end = (RIM + ROWS) * EC
    both = jnp.concatenate([rim_a[...].reshape(edge, D), rim_b[...].reshape(edge, D)], axis=0)
    unit_r, _ = unit_of(both.astype(F32))
    ne_r = (unit_r * gains[0:1, :]).astype(BF16)
    kv_r = nn(ne_r, w_qkv[:, D:]).astype(BF16)
    for ref, mid, rims in ((ne_o, ne_i, ne_r), (kv_o, kv_i, kv_r)):
        ref[edge:end, :] = mid[...]
        ref[pl.ds(at_a, edge), :] = rims[:edge]
        ref[pl.ds(at_b, edge), :] = rims[edge:]
        ref[end + edge :, :] = jnp.zeros((EXT - end - edge, ref.shape[1]), BF16)
    xt = tok[...].astype(F32)
    attn_s[QT : 2 * QT, :] = attn_i[...]
    for i, t in enumerate((0, 2)):
        rows = slice(t * 128, t * 128 + KT)
        for g in range(2):
            cols = slice(g * 256, (g + 1) * 256)
            vcols = slice(D + g * 256, D + (g + 1) * 256)
            prob, o = attend(q_i[t * QT : (t + 1) * QT, cols], kv_o[rows, cols], kv_o[rows, vcols], bias[t])
            p_o[i * 2 + g] = prob
            attn_s[t * QT : (t + 1) * QT, cols] = o
    attn = attn_s[...]
    mixed = (xt + nn(attn, w_out[...])).astype(BF16)
    um, inv_m = unit_of(mixed.astype(F32))
    nm = (um * gains[1:2, :]).astype(BF16)
    nmt = nt(pt_u[...], nm).astype(BF16)
    gn = jnp.zeros((TOK, D), F32)
    for c in range(4):
        cols = slice(c * 512, (c + 1) * 512)
        pre = nn(nm, w_up[:, cols])
        th = jnp.tanh(GELU_C * (pre + 0.044715 * (pre * pre * pre)))
        half = 0.5 * (1.0 + th)
        act = (pre * half).astype(BF16)
        slope = half + 0.5 * pre * (1.0 - th * th) * (GELU_C * (1.0 + 0.134145 * (pre * pre)))
        gp = (gact[:, cols] * slope).astype(BF16)
        gn = gn + nt(gp, w_up[:, cols])
        gu = nn(nmt, gp).astype(BF16)
        u_keep[:, c] = gu[:256].reshape(16, 16, D)
        u_send[:, c] = gu[256:].reshape(16, 16, D)
        act_t = nt(pt_d[...], act).astype(BF16)
        gd = nn(act_t, cot[...]).astype(BF16)
        xh = (c & 1) ^ ((coord[2] >> 6) & 1)
        for y in range(4):
            for xl in range(2):
                at = (y * 2 + xl) * 32
                d_keep[y, xh * 2 + xl, c >> 1] = gd[at : at + 32]
                d_send[y, xh * 2 + xl, c >> 1] = gd[256 + at : 256 + at + 32]
    g = gn * gains[1:2, :]
    gm = (cot[...].astype(F32) + inv_m * (g - um * jnp.mean(g * um, axis=-1, keepdims=True))).astype(BF16)
    gm_o[...] = gm
    gain_o[...] = jnp.sum(gn * um, axis=0, keepdims=True)
    go = nn(nt(pt_u[...], attn).astype(BF16), gm).astype(BF16)
    u_keep[:, 4] = go[:256].reshape(16, 16, D)
    u_send[:, 4] = go[256:].reshape(16, 16, D)


def backward_kernel(
    gm, w_out, q, kv, p_mid, p_out, ne, no, pt_u, pt_k,
    k_keep, k_send, dq_s, dkv_o, dkv_s,
):
    ga = nt(gm[...], w_out[...]).astype(BF16)
    dkv_s[...] = jnp.zeros_like(dkv_s)
    for t in range(TILES):
        for g in range(2):
            cols = slice(g * 256, (g + 1) * 256)
            vcols = slice(D + g * 256, D + (g + 1) * 256)
            rows = slice(t * 128, t * 128 + KT)
            prob = p_mid[g] if t == 1 else p_out[t + g]
            gas = stack_heads(ga[t * QT : (t + 1) * QT, cols])
            qs = stack_heads(q[t * QT : (t + 1) * QT, cols])
            gp = nt(gas, kv[rows, vcols])
            inner = jnp.sum(prob * gp, axis=-1, keepdims=True)
            ds = (prob * (gp - inner) * 0.125).astype(BF16)
            dq_s[t * QT : (t + 1) * QT, cols] = unstack_heads(nn(ds, kv[rows, cols])).astype(BF16)
            dkv_s[rows, cols] += tn(ds, qs)
            dkv_s[rows, vcols] += tn(prob.astype(BF16), gas)
    dkv = dkv_s[...].astype(BF16)
    dkv_o[...] = dkv
    gk = nn(nt(pt_k[...], ne[...]).astype(BF16), dkv).astype(BF16)
    gq = nn(nt(pt_u[...], no[...]).astype(BF16), dq_s[...]).astype(BF16)
    for at, out in ((0, k_keep), (256, k_send)):
        out[:16] = gq[at : at + 256].reshape(16, 16, D)
        for i in range(2):
            for j in range(16):
                out[16 + j * 2 + i] = gk[at + j * 16 : at + j * 16 + 16, i * D : (i + 1) * D]


def inputs_kernel(coord, dq, dkv, w_qkv, mid, rim_a, rim_b, tok, gain_mid, gne_o, gnq_o, gain_o, row_a, row_b):
    gne = nt(dkv[...], w_qkv[:, D:])
    gnq = nt(dq[...], w_qkv[:, :D])
    gne_o[...] = gne[: (ROWS + 2 * RIM) * EC]
    gnq_o[...] = gnq
    gain_in = jnp.sum(gnq * unit_of(tok[...].astype(F32))[0], axis=0, keepdims=True)
    odd = coord[0] & 1
    for ref, at in ((rim_a, odd * (RIM + ROWS)), (mid, RIM), (rim_b, (1 - odd) * (RIM + ROWS))):
        size = ref.shape[0] * EC
        unit, _ = unit_of(ref[...].reshape(size, D).astype(F32))
        part = gne_o[pl.ds(pl.multiple_of(at * EC, EC), size), :]
        gain_in = gain_in + jnp.sum(part * unit, axis=0, keepdims=True)
    spread = jnp.concatenate([gain_in, gain_mid[...], jnp.zeros((14, D), F32)], axis=0).astype(BF16)
    gain_o[...] = spread
    for ref, at in ((row_a, odd * (RIM + ROWS)), (row_b, (1 - odd) * (RIM + ROWS))):
        rim = gne_o[pl.ds(pl.multiple_of(at * EC, EC), RIM * EC), :]
        ref[...] = rim.astype(BF16).reshape(RIM, EC, D)


def add2(a, b):
    return (a.astype(F32) + b.astype(F32)).astype(BF16)


def add4(parts):
    a, b, c, d = [v.astype(F32) for v in parts]
    return ((a + b) + (c + d)).astype(BF16)


def halves():
    return ((0, (1, 2), (0, 3)), (1, (3, 2), (0, 1)))


def join_down_kv_kernel(dk, dg, kk, kg, gk, gg, *outs):
    gain = add2(gk[...], gg[...])
    for h, away, stay in halves():
        for out, chunks in ((outs[h], away), (outs[2 + h], stay)):
            for i, d in enumerate(chunks):
                lo, at = d * 16 + h * 8, i * 12
                out[at : at + 8] = add2(dk[lo : lo + 8], dg[lo : lo + 8])
                lo = 16 + d * 8 + h * 4
                out[at + 8 : at + 12] = add2(kk[lo : lo + 4], kg[lo : lo + 4])
    outs[0][24] = gain
    outs[2][24] = gain


def join_up_q_kernel(uk, ug, kk, kg, ride, *outs):
    outs[0][24:] = ride[...]
    for h, away, stay in halves():
        for out, chunks in ((outs[h], away), (outs[2 + h], stay)):
            for i, d in enumerate(chunks):
                lo, at = d * 20 + h * 10, i * 12
                out[at : at + 10] = add2(uk[lo : lo + 10], ug[lo : lo + 10])
                lo = d * 4 + h * 2
                out[at + 10 : at + 12] = add2(kk[lo : lo + 2], kg[lo : lo + 2])


def second_kernel(p_got, q_got, p_keep, q_keep, p_send, q_send, p_own, q_own):
    p_own[:12] = add2(p_keep[:12], p_got[:12])
    p_send[:12] = add2(p_keep[12:24], p_got[12:24])
    q_own[...] = add2(q_keep[:12], q_got[:12])
    q_send[...] = add2(q_keep[12:], q_got[12:])
    if p_keep.shape[0] == 25:
        gain = add2(p_keep[24], p_got[24])
        p_own[12] = gain
        p_send[12] = gain


def sum_up_q_kernel(p_got, q_got, p_own, q_own, *outs):
    for h, got, own in ((0, p_got, p_own), (1, q_got, q_own)):
        for i in range(2):
            outs[2 * h + i][:5] = add2(got[i * 5 : i * 5 + 5], own[i * 5 : i * 5 + 5])
            outs[2 * h + i][5] = add2(got[10 + i], own[10 + i])


def sum_down_kv_kernel(p_got, q_got, p_own, q_own, *outs):
    gain = add2(p_got[12], p_own[12])
    for h, got, own in ((0, p_got, p_own), (1, q_got, q_own)):
        for i in range(2):
            out = outs[2 * h + i]
            out[:4] = add2(got[i * 4 : i * 4 + 4], own[i * 4 : i * 4 + 4])
            out[4:6] = add2(got[8 + i * 2 : 10 + i * 2], own[8 + i * 2 : 10 + i * 2])
            out[6] = gain


def reduce_xy_kernel(*refs):
    out, flat_s = refs[8:]
    sums = [add4([r[...] for r in refs[:4]]).reshape(-1, D), add4([r[...] for r in refs[4:8]]).reshape(-1, D)]
    acc = jnp.concatenate(sums, axis=0)
    rows = acc.shape[0]
    per = ZROWS // 4
    i = lax.broadcasted_iota(jnp.int32, (8 * per, rows), 0)
    lane = lax.broadcasted_iota(jnp.int32, (8 * per, rows), 1)
    z = i // per
    r = i % per
    up = (r % 4) * 16 + z * 2 + r // 4
    down = 96 + z * 8 + (r - 8)
    o = 64 + z * 2 + (r - 16)
    part = (r - 18) % 3
    qkv = jnp.where(part == 0, 80, 144 + part * 16) + z * 2 + (r - 18) // 3
    gain = 192 + (r - 24)
    src = jnp.where(r < 8, up, jnp.where(r < 16, down, jnp.where(r < 18, o, jnp.where(r < 24, qkv, gain))))
    picked = nn(jnp.where((lane == src) & (r < 26), 1.0, 0.0).astype(BF16), acc)
    for j in range(4):
        flat_s[pl.ds(j, 8 * per, stride=4), :] = picked[:, j * 128 : (j + 1) * 128]
    out[...] = flat_s[...].astype(BF16).reshape(8, ZROWS, 128)


def reduce_z_kernel(got, up, down, o, qkv, gain):
    acc = got[0].astype(F32)
    for j in range(1, 8):
        acc = acc + got[j].astype(F32)
    acc = acc * (1.0 / math.sqrt(GRID_ROWS * GRID_COLS))
    at = 0
    for ref in (up, down, o, qkv):
        ref[...] = acc[at : at + ref.shape[0]]
        at += ref.shape[0]
    for r in range(2):
        for j in range(4):
            gain[r : r + 1, j * 128 : (j + 1) * 128] = acc[at + 4 * r + j : at + 4 * r + j + 1]


def call(body, outs, scratch, n_smem, n_in, flops, nbytes, mib):
    smem = pl.BlockSpec(memory_space=pltpu.SMEM)
    vmem = pl.BlockSpec(memory_space=pltpu.VMEM)
    return pl.pallas_call(
        body,
        out_shape=[jax.ShapeDtypeStruct(s, d) for s, d in outs],
        in_specs=[smem] * n_smem + [vmem] * n_in,
        out_specs=[vmem] * len(outs),
        scratch_shapes=scratch,
        compiler_params=pltpu.CompilerParams(vmem_limit_bytes=mib * 1024 * 1024),
        cost_estimate=pl.CostEstimate(flops=flops, bytes_accessed=nbytes, transcendentals=0),
    )


def pairs(stride, count, first):
    out = []
    for k in range(256):
        at = (k // stride) % count
        other = at + 1 if (at - first) % 2 == 0 else at - 1
        if 0 <= other < count:
            out.append((k, k + (other - at) * stride))
    return out


ROW_A, ROW_B = pairs(N_COL, 8, 1), pairs(N_COL, 8, 0)
COL_A, COL_B = pairs(1, N_COL, 1), pairs(1, N_COL, 0)
CORE_SWAP = [(k, k ^ 1) for k in range(256)]
X_BIT = 32
Y_BIT = 8
Z_GROUPS = [[zh * 128 + x * 32 + y * 8 + zl * 2 + c for zh in range(2) for zl in range(4)] for x in range(4) for y in range(4) for c in range(2)]


def send(x, perm):
    return lax.ppermute(x, AXES, perm)


def by(bits):
    return [(k, k ^ bits) for k in range(256)]


def to_three(chunks, bit):
    return [chunks[0]] + [send(chunks[d], by(bit * d)) for d in (1, 3, 2)]


def exchange(x, groups):
    return lax.all_to_all(x, AXES, 0, 0, axis_index_groups=groups, tiled=True)


def per_device(tokens, cotangent, gains, w_qkv, w_out, w_up, w_down, tile_mask):
    row = lax.axis_index("row")
    col = lax.axis_index("col")
    coord = jnp.stack([row, col, row * N_COL + col]).astype(jnp.int32)
    tok = tokens.reshape(TOK, D)
    cot = cotangent.reshape(TOK, D)

    row_odd = (row & 1) == 1
    col_odd = (col & 1) == 1
    first, last = tokens[:, :RIM], tokens[:, COLS - RIM :]
    side_b = send(jnp.where(col_odd, first, last), COL_B)
    side_a = send(jnp.where(col_odd, last, first), COL_A)
    (bias,) = call(
        prep_mask_kernel, [((TILES, QT, KT), F32)], [], 2, 0, 2 * TOK * D * FF, 4_000_000, 8,
    )(coord, tile_mask)
    side_a, side_b, cot, bias, coord = lax.optimization_barrier((side_a, side_b, cot, bias, coord))
    mid = jnp.concatenate([tokens, side_a, side_b, jnp.zeros((ROWS, EC - COLS - 2 * RIM, D), BF16)], axis=1)
    rim_b = send(jnp.where(row_odd, mid[:RIM], mid[ROWS - RIM :]), ROW_B)
    rim_a = send(jnp.where(row_odd, mid[ROWS - RIM :], mid[:RIM]), ROW_A)
    pt_u, pt_k, pt_d = call(
        prep_order_kernel, [((D, D), BF16)] * 3, [], 1, 0, 2 * TOK * D * FF, 4_000_000, 8,
    )(coord)
    (gact,) = call(
        prep_front_kernel, [((TOK, FF), F32)], [], 0, 2, 2 * TOK * D * FF, 4_000_000, 8,
    )(cot, w_down)

    q, no, ne_mid, kv_mid, p_mid, attn_mid = call(
        middle_kernel,
        [
            ((TOK, D), BF16), ((TOK, D), BF16), ((ROWS * EC, D), BF16), ((ROWS * EC, 2 * D), BF16),
            ((2, 256, KT), F32), ((QT, D), BF16),
        ],
        [], 0, 5, 600_000_000, 5_000_000, 10,
    )(mid, tok, gains, w_qkv, bias)

    half_u, half_d = ((16, 5, 16, D), BF16), ((4, 4, 2, 32, D), BF16)
    half_q, half_k = ((16, 16, D), BF16), ((48, 16, D), BF16)
    u_keep, u_send, d_keep, d_send, gm, kv, p_out, ne, gain_mid = call(
        forward_kernel,
        [
            half_u, half_u, half_d, half_d, ((TOK, D), BF16), ((EXT, 2 * D), BF16), ((4, 256, KT), F32),
            ((EXT, D), BF16), ((1, D), F32),
        ],
        [pltpu.VMEM((TOK, D), BF16)], 1, 16, 4_000_000_000, 20_000_000, 16,
    )(coord, rim_a, rim_b, tok, cot, gains, w_qkv, w_out, w_up, gact, bias, pt_u, pt_d, q, ne_mid, kv_mid, attn_mid)

    u_got = send(u_send, CORE_SWAP)
    d_got = send(d_send, CORE_SWAP)
    k_keep, k_send, dq, dkv = call(
        backward_kernel,
        [half_k, half_k, ((TOK, D), BF16), ((EXT, 2 * D), BF16)],
        [pltpu.VMEM((EXT, 2 * D), F32)], 0, 10, 2_500_000_000, 10_000_000, 12,
    )(gm, w_out, q, kv, p_mid, p_out, ne, no, pt_u, pt_k)
    u_got, d_got, k_send = lax.optimization_barrier((u_got, d_got, k_send))
    k_got = send(k_send, CORE_SWAP)
    gne, gnq, gain, row_a, row_b = call(
        inputs_kernel,
        [
            (((ROWS + 2 * RIM) * EC, D), F32), ((TOK, D), F32), ((16, D), BF16),
            ((RIM, EC, D), BF16), ((RIM, EC, D), BF16),
        ],
        [], 1, 8, 600_000_000, 4_000_000, 6,
    )(coord, dq, dkv, w_qkv, mid, rim_a, rim_b, tok, gain_mid)
    gain_got = send(gain, CORE_SWAP)

    def place(x, axis, odd, end_if_odd, size):
        gap = size - RIM
        after = [(0, 0)] * 3
        before = [(0, 0)] * 3
        after[axis], before[axis] = (0, gap), (gap, 0)
        x = x.astype(F32)
        x_odd, x_even = (before, after) if end_if_odd else (after, before)
        return jnp.where(odd, jnp.pad(x, x_odd), jnp.pad(x, x_even))

    def join(body, ins, outs):
        return list(call(body, [(o, BF16) for o in outs], [], 0, len(ins), 1_000_000, 4_000_000, 6)(*ins))

    def first(sent, bit):
        return send(sent[0], by(bit)), send(sent[1], by(3 * bit))

    def second(sent, bit):
        return send(sent[0], by(3 * bit)), send(sent[1], by(bit))

    k_got, gnq = lax.optimization_barrier((k_got, gnq))
    u_p, u_q, *u_stay = join(
        join_up_q_kernel, [u_keep.reshape(80, 16, D), u_got.reshape(80, 16, D), k_keep, k_got, row_b],
        [(27, 16, D)] + [(24, 16, D)] * 3,
    )
    u_first = first((u_p, u_q), X_BIT)
    b_p, b_q, *b_stay = join(
        join_down_kv_kernel, [d_keep.reshape(64, 16, D), d_got.reshape(64, 16, D), k_keep, k_got, gain, gain_got],
        [(25, 16, D), (24, 16, D)] * 2,
    )
    b_first = first((b_p, b_q), Y_BIT)
    row_a = send(row_a, ROW_A)
    b_first, row_a = lax.optimization_barrier((b_first, row_a))
    u_p, u_q, *u_own = join(second_kernel, [*u_first, *u_stay], [(12, 16, D)] * 4)
    u_second = second((u_p, u_q), X_BIT)
    b_p, b_q, *b_own = join(second_kernel, [*b_first, *b_stay], [(13, 16, D), (12, 16, D)] * 2)
    b_second = second((b_p, b_q), Y_BIT)
    gne = gne.reshape(ROWS + 2 * RIM, EC, D)[RIM : RIM + ROWS]
    gne = gne + place(row_a, 0, row_odd, True, ROWS) + place(u_first[0][24:], 0, row_odd, False, ROWS)
    u = join(sum_up_q_kernel, [*u_second, *u_own], [(6, 16, D)] * 4)
    u = to_three(u, Y_BIT)
    b = join(sum_down_kv_kernel, [*b_second, *b_own], [(7, 16, D)] * 4)
    b = to_three(b, X_BIT)
    (spread,) = call(
        reduce_xy_kernel, [((8, ZROWS, 128), BF16)], [pltpu.VMEM((8 * ZROWS, 128), F32)], 0, 8, 60_000_000, 4_000_000, 5,
    )(*u, *b)
    got_z = exchange(spread, Z_GROUPS)
    back_b = send(gne[:, COLS + RIM : COLS + 2 * RIM].astype(BF16), COL_B)
    back_a = send(gne[:, COLS : COLS + RIM].astype(BF16), COL_A)
    got_z, back_a, back_b = lax.optimization_barrier((got_z, back_a, back_b))
    g_up, g_down, g_out, g_qkv, g_gains = call(
        reduce_z_kernel,
        [((32, 128), F32), ((32, 128), F32), ((8, 128), F32), ((24, 128), F32), ((2, D), F32)],
        [], 0, 1, 100_000_000_000, 400_000, 4,
    )(got_z)

    gn = gne[:, :COLS] + place(back_a, 1, col_odd, True, COLS) + place(back_b, 1, col_odd, False, COLS)
    gn = gn + gnq.reshape(ROWS, COLS, D)
    unit, inv = unit_of(tokens.astype(F32))
    g1 = gn * gains[0]
    front = inv * (g1 - unit * jnp.mean(g1 * unit, axis=-1, keepdims=True))
    grad_tokens = (gm.reshape(ROWS, COLS, D).astype(F32) + front).astype(BF16)
    return (grad_tokens, g_qkv.reshape(-1), g_out.reshape(-1), g_up.reshape(-1), g_down.reshape(-1), g_gains)


def solution(mesh):
    block = P("row", "col", None)
    flat = P(("row", "col"))
    return jax.shard_map(
        per_device,
        mesh=mesh,
        in_specs=(block, block, P(), P(), P(), P(), P(), block),
        out_specs=(block, flat, flat, flat, flat, P()),
        check_vma=False,
    )
```

```python
import math

import jax
import jax.numpy as jnp
from jax import lax
from jax.experimental import pallas as pl
from jax.experimental.pallas import tpu as pltpu
from jax.sharding import PartitionSpec as P

D = 512
FF = 2048
HEADS = 8
WINDOW = 7
TILE = 8
RIM = WINDOW // 2
EPS = 1e-06
AXES = ("row", "col")
N_COL = 32
GRID_ROWS = 192
GRID_COLS = 256
ROWS = 24
COLS = 8
TOK = ROWS * COLS
TILES = ROWS // TILE
ER = 32
EC = 16
EXT = ER * EC
QT = TILE * TILE
ZROWS = 112
KT = 256
F32 = jnp.float32
BF16 = jnp.bfloat16
GELU_C = math.sqrt(2.0 / math.pi)


def nn(a, b):
    return lax.dot_general(a, b, (((1,), (0,)), ((), ())), preferred_element_type=F32)


def nt(a, b):
    return lax.dot_general(a, b, (((1,), (1,)), ((), ())), preferred_element_type=F32)


def tn(a, b):
    return lax.dot_general(a, b, (((0,), (0,)), ((), ())), preferred_element_type=F32)


def unit_of(x):
    inv = lax.rsqrt(jnp.mean(x * x, axis=-1, keepdims=True) + EPS)
    return x * inv, inv


def head_mask(rows, h):
    lane = lax.broadcasted_iota(jnp.int32, (rows, 256), 1)
    return (lane // 64) == h


def stack_heads(x):
    zero = jnp.zeros_like(x)
    return jnp.concatenate([jnp.where(head_mask(x.shape[0], h), x, zero) for h in range(4)], axis=0)


def unstack_heads(x):
    rows = x.shape[0] // 4
    out = jnp.where(head_mask(rows, 0), x[:rows], 0.0)
    for h in range(1, 4):
        out = out + jnp.where(head_mask(rows, h), x[h * rows : (h + 1) * rows], 0.0)
    return out


def prep_front_kernel(cot, w_down, gact):
    for c in range(4):
        gact[:, c * 512 : (c + 1) * 512] = nt(cot[...], w_down[c * 512 : (c + 1) * 512, :])


def prep_mask_kernel(coord, mask, bias):
    q = lax.broadcasted_iota(jnp.int32, (QT, KT), 0)
    k = lax.broadcasted_iota(jnp.int32, (QT, KT), 1)
    ki = k // EC
    kc = k % EC
    odd = coord[1] & 1
    near = kc - COLS + odd * (COLS + RIM)
    far = kc - COLS - RIM + (1 - odd) * (COLS + RIM)
    kj = jnp.where(kc < COLS, kc + RIM, jnp.where(kc < COLS + RIM, near, jnp.where(kc < COLS + 2 * RIM, far, -99)))
    da = ki - q // TILE
    db = kj - q % TILE
    slot = jnp.where((da >= 0) & (da < WINDOW) & (db >= 0) & (db < WINDOW), da * WINDOW + db, -1)
    allowed = [jnp.zeros((QT, KT), jnp.int32) for _ in range(TILES)]
    for s in range(WINDOW * WINDOW):
        here = slot == s
        for t in range(TILES):
            allowed[t] = jnp.where(here, mask[t, 0, s], allowed[t])
    gc = coord[1] * COLS + kj - RIM
    for t in range(TILES):
        gr = coord[0] * ROWS + t * TILE + ki - RIM
        ok = (allowed[t] == 1) & (gr >= 0) & (gr < GRID_ROWS) & (gc >= 0) & (gc < GRID_COLS)
        bias[t] = jnp.where(ok, 0.0, -1e30)


def prep_order_kernel(coord, pt_u, pt_k):
    me = coord[2]
    lane = lax.broadcasted_iota(jnp.int32, (512, 512), 1)
    p = lax.broadcasted_iota(jnp.int32, (512, 512), 0)
    core_z = ((p >> 3) & 1) * 128 + ((p >> 1) & 3) * 2 + (p >> 8)
    hi, lo = (p >> 6) & 3, (p >> 4) & 3
    here = me & 121
    pt_u[...] = jnp.where(lane == ((core_z + hi * 32 + lo * 8) ^ here) * 2 + (p & 1), 1.0, 0.0).astype(BF16)
    pt_k[...] = jnp.where(lane == ((core_z + hi * 8 + lo * 32) ^ here) * 2 + (p & 1), 1.0, 0.0).astype(BF16)


def attend(qt, keys, vals, bias_t):
    s = nt(stack_heads(qt), keys) * 0.125 + jnp.concatenate([bias_t] * 4, axis=0)
    e = jnp.exp(s - jnp.max(s, axis=-1, keepdims=True))
    prob = e / jnp.sum(e, axis=-1, keepdims=True)
    return prob, unstack_heads(nn(prob.astype(BF16), vals)).astype(BF16)


def middle_kernel(mid, tok, gains, w_qkv, bias, q_o, no_o, ne_o, kv_o, p_o, attn_o):
    unit_e, _ = unit_of(mid[...].reshape(ROWS * EC, D).astype(F32))
    ne = (unit_e * gains[0:1, :]).astype(BF16)
    ne_o[...] = ne
    kv_o[...] = nn(ne, w_qkv[:, D:]).astype(BF16)
    unit_o, _ = unit_of(tok[...].astype(F32))
    no = (unit_o * gains[0:1, :]).astype(BF16)
    no_o[...] = no
    q_o[...] = nn(no, w_qkv[:, :D]).astype(BF16)
    at = 128 - RIM * EC
    for g in range(2):
        cols = slice(g * 256, (g + 1) * 256)
        vcols = slice(D + g * 256, D + (g + 1) * 256)
        prob, o = attend(q_o[QT : 2 * QT, cols], kv_o[at : at + KT, cols], kv_o[at : at + KT, vcols], bias[1])
        p_o[g] = prob
        attn_o[:, cols] = o


def forward_kernel(
    coord, rim_a, rim_b, tok, cot, gains, w_qkv, w_out, w_up, gact, bias, pt_u, q_i, ne_i, kv_i, attn_i,
    u_keep, u_send, d_keep, d_send, gm_o, kv_o, p_o, ne_o, gain_o, attn_s, rows_s,
):
    odd = coord[0] & 1
    edge = RIM * EC
    at_a = pl.multiple_of(odd * (RIM + ROWS) * EC, EC)
    at_b = pl.multiple_of((1 - odd) * (RIM + ROWS) * EC, EC)
    end = (RIM + ROWS) * EC
    both = jnp.concatenate([rim_a[...].reshape(edge, D), rim_b[...].reshape(edge, D)], axis=0)
    unit_r, _ = unit_of(both.astype(F32))
    ne_r = (unit_r * gains[0:1, :]).astype(BF16)
    kv_r = nn(ne_r, w_qkv[:, D:]).astype(BF16)
    for ref, mid, rims in ((ne_o, ne_i, ne_r), (kv_o, kv_i, kv_r)):
        ref[edge:end, :] = mid[...]
        ref[pl.ds(at_a, edge), :] = rims[:edge]
        ref[pl.ds(at_b, edge), :] = rims[edge:]
        ref[end + edge :, :] = jnp.zeros((EXT - end - edge, ref.shape[1]), BF16)
    xt = tok[...].astype(F32)
    attn_s[QT : 2 * QT, :] = attn_i[...]
    for i, t in enumerate((0, 2)):
        rows = slice(t * 128, t * 128 + KT)
        for g in range(2):
            cols = slice(g * 256, (g + 1) * 256)
            vcols = slice(D + g * 256, D + (g + 1) * 256)
            prob, o = attend(q_i[t * QT : (t + 1) * QT, cols], kv_o[rows, cols], kv_o[rows, vcols], bias[t])
            p_o[i * 2 + g] = prob
            attn_s[t * QT : (t + 1) * QT, cols] = o
    attn = attn_s[...]
    mixed = (xt + nn(attn, w_out[...])).astype(BF16)
    um, inv_m = unit_of(mixed.astype(F32))
    nm = (um * gains[1:2, :]).astype(BF16)
    nmt = nt(pt_u[...], nm).astype(BF16)
    gn = jnp.zeros((TOK, D), F32)
    for c in range(4):
        cols = slice(c * 512, (c + 1) * 512)
        pre = nn(nm, w_up[:, cols])
        th = jnp.tanh(GELU_C * (pre + 0.044715 * (pre * pre * pre)))
        half = 0.5 * (1.0 + th)
        act = (pre * half).astype(BF16)
        slope = half + 0.5 * pre * (1.0 - th * th) * (GELU_C * (1.0 + 0.134145 * (pre * pre)))
        gp = (gact[:, cols] * slope).astype(BF16)
        gn = gn + nt(gp, w_up[:, cols])
        gu = nn(nmt, gp).astype(BF16)
        u_keep[:, c] = gu[:256].reshape(16, 16, D)
        u_send[:, c] = gu[256:].reshape(16, 16, D)
        rows_s[c & 1] = tn(act, cot[...]).reshape(64, 8, D)
        xh = (c & 1) ^ ((coord[2] >> 6) & 1)
        for y in range(4):
            for xl in range(2):
                for co, ref in ((0, d_keep), (1, d_send)):
                    at = (xl * 32 + y * 8 + co) ^ (coord[2] & 57)
                    part = jnp.concatenate([rows_s[c & 1, at + 2 * zl] for zl in range(4)], axis=0)
                    ref[y, xh * 2 + xl, c >> 1] = part.astype(BF16)
    g = gn * gains[1:2, :]
    gm = (cot[...].astype(F32) + inv_m * (g - um * jnp.mean(g * um, axis=-1, keepdims=True))).astype(BF16)
    gm_o[...] = gm
    gain_o[...] = jnp.sum(gn * um, axis=0, keepdims=True)
    go = nn(nt(pt_u[...], attn).astype(BF16), gm).astype(BF16)
    u_keep[:, 4] = go[:256].reshape(16, 16, D)
    u_send[:, 4] = go[256:].reshape(16, 16, D)


def backward_kernel(
    gm, w_out, q, kv, p_mid, p_out, ne, no, pt_u, pt_k,
    k_keep, k_send, dq_s, dkv_o,
):
    ga = nt(gm[...], w_out[...]).astype(BF16)
    for g in range(2):
        cols = slice(g * 256, (g + 1) * 256)
        vcols = slice(D + g * 256, D + (g + 1) * 256)
        left_k = left_v = None
        for t in range(TILES):
            rows = slice(t * 128, t * 128 + KT)
            prob = p_mid[g] if t == 1 else p_out[t + g]
            gas = stack_heads(ga[t * QT : (t + 1) * QT, cols])
            qs = stack_heads(q[t * QT : (t + 1) * QT, cols])
            gp = nt(gas, kv[rows, vcols])
            inner = jnp.sum(prob * gp, axis=-1, keepdims=True)
            ds = (prob * (gp - inner) * 0.125).astype(BF16)
            dq_s[t * QT : (t + 1) * QT, cols] = unstack_heads(nn(ds, kv[rows, cols])).astype(BF16)
            dk, dv = tn(ds, qs), tn(prob.astype(BF16), gas)
            top_k, top_v = dk[:128], dv[:128]
            if t:
                top_k, top_v = top_k + left_k, top_v + left_v
            left_k, left_v = dk[128:], dv[128:]
            dkv_o[t * 128 : t * 128 + 128, cols] = top_k.astype(BF16)
            dkv_o[t * 128 : t * 128 + 128, vcols] = top_v.astype(BF16)
        dkv_o[TILES * 128 :, cols] = left_k.astype(BF16)
        dkv_o[TILES * 128 :, vcols] = left_v.astype(BF16)
    dkv = dkv_o[...]
    gk = nn(nt(pt_k[...], ne[...]).astype(BF16), dkv).astype(BF16)
    gq = nn(nt(pt_u[...], no[...]).astype(BF16), dq_s[...]).astype(BF16)
    for at, out in ((0, k_keep), (256, k_send)):
        out[:16] = gq[at : at + 256].reshape(16, 16, D)
        for i in range(2):
            for j in range(16):
                out[16 + j * 2 + i] = gk[at + j * 16 : at + j * 16 + 16, i * D : (i + 1) * D]


def inputs_kernel(coord, dq, dkv, w_qkv, mid, rim_a, rim_b, tok, gain_mid, gne_o, gnq_o, gain_o, row_a, row_b):
    gne = nt(dkv[...], w_qkv[:, D:])
    gnq = nt(dq[...], w_qkv[:, :D])
    gne_o[...] = gne[: (ROWS + 2 * RIM) * EC]
    gnq_o[...] = gnq
    gain_in = jnp.sum(gnq * unit_of(tok[...].astype(F32))[0], axis=0, keepdims=True)
    odd = coord[0] & 1
    for ref, at in ((rim_a, odd * (RIM + ROWS)), (mid, RIM), (rim_b, (1 - odd) * (RIM + ROWS))):
        size = ref.shape[0] * EC
        unit, _ = unit_of(ref[...].reshape(size, D).astype(F32))
        part = gne_o[pl.ds(pl.multiple_of(at * EC, EC), size), :]
        gain_in = gain_in + jnp.sum(part * unit, axis=0, keepdims=True)
    spread = jnp.concatenate([gain_in, gain_mid[...], jnp.zeros((14, D), F32)], axis=0).astype(BF16)
    gain_o[...] = spread
    for ref, at in ((row_a, odd * (RIM + ROWS)), (row_b, (1 - odd) * (RIM + ROWS))):
        rim = gne_o[pl.ds(pl.multiple_of(at * EC, EC), RIM * EC), :]
        ref[...] = rim.astype(BF16).reshape(RIM, EC, D)


def add2(a, b):
    return (a.astype(F32) + b.astype(F32)).astype(BF16)


def add4(parts):
    a, b, c, d = [v.astype(F32) for v in parts]
    return ((a + b) + (c + d)).astype(BF16)


def halves():
    return ((0, (1, 2), (0, 3)), (1, (3, 2), (0, 1)))


def join_down_kv_kernel(dk, dg, kk, kg, *outs):
    for h, away, stay in halves():
        for out, chunks in ((outs[h], away), (outs[2 + h], stay)):
            for i, d in enumerate(chunks):
                lo, at = d * 16 + h * 8, i * 12
                out[at : at + 8] = add2(dk[lo : lo + 8], dg[lo : lo + 8])
                lo = 16 + d * 8 + h * 4
                out[at + 8 : at + 12] = add2(kk[lo : lo + 4], kg[lo : lo + 4])


def join_up_q_kernel(uk, ug, kk, kg, gk, gg, ride, *outs):
    for h, away, stay in halves():
        for out, chunks in ((outs[h], away), (outs[2 + h], stay)):
            for i, d in enumerate(chunks):
                lo, at = d * 20 + h * 10, i * 12
                out[at : at + 10] = add2(uk[lo : lo + 10], ug[lo : lo + 10])
                lo = d * 4 + h * 2
                out[at + 10 : at + 12] = add2(kk[lo : lo + 2], kg[lo : lo + 2])
    gain = add2(gk[...], gg[...])
    outs[0][24] = gain
    outs[2][24] = gain
    outs[0][25:] = ride[...]


def second_kernel(p_got, q_got, p_keep, q_keep, p_send, q_send, p_own, q_own):
    p_own[:12] = add2(p_keep[:12], p_got[:12])
    p_send[:12] = add2(p_keep[12:24], p_got[12:24])
    q_own[...] = add2(q_keep[:12], q_got[:12])
    q_send[...] = add2(q_keep[12:], q_got[12:])
    if p_keep.shape[0] == 25:
        gain = add2(p_keep[24], p_got[24])
        p_own[12] = gain
        p_send[12] = gain


def sum_up_q_kernel(p_got, q_got, p_own, q_own, *outs):
    gain = add2(p_got[12], p_own[12])
    for h, got, own in ((0, p_got, p_own), (1, q_got, q_own)):
        for i in range(2):
            out = outs[2 * h + i]
            out[:5] = add2(got[i * 5 : i * 5 + 5], own[i * 5 : i * 5 + 5])
            out[5] = add2(got[10 + i], own[10 + i])
            out[6] = gain


def sum_down_kv_kernel(p_got, q_got, p_own, q_own, *outs):
    for h, got, own in ((0, p_got, p_own), (1, q_got, q_own)):
        for i in range(2):
            out = outs[2 * h + i]
            out[:4] = add2(got[i * 4 : i * 4 + 4], own[i * 4 : i * 4 + 4])
            out[4:] = add2(got[8 + i * 2 : 10 + i * 2], own[8 + i * 2 : 10 + i * 2])


def reduce_xy_kernel(*refs):
    out, flat_s = refs[8:]
    sums = [add4([r[...] for r in refs[:4]]).reshape(-1, D), add4([r[...] for r in refs[4:8]]).reshape(-1, D)]
    acc = jnp.concatenate(sums, axis=0)
    rows = acc.shape[0]
    per = ZROWS // 4
    i = lax.broadcasted_iota(jnp.int32, (8 * per, rows), 0)
    lane = lax.broadcasted_iota(jnp.int32, (8 * per, rows), 1)
    z = i // per
    r = i % per
    up = (r % 4) * 16 + z * 2 + r // 4
    down = 112 + z * 8 + (r - 8)
    o = 64 + z * 2 + (r - 16)
    part = (r - 18) % 3
    qkv = jnp.where(part == 0, 80, 160 + part * 16) + z * 2 + (r - 18) // 3
    gain = 96 + (r - 24)
    src = jnp.where(r < 8, up, jnp.where(r < 16, down, jnp.where(r < 18, o, jnp.where(r < 24, qkv, gain))))
    picked = nn(jnp.where((lane == src) & (r < 26), 1.0, 0.0).astype(BF16), acc)
    for j in range(4):
        flat_s[pl.ds(j, 8 * per, stride=4), :] = picked[:, j * 128 : (j + 1) * 128]
    out[...] = flat_s[...].astype(BF16).reshape(8, ZROWS, 128)


def reduce_z_kernel(got, up, down, o, qkv, gain):
    acc = got[0].astype(F32)
    for j in range(1, 8):
        acc = acc + got[j].astype(F32)
    acc = acc * (1.0 / math.sqrt(GRID_ROWS * GRID_COLS))
    at = 0
    for ref in (up, down, o, qkv):
        ref[...] = acc[at : at + ref.shape[0]]
        at += ref.shape[0]
    for r in range(2):
        for j in range(4):
            gain[r : r + 1, j * 128 : (j + 1) * 128] = acc[at + 4 * r + j : at + 4 * r + j + 1]


def call(body, outs, scratch, n_smem, n_in, flops, nbytes, mib):
    smem = pl.BlockSpec(memory_space=pltpu.SMEM)
    vmem = pl.BlockSpec(memory_space=pltpu.VMEM)
    return pl.pallas_call(
        body,
        out_shape=[jax.ShapeDtypeStruct(s, d) for s, d in outs],
        in_specs=[smem] * n_smem + [vmem] * n_in,
        out_specs=[vmem] * len(outs),
        scratch_shapes=scratch,
        compiler_params=pltpu.CompilerParams(vmem_limit_bytes=mib * 1024 * 1024),
        cost_estimate=pl.CostEstimate(flops=flops, bytes_accessed=nbytes, transcendentals=0),
    )


def pairs(stride, count, first):
    out = []
    for k in range(256):
        at = (k // stride) % count
        other = at + 1 if (at - first) % 2 == 0 else at - 1
        if 0 <= other < count:
            out.append((k, k + (other - at) * stride))
    return out


ROW_A, ROW_B = pairs(N_COL, 8, 1), pairs(N_COL, 8, 0)
COL_A, COL_B = pairs(1, N_COL, 1), pairs(1, N_COL, 0)
CORE_SWAP = [(k, k ^ 1) for k in range(256)]
X_BIT = 32
Y_BIT = 8
Z_GROUPS = [[zh * 128 + x * 32 + y * 8 + zl * 2 + c for zh in range(2) for zl in range(4)] for x in range(4) for y in range(4) for c in range(2)]


def send(x, perm):
    return lax.ppermute(x, AXES, perm)


def by(bits):
    return [(k, k ^ bits) for k in range(256)]


def to_three(chunks, bit):
    return [chunks[0]] + [send(chunks[d], by(bit * d)) for d in (1, 3, 2)]


def exchange(x, groups):
    return lax.all_to_all(x, AXES, 0, 0, axis_index_groups=groups, tiled=True)


def per_device(tokens, cotangent, gains, w_qkv, w_out, w_up, w_down, tile_mask):
    row = lax.axis_index("row")
    col = lax.axis_index("col")
    coord = jnp.stack([row, col, row * N_COL + col]).astype(jnp.int32)
    tok = tokens.reshape(TOK, D)
    cot = cotangent.reshape(TOK, D)

    row_odd = (row & 1) == 1
    col_odd = (col & 1) == 1
    first, last = tokens[:, :RIM], tokens[:, COLS - RIM :]
    side_b = send(jnp.where(col_odd, first, last), COL_B)
    side_a = send(jnp.where(col_odd, last, first), COL_A)
    (bias,) = call(
        prep_mask_kernel, [((TILES, QT, KT), F32)], [], 2, 0, 2 * TOK * D * FF, 4_000_000, 8,
    )(coord, tile_mask)
    side_a, side_b, cot, bias, coord = lax.optimization_barrier((side_a, side_b, cot, bias, coord))
    mid = jnp.concatenate([tokens, side_a, side_b, jnp.zeros((ROWS, EC - COLS - 2 * RIM, D), BF16)], axis=1)
    rim_b = send(jnp.where(row_odd, mid[:RIM], mid[ROWS - RIM :]), ROW_B)
    rim_a = send(jnp.where(row_odd, mid[ROWS - RIM :], mid[:RIM]), ROW_A)
    pt_u, pt_k = call(
        prep_order_kernel, [((D, D), BF16)] * 2, [], 1, 0, 2 * TOK * D * FF, 4_000_000, 8,
    )(coord)
    (gact,) = call(
        prep_front_kernel, [((TOK, FF), F32)], [], 0, 2, 2 * TOK * D * FF, 4_000_000, 8,
    )(cot, w_down)

    q, no, ne_mid, kv_mid, p_mid, attn_mid = call(
        middle_kernel,
        [
            ((TOK, D), BF16), ((TOK, D), BF16), ((ROWS * EC, D), BF16), ((ROWS * EC, 2 * D), BF16),
            ((2, 256, KT), F32), ((QT, D), BF16),
        ],
        [], 0, 5, 600_000_000, 5_000_000, 10,
    )(mid, tok, gains, w_qkv, bias)

    half_u, half_d = ((16, 5, 16, D), BF16), ((4, 4, 2, 32, D), BF16)
    half_q, half_k = ((16, 16, D), BF16), ((48, 16, D), BF16)
    u_keep, u_send, d_keep, d_send, gm, kv, p_out, ne, gain_mid = call(
        forward_kernel,
        [
            half_u, half_u, half_d, half_d, ((TOK, D), BF16), ((EXT, 2 * D), BF16), ((4, 256, KT), F32),
            ((EXT, D), BF16), ((1, D), F32),
        ],
        [pltpu.VMEM((TOK, D), BF16), pltpu.VMEM((2, 64, 8, D), F32)], 1, 15, 4_000_000_000, 20_000_000, 16,
    )(coord, rim_a, rim_b, tok, cot, gains, w_qkv, w_out, w_up, gact, bias, pt_u, q, ne_mid, kv_mid, attn_mid)

    u_got = send(u_send, CORE_SWAP)
    d_got = send(d_send, CORE_SWAP)
    k_keep, k_send, dq, dkv = call(
        backward_kernel,
        [half_k, half_k, ((TOK, D), BF16), ((EXT, 2 * D), BF16)],
        [], 0, 10, 2_500_000_000, 10_000_000, 12,
    )(gm, w_out, q, kv, p_mid, p_out, ne, no, pt_u, pt_k)
    u_got, d_got, k_send = lax.optimization_barrier((u_got, d_got, k_send))
    k_got = send(k_send, CORE_SWAP)
    gne, gnq, gain, row_a, row_b = call(
        inputs_kernel,
        [
            (((ROWS + 2 * RIM) * EC, D), F32), ((TOK, D), F32), ((16, D), BF16),
            ((RIM, EC, D), BF16), ((RIM, EC, D), BF16),
        ],
        [], 1, 8, 600_000_000, 4_000_000, 6,
    )(coord, dq, dkv, w_qkv, mid, rim_a, rim_b, tok, gain_mid)
    gain_got = send(gain, CORE_SWAP)

    def place(x, axis, odd, end_if_odd, size):
        gap = size - RIM
        after = [(0, 0)] * 3
        before = [(0, 0)] * 3
        after[axis], before[axis] = (0, gap), (gap, 0)
        x = x.astype(F32)
        x_odd, x_even = (before, after) if end_if_odd else (after, before)
        return jnp.where(odd, jnp.pad(x, x_odd), jnp.pad(x, x_even))

    def join(body, ins, outs):
        return list(call(body, [(o, BF16) for o in outs], [], 0, len(ins), 1_000_000, 4_000_000, 6)(*ins))

    def first(sent, bit):
        return send(sent[0], by(bit)), send(sent[1], by(3 * bit))

    def second(sent, bit):
        return send(sent[0], by(3 * bit)), send(sent[1], by(bit))

    k_got, gnq, gain_got = lax.optimization_barrier((k_got, gnq, gain_got))
    u_p, u_q, *u_stay = join(
        join_up_q_kernel, [u_keep.reshape(80, 16, D), u_got.reshape(80, 16, D), k_keep, k_got, gain, gain_got, row_b],
        [(28, 16, D), (24, 16, D), (25, 16, D), (24, 16, D)],
    )
    u_first = first((u_p, u_q), X_BIT)
    b_p, b_q, *b_stay = join(
        join_down_kv_kernel, [d_keep.reshape(64, 16, D), d_got.reshape(64, 16, D), k_keep, k_got], [(24, 16, D)] * 4,
    )
    b_first = first((b_p, b_q), Y_BIT)
    row_a = send(row_a, ROW_A)
    b_first, row_a = lax.optimization_barrier((b_first, row_a))
    u_p, u_q, *u_own = join(second_kernel, [*u_first, *u_stay], [(13, 16, D), (12, 16, D)] * 2)
    u_second = second((u_p, u_q), X_BIT)
    b_p, b_q, *b_own = join(second_kernel, [*b_first, *b_stay], [(12, 16, D)] * 4)
    b_second = second((b_p, b_q), Y_BIT)
    gne = gne.reshape(ROWS + 2 * RIM, EC, D)[RIM : RIM + ROWS]
    gne = gne + place(row_a, 0, row_odd, True, ROWS) + place(u_first[0][25:], 0, row_odd, False, ROWS)
    u = join(sum_up_q_kernel, [*u_second, *u_own], [(7, 16, D)] * 4)
    u = to_three(u, Y_BIT)
    b = join(sum_down_kv_kernel, [*b_second, *b_own], [(6, 16, D)] * 4)
    b = to_three(b, X_BIT)
    (spread,) = call(
        reduce_xy_kernel, [((8, ZROWS, 128), BF16)], [pltpu.VMEM((8 * ZROWS, 128), F32)], 0, 8, 60_000_000, 4_000_000, 5,
    )(*u, *b)
    got_z = exchange(spread, Z_GROUPS)
    back_b = send(gne[:, COLS + RIM : COLS + 2 * RIM].astype(BF16), COL_B)
    back_a = send(gne[:, COLS : COLS + RIM].astype(BF16), COL_A)
    got_z, back_a, back_b = lax.optimization_barrier((got_z, back_a, back_b))
    g_up, g_down, g_out, g_qkv, g_gains = call(
        reduce_z_kernel,
        [((32, 128), F32), ((32, 128), F32), ((8, 128), F32), ((24, 128), F32), ((2, D), F32)],
        [], 0, 1, 100_000_000_000, 400_000, 4,
    )(got_z)

    gn = gne[:, :COLS] + place(back_a, 1, col_odd, True, COLS) + place(back_b, 1, col_odd, False, COLS)
    gn = gn + gnq.reshape(ROWS, COLS, D)
    unit, inv = unit_of(tokens.astype(F32))
    g1 = gn * gains[0]
    front = inv * (g1 - unit * jnp.mean(g1 * unit, axis=-1, keepdims=True))
    grad_tokens = (gm.reshape(ROWS, COLS, D).astype(F32) + front).astype(BF16)
    return (grad_tokens, g_qkv.reshape(-1), g_out.reshape(-1), g_up.reshape(-1), g_down.reshape(-1), g_gains)


def solution(mesh):
    block = P("row", "col", None)
    flat = P(("row", "col"))
    return jax.shard_map(
        per_device,
        mesh=mesh,
        in_specs=(block, block, P(), P(), P(), P(), P(), block),
        out_specs=(block, flat, flat, flat, flat, P()),
        check_vma=False,
    )
```

```python
import math

import jax
import jax.numpy as jnp
from jax import lax
from jax.experimental import pallas as pl
from jax.experimental.pallas import tpu as pltpu
from jax.sharding import PartitionSpec as P

D = 512
FF = 2048
HEADS = 8
WINDOW = 7
TILE = 8
RIM = WINDOW // 2
EPS = 1e-06
AXES = ("row", "col")
N_COL = 32
GRID_ROWS = 192
GRID_COLS = 256
ROWS = 24
COLS = 8
TOK = ROWS * COLS
TILES = ROWS // TILE
ER = 32
EC = 16
EXT = ER * EC
QT = TILE * TILE
ZROWS = 112
KT = 256
F32 = jnp.float32
BF16 = jnp.bfloat16
GELU_C = math.sqrt(2.0 / math.pi)


def nn(a, b):
    return lax.dot_general(a, b, (((1,), (0,)), ((), ())), preferred_element_type=F32)


def nt(a, b):
    return lax.dot_general(a, b, (((1,), (1,)), ((), ())), preferred_element_type=F32)


def tn(a, b):
    return lax.dot_general(a, b, (((0,), (0,)), ((), ())), preferred_element_type=F32)


def unit_of(x):
    inv = lax.rsqrt(jnp.mean(x * x, axis=-1, keepdims=True) + EPS)
    return x * inv, inv


def head_mask(rows, h):
    lane = lax.broadcasted_iota(jnp.int32, (rows, 256), 1)
    return (lane // 64) == h


def stack_heads(x):
    zero = jnp.zeros_like(x)
    return jnp.concatenate([jnp.where(head_mask(x.shape[0], h), x, zero) for h in range(4)], axis=0)


def unstack_heads(x):
    rows = x.shape[0] // 4
    out = jnp.where(head_mask(rows, 0), x[:rows], 0.0)
    for h in range(1, 4):
        out = out + jnp.where(head_mask(rows, h), x[h * rows : (h + 1) * rows], 0.0)
    return out


def prep_front_kernel(cot, w_down, gact):
    for c in range(4):
        gact[:, c * 512 : (c + 1) * 512] = nt(cot[...], w_down[c * 512 : (c + 1) * 512, :])


def prep_mask_kernel(coord, mask, bias):
    q = lax.broadcasted_iota(jnp.int32, (QT, KT), 0)
    k = lax.broadcasted_iota(jnp.int32, (QT, KT), 1)
    ki = k // EC
    kc = k % EC
    odd = coord[1] & 1
    near = kc - COLS + odd * (COLS + RIM)
    far = kc - COLS - RIM + (1 - odd) * (COLS + RIM)
    kj = jnp.where(kc < COLS, kc + RIM, jnp.where(kc < COLS + RIM, near, jnp.where(kc < COLS + 2 * RIM, far, -99)))
    da = ki - q // TILE
    db = kj - q % TILE
    slot = jnp.where((da >= 0) & (da < WINDOW) & (db >= 0) & (db < WINDOW), da * WINDOW + db, -1)
    allowed = [jnp.zeros((QT, KT), jnp.int32) for _ in range(TILES)]
    for s in range(WINDOW * WINDOW):
        here = slot == s
        for t in range(TILES):
            allowed[t] = jnp.where(here, mask[t, 0, s], allowed[t])
    gc = coord[1] * COLS + kj - RIM
    for t in range(TILES):
        gr = coord[0] * ROWS + t * TILE + ki - RIM
        ok = (allowed[t] == 1) & (gr >= 0) & (gr < GRID_ROWS) & (gc >= 0) & (gc < GRID_COLS)
        bias[t] = jnp.where(ok, 0.0, -1e30)


def prep_order_kernel(coord, pt_u, pt_k):
    me = coord[2]
    lane = lax.broadcasted_iota(jnp.int32, (512, 512), 1)
    p = lax.broadcasted_iota(jnp.int32, (512, 512), 0)
    core_z = ((p >> 3) & 1) * 128 + ((p >> 1) & 3) * 2 + (p >> 8)
    hi, lo = (p >> 6) & 3, (p >> 4) & 3
    here = me & 121
    pt_u[...] = jnp.where(lane == ((core_z + hi * 32 + lo * 8) ^ here) * 2 + (p & 1), 1.0, 0.0).astype(BF16)
    pt_k[...] = jnp.where(lane == ((core_z + hi * 8 + lo * 32) ^ here) * 2 + (p & 1), 1.0, 0.0).astype(BF16)


def attend(qt, keys, vals, bias_t):
    s = nt(stack_heads(qt), keys) * 0.125 + jnp.concatenate([bias_t] * 4, axis=0)
    e = jnp.exp(s - jnp.max(s, axis=-1, keepdims=True))
    prob = e / jnp.sum(e, axis=-1, keepdims=True)
    return prob, unstack_heads(nn(prob.astype(BF16), vals)).astype(BF16)


def middle_kernel(mid, tok, gains, w_qkv, bias, q_o, no_o, ne_o, kv_o, p_o, attn_o):
    unit_e, _ = unit_of(mid[...].reshape(ROWS * EC, D).astype(F32))
    ne = (unit_e * gains[0:1, :]).astype(BF16)
    ne_o[...] = ne
    kv_o[...] = nn(ne, w_qkv[:, D:]).astype(BF16)
    unit_o, _ = unit_of(tok[...].astype(F32))
    no = (unit_o * gains[0:1, :]).astype(BF16)
    no_o[...] = no
    q_o[...] = nn(no, w_qkv[:, :D]).astype(BF16)
    at = 128 - RIM * EC
    for g in range(2):
        cols = slice(g * 256, (g + 1) * 256)
        vcols = slice(D + g * 256, D + (g + 1) * 256)
        prob, o = attend(q_o[QT : 2 * QT, cols], kv_o[at : at + KT, cols], kv_o[at : at + KT, vcols], bias[1])
        p_o[g] = prob
        attn_o[:, cols] = o


def forward_kernel(
    coord, rim_a, rim_b, tok, cot, gains, w_qkv, w_out, w_up, gact, bias, pt_u, q_i, ne_i, kv_i, attn_i,
    u_keep, u_send, d_keep, d_send, gm_o, kv_o, p_o, ne_o, gain_o, attn_s, rows_s,
):
    odd = coord[0] & 1
    edge = RIM * EC
    at_a = pl.multiple_of(odd * (RIM + ROWS) * EC, EC)
    at_b = pl.multiple_of((1 - odd) * (RIM + ROWS) * EC, EC)
    end = (RIM + ROWS) * EC
    both = jnp.concatenate([rim_a[...].reshape(edge, D), rim_b[...].reshape(edge, D)], axis=0)
    unit_r, _ = unit_of(both.astype(F32))
    ne_r = (unit_r * gains[0:1, :]).astype(BF16)
    kv_r = nn(ne_r, w_qkv[:, D:]).astype(BF16)
    for ref, mid, rims in ((ne_o, ne_i, ne_r), (kv_o, kv_i, kv_r)):
        ref[edge:end, :] = mid[...]
        ref[pl.ds(at_a, edge), :] = rims[:edge]
        ref[pl.ds(at_b, edge), :] = rims[edge:]
        ref[end + edge :, :] = jnp.zeros((EXT - end - edge, ref.shape[1]), BF16)
    xt = tok[...].astype(F32)
    attn_s[QT : 2 * QT, :] = attn_i[...]
    for i, t in enumerate((0, 2)):
        rows = slice(t * 128, t * 128 + KT)
        for g in range(2):
            cols = slice(g * 256, (g + 1) * 256)
            vcols = slice(D + g * 256, D + (g + 1) * 256)
            prob, o = attend(q_i[t * QT : (t + 1) * QT, cols], kv_o[rows, cols], kv_o[rows, vcols], bias[t])
            p_o[i * 2 + g] = prob
            attn_s[t * QT : (t + 1) * QT, cols] = o
    attn = attn_s[...]
    mixed = (xt + nn(attn, w_out[...])).astype(BF16)
    um, inv_m = unit_of(mixed.astype(F32))
    nm = (um * gains[1:2, :]).astype(BF16)
    nmt = nt(pt_u[...], nm).astype(BF16)
    gn = jnp.zeros((TOK, D), F32)
    for c in range(4):
        cols = slice(c * 512, (c + 1) * 512)
        pre = nn(nm, w_up[:, cols])
        th = jnp.tanh(GELU_C * (pre + 0.044715 * (pre * pre * pre)))
        half = 0.5 * (1.0 + th)
        act = (pre * half).astype(BF16)
        slope = half + 0.5 * pre * (1.0 - th * th) * (GELU_C * (1.0 + 0.134145 * (pre * pre)))
        gp = (gact[:, cols] * slope).astype(BF16)
        gn = gn + nt(gp, w_up[:, cols])
        gu = nn(nmt, gp).astype(BF16)
        u_keep[:, c] = gu[:256].reshape(16, 16, D)
        u_send[:, c] = gu[256:].reshape(16, 16, D)
        rows_s[c & 1] = tn(act, cot[...]).reshape(64, 8, D)
        xh = (c & 1) ^ ((coord[2] >> 6) & 1)
        for y in range(4):
            for xl in range(2):
                for co, ref in ((0, d_keep), (1, d_send)):
                    at = (xl * 32 + y * 8 + co) ^ (coord[2] & 57)
                    part = jnp.concatenate([rows_s[c & 1, at + 2 * zl] for zl in range(4)], axis=0)
                    ref[y, xh * 2 + xl, c >> 1] = part.astype(BF16)
    g = gn * gains[1:2, :]
    gm = (cot[...].astype(F32) + inv_m * (g - um * jnp.mean(g * um, axis=-1, keepdims=True))).astype(BF16)
    gm_o[...] = gm
    gain_o[...] = jnp.sum(gn * um, axis=0, keepdims=True)
    go = nn(nt(pt_u[...], attn).astype(BF16), gm).astype(BF16)
    u_keep[:, 4] = go[:256].reshape(16, 16, D)
    u_send[:, 4] = go[256:].reshape(16, 16, D)


def backward_kernel(
    gm, w_out, q, kv, p_mid, p_out, ne, no, pt_u, pt_k,
    k_keep, k_send, dq_s, dkv_o,
):
    ga = nt(gm[...], w_out[...]).astype(BF16)
    for g in range(2):
        cols = slice(g * 256, (g + 1) * 256)
        vcols = slice(D + g * 256, D + (g + 1) * 256)
        left_k = left_v = None
        for t in range(TILES):
            rows = slice(t * 128, t * 128 + KT)
            prob = p_mid[g] if t == 1 else p_out[t + g]
            gas = stack_heads(ga[t * QT : (t + 1) * QT, cols])
            qs = stack_heads(q[t * QT : (t + 1) * QT, cols])
            gp = nt(gas, kv[rows, vcols])
            inner = jnp.sum(prob * gp, axis=-1, keepdims=True)
            ds = (prob * (gp - inner) * 0.125).astype(BF16)
            dq_s[t * QT : (t + 1) * QT, cols] = unstack_heads(nn(ds, kv[rows, cols])).astype(BF16)
            dk, dv = tn(ds, qs), tn(prob.astype(BF16), gas)
            top_k, top_v = dk[:128], dv[:128]
            if t:
                top_k, top_v = top_k + left_k, top_v + left_v
            left_k, left_v = dk[128:], dv[128:]
            dkv_o[t * 128 : t * 128 + 128, cols] = top_k.astype(BF16)
            dkv_o[t * 128 : t * 128 + 128, vcols] = top_v.astype(BF16)
        dkv_o[TILES * 128 :, cols] = left_k.astype(BF16)
        dkv_o[TILES * 128 :, vcols] = left_v.astype(BF16)
    dkv = dkv_o[...]
    gk = nn(nt(pt_k[...], ne[...]).astype(BF16), dkv).astype(BF16)
    gq = nn(nt(pt_u[...], no[...]).astype(BF16), dq_s[...]).astype(BF16)
    for at, out in ((0, k_keep), (256, k_send)):
        out[:16] = gq[at : at + 256].reshape(16, 16, D)
        for i in range(2):
            for j in range(16):
                out[16 + j * 2 + i] = gk[at + j * 16 : at + j * 16 + 16, i * D : (i + 1) * D]


def inputs_kernel(coord, dq, dkv, w_qkv, mid, rim_a, rim_b, tok, gain_mid, gne_o, gnq_o, gain_o, row_a, row_b, gne_s):
    gne = nt(dkv[...], w_qkv[:, D:])
    gnq = nt(dq[...], w_qkv[:, :D])
    gne_s[...] = gne[: (ROWS + 2 * RIM) * EC]
    gne_o[...] = gne[RIM * EC : (RIM + ROWS) * EC]
    gnq_o[...] = gnq
    gain_in = jnp.sum(gnq * unit_of(tok[...].astype(F32))[0], axis=0, keepdims=True)
    odd = coord[0] & 1
    for ref, at in ((rim_a, odd * (RIM + ROWS)), (mid, RIM), (rim_b, (1 - odd) * (RIM + ROWS))):
        size = ref.shape[0] * EC
        unit, _ = unit_of(ref[...].reshape(size, D).astype(F32))
        part = gne_s[pl.ds(pl.multiple_of(at * EC, EC), size), :]
        gain_in = gain_in + jnp.sum(part * unit, axis=0, keepdims=True)
    spread = jnp.concatenate([gain_in, gain_mid[...], jnp.zeros((14, D), F32)], axis=0).astype(BF16)
    gain_o[...] = spread
    for ref, at in ((row_a, odd * (RIM + ROWS)), (row_b, (1 - odd) * (RIM + ROWS))):
        rim = gne_s[pl.ds(pl.multiple_of(at * EC, EC), RIM * EC), :]
        ref[...] = rim.astype(BF16).reshape(RIM, EC, D)


def add2(a, b):
    return (a.astype(F32) + b.astype(F32)).astype(BF16)


def add4(parts):
    a, b, c, d = [v.astype(F32) for v in parts]
    return ((a + b) + (c + d)).astype(BF16)


def halves():
    return ((0, (1, 2), (0, 3)), (1, (3, 2), (0, 1)))


def join_down_kv_kernel(dk, dg, kk, kg, *outs):
    for h, away, stay in halves():
        for out, chunks in ((outs[h], away), (outs[2 + h], stay)):
            for i, d in enumerate(chunks):
                lo, at = d * 16 + h * 8, i * 12
                out[at : at + 8] = add2(dk[lo : lo + 8], dg[lo : lo + 8])
                lo = 16 + d * 8 + h * 4
                out[at + 8 : at + 12] = add2(kk[lo : lo + 4], kg[lo : lo + 4])


def join_up_q_kernel(uk, ug, kk, kg, gk, gg, ride, *outs):
    for h, away, stay in halves():
        for out, chunks in ((outs[h], away), (outs[2 + h], stay)):
            for i, d in enumerate(chunks):
                lo, at = d * 20 + h * 10, i * 12
                out[at : at + 10] = add2(uk[lo : lo + 10], ug[lo : lo + 10])
                lo = d * 4 + h * 2
                out[at + 10 : at + 12] = add2(kk[lo : lo + 2], kg[lo : lo + 2])
    gain = add2(gk[...], gg[...])
    outs[0][24] = gain
    outs[2][24] = gain
    outs[0][25:] = ride[...]


def second_kernel(p_got, q_got, p_keep, q_keep, p_send, q_send, p_own, q_own):
    p_own[:12] = add2(p_keep[:12], p_got[:12])
    p_send[:12] = add2(p_keep[12:24], p_got[12:24])
    q_own[...] = add2(q_keep[:12], q_got[:12])
    q_send[...] = add2(q_keep[12:], q_got[12:])
    if p_keep.shape[0] == 25:
        gain = add2(p_keep[24], p_got[24])
        p_own[12] = gain
        p_send[12] = gain


def sum_up_q_kernel(p_got, q_got, p_own, q_own, *outs):
    gain = add2(p_got[12], p_own[12])
    for h, got, own in ((0, p_got, p_own), (1, q_got, q_own)):
        for i in range(2):
            out = outs[2 * h + i]
            out[:5] = add2(got[i * 5 : i * 5 + 5], own[i * 5 : i * 5 + 5])
            out[5] = add2(got[10 + i], own[10 + i])
            out[6] = gain


def sum_down_kv_kernel(p_got, q_got, p_own, q_own, *outs):
    for h, got, own in ((0, p_got, p_own), (1, q_got, q_own)):
        for i in range(2):
            out = outs[2 * h + i]
            out[:4] = add2(got[i * 4 : i * 4 + 4], own[i * 4 : i * 4 + 4])
            out[4:] = add2(got[8 + i * 2 : 10 + i * 2], own[8 + i * 2 : 10 + i * 2])


def reduce_xy_kernel(*refs):
    out, flat_s = refs[8:]
    sums = [add4([r[...] for r in refs[:4]]).reshape(-1, D), add4([r[...] for r in refs[4:8]]).reshape(-1, D)]
    acc = jnp.concatenate(sums, axis=0)
    rows = acc.shape[0]
    per = ZROWS // 4
    i = lax.broadcasted_iota(jnp.int32, (8 * per, rows), 0)
    lane = lax.broadcasted_iota(jnp.int32, (8 * per, rows), 1)
    z = i // per
    r = i % per
    up = (r % 4) * 16 + z * 2 + r // 4
    down = 112 + z * 8 + (r - 8)
    o = 64 + z * 2 + (r - 16)
    part = (r - 18) % 3
    qkv = jnp.where(part == 0, 80, 160 + part * 16) + z * 2 + (r - 18) // 3
    gain = 96 + (r - 24)
    src = jnp.where(r < 8, up, jnp.where(r < 16, down, jnp.where(r < 18, o, jnp.where(r < 24, qkv, gain))))
    picked = nn(jnp.where((lane == src) & (r < 26), 1.0, 0.0).astype(BF16), acc)
    for j in range(4):
        flat_s[pl.ds(j, 8 * per, stride=4), :] = picked[:, j * 128 : (j + 1) * 128]
    out[...] = flat_s[...].astype(BF16).reshape(8, ZROWS, 128)


def reduce_z_kernel(got, up, down, o, qkv, gain):
    acc = got[0].astype(F32)
    for j in range(1, 8):
        acc = acc + got[j].astype(F32)
    acc = acc * (1.0 / math.sqrt(GRID_ROWS * GRID_COLS))
    at = 0
    for ref in (up, down, o, qkv):
        ref[...] = acc[at : at + ref.shape[0]]
        at += ref.shape[0]
    for r in range(2):
        for j in range(4):
            gain[r : r + 1, j * 128 : (j + 1) * 128] = acc[at + 4 * r + j : at + 4 * r + j + 1]


def call(body, outs, scratch, n_smem, n_in, flops, nbytes, mib):
    smem = pl.BlockSpec(memory_space=pltpu.SMEM)
    vmem = pl.BlockSpec(memory_space=pltpu.VMEM)
    return pl.pallas_call(
        body,
        out_shape=[jax.ShapeDtypeStruct(s, d) for s, d in outs],
        in_specs=[smem] * n_smem + [vmem] * n_in,
        out_specs=[vmem] * len(outs),
        scratch_shapes=scratch,
        compiler_params=pltpu.CompilerParams(vmem_limit_bytes=mib * 1024 * 1024),
        cost_estimate=pl.CostEstimate(flops=flops, bytes_accessed=nbytes, transcendentals=0),
    )


def pairs(stride, count, first):
    out = []
    for k in range(256):
        at = (k // stride) % count
        other = at + 1 if (at - first) % 2 == 0 else at - 1
        if 0 <= other < count:
            out.append((k, k + (other - at) * stride))
    return out


ROW_A, ROW_B = pairs(N_COL, 8, 1), pairs(N_COL, 8, 0)
COL_A, COL_B = pairs(1, N_COL, 1), pairs(1, N_COL, 0)
CORE_SWAP = [(k, k ^ 1) for k in range(256)]
X_BIT = 32
Y_BIT = 8
Z_GROUPS = [[zh * 128 + x * 32 + y * 8 + zl * 2 + c for zh in range(2) for zl in range(4)] for x in range(4) for y in range(4) for c in range(2)]


def send(x, perm):
    return lax.ppermute(x, AXES, perm)


def by(bits):
    return [(k, k ^ bits) for k in range(256)]


def to_three(chunks, bit):
    return [chunks[0]] + [send(chunks[d], by(bit * d)) for d in (1, 3, 2)]


def exchange(x, groups):
    return lax.all_to_all(x, AXES, 0, 0, axis_index_groups=groups, tiled=True)


def per_device(tokens, cotangent, gains, w_qkv, w_out, w_up, w_down, tile_mask):
    row = lax.axis_index("row")
    col = lax.axis_index("col")
    coord = jnp.stack([row, col, row * N_COL + col]).astype(jnp.int32)
    tok = tokens.reshape(TOK, D)
    cot = cotangent.reshape(TOK, D)

    row_odd = (row & 1) == 1
    col_odd = (col & 1) == 1
    first, last = tokens[:, :RIM], tokens[:, COLS - RIM :]
    side_b = send(jnp.where(col_odd, first, last), COL_B)
    side_a = send(jnp.where(col_odd, last, first), COL_A)
    (bias,) = call(
        prep_mask_kernel, [((TILES, QT, KT), F32)], [], 2, 0, 2 * TOK * D * FF, 4_000_000, 8,
    )(coord, tile_mask)
    side_a, side_b, cot, bias, coord = lax.optimization_barrier((side_a, side_b, cot, bias, coord))
    mid = jnp.concatenate([tokens, side_a, side_b, jnp.zeros((ROWS, EC - COLS - 2 * RIM, D), BF16)], axis=1)
    rim_b = send(jnp.where(row_odd, mid[:RIM], mid[ROWS - RIM :]), ROW_B)
    rim_a = send(jnp.where(row_odd, mid[ROWS - RIM :], mid[:RIM]), ROW_A)
    pt_u, pt_k = call(
        prep_order_kernel, [((D, D), BF16)] * 2, [], 1, 0, 2 * TOK * D * FF, 4_000_000, 8,
    )(coord)
    (gact,) = call(
        prep_front_kernel, [((TOK, FF), F32)], [], 0, 2, 2 * TOK * D * FF, 4_000_000, 8,
    )(cot, w_down)

    q, no, ne_mid, kv_mid, p_mid, attn_mid = call(
        middle_kernel,
        [
            ((TOK, D), BF16), ((TOK, D), BF16), ((ROWS * EC, D), BF16), ((ROWS * EC, 2 * D), BF16),
            ((2, 256, KT), F32), ((QT, D), BF16),
        ],
        [], 0, 5, 600_000_000, 5_000_000, 10,
    )(mid, tok, gains, w_qkv, bias)

    half_u, half_d = ((16, 5, 16, D), BF16), ((4, 4, 2, 32, D), BF16)
    half_q, half_k = ((16, 16, D), BF16), ((48, 16, D), BF16)
    u_keep, u_send, d_keep, d_send, gm, kv, p_out, ne, gain_mid = call(
        forward_kernel,
        [
            half_u, half_u, half_d, half_d, ((TOK, D), BF16), ((EXT, 2 * D), BF16), ((4, 256, KT), F32),
            ((EXT, D), BF16), ((1, D), F32),
        ],
        [pltpu.VMEM((TOK, D), BF16), pltpu.VMEM((2, 64, 8, D), F32)], 1, 15, 4_000_000_000, 20_000_000, 16,
    )(coord, rim_a, rim_b, tok, cot, gains, w_qkv, w_out, w_up, gact, bias, pt_u, q, ne_mid, kv_mid, attn_mid)

    u_got = send(u_send, CORE_SWAP)
    d_got = send(d_send, CORE_SWAP)
    k_keep, k_send, dq, dkv = call(
        backward_kernel,
        [half_k, half_k, ((TOK, D), BF16), ((EXT, 2 * D), BF16)],
        [], 0, 10, 2_500_000_000, 10_000_000, 12,
    )(gm, w_out, q, kv, p_mid, p_out, ne, no, pt_u, pt_k)
    u_got, d_got, k_send = lax.optimization_barrier((u_got, d_got, k_send))
    k_got = send(k_send, CORE_SWAP)
    gne, gnq, gain, row_a, row_b = call(
        inputs_kernel,
        [
            ((ROWS * EC, D), F32), ((TOK, D), F32), ((16, D), BF16),
            ((RIM, EC, D), BF16), ((RIM, EC, D), BF16),
        ],
        [pltpu.VMEM(((ROWS + 2 * RIM) * EC, D), F32)], 1, 8, 600_000_000, 4_000_000, 6,
    )(coord, dq, dkv, w_qkv, mid, rim_a, rim_b, tok, gain_mid)
    gain_got = send(gain, CORE_SWAP)

    def place(x, axis, odd, end_if_odd, size):
        gap = size - RIM
        after = [(0, 0)] * 3
        before = [(0, 0)] * 3
        after[axis], before[axis] = (0, gap), (gap, 0)
        x = x.astype(F32)
        x_odd, x_even = (before, after) if end_if_odd else (after, before)
        return jnp.where(odd, jnp.pad(x, x_odd), jnp.pad(x, x_even))

    def join(body, ins, outs):
        return list(call(body, [(o, BF16) for o in outs], [], 0, len(ins), 1_000_000, 4_000_000, 6)(*ins))

    def first(sent, bit):
        return send(sent[0], by(bit)), send(sent[1], by(3 * bit))

    def second(sent, bit):
        return send(sent[0], by(3 * bit)), send(sent[1], by(bit))

    k_got, gnq, gain_got = lax.optimization_barrier((k_got, gnq, gain_got))
    u_p, u_q, *u_stay = join(
        join_up_q_kernel, [u_keep.reshape(80, 16, D), u_got.reshape(80, 16, D), k_keep, k_got, gain, gain_got, row_b],
        [(28, 16, D), (24, 16, D), (25, 16, D), (24, 16, D)],
    )
    u_first = first((u_p, u_q), X_BIT)
    b_p, b_q, *b_stay = join(
        join_down_kv_kernel, [d_keep.reshape(64, 16, D), d_got.reshape(64, 16, D), k_keep, k_got], [(24, 16, D)] * 4,
    )
    b_first = first((b_p, b_q), Y_BIT)
    row_a = send(row_a, ROW_A)
    b_first, row_a = lax.optimization_barrier((b_first, row_a))
    u_p, u_q, *u_own = join(second_kernel, [*u_first, *u_stay], [(13, 16, D), (12, 16, D)] * 2)
    u_second = second((u_p, u_q), X_BIT)
    b_p, b_q, *b_own = join(second_kernel, [*b_first, *b_stay], [(12, 16, D)] * 4)
    b_second = second((b_p, b_q), Y_BIT)
    gne = gne.reshape(ROWS, EC, D)
    gne = gne + place(row_a, 0, row_odd, True, ROWS) + place(u_first[0][25:], 0, row_odd, False, ROWS)
    u = join(sum_up_q_kernel, [*u_second, *u_own], [(7, 16, D)] * 4)
    u = to_three(u, Y_BIT)
    b = join(sum_down_kv_kernel, [*b_second, *b_own], [(6, 16, D)] * 4)
    b = to_three(b, X_BIT)
    to_a = gne[:, COLS : COLS + RIM].astype(BF16)
    to_b = gne[:, COLS + RIM : COLS + 2 * RIM].astype(BF16)
    u, b, gne, to_a, to_b = lax.optimization_barrier((u, b, gne, to_a, to_b))
    (spread,) = call(
        reduce_xy_kernel, [((8, ZROWS, 128), BF16)], [pltpu.VMEM((8 * ZROWS, 128), F32)], 0, 8, 60_000_000, 4_000_000, 5,
    )(*u, *b)
    got_z = exchange(spread, Z_GROUPS)
    back_b, back_a = send(to_b, COL_B), send(to_a, COL_A)
    g_up, g_down, g_out, g_qkv, g_gains = call(
        reduce_z_kernel,
        [((32, 128), F32), ((32, 128), F32), ((8, 128), F32), ((24, 128), F32), ((2, D), F32)],
        [], 0, 1, 100_000_000_000, 400_000, 4,
    )(got_z)

    g_gains, back_a, back_b = lax.optimization_barrier((g_gains, back_a, back_b))
    gn = gne[:, :COLS] + place(back_a, 1, col_odd, True, COLS) + place(back_b, 1, col_odd, False, COLS)
    gn = gn + gnq.reshape(ROWS, COLS, D)
    unit, inv = unit_of(tokens.astype(F32))
    g1 = gn * gains[0]
    front = inv * (g1 - unit * jnp.mean(g1 * unit, axis=-1, keepdims=True))
    grad_tokens = (gm.reshape(ROWS, COLS, D).astype(F32) + front).astype(BF16)
    return (grad_tokens, g_qkv.reshape(-1), g_out.reshape(-1), g_up.reshape(-1), g_down.reshape(-1), g_gains)


def solution(mesh):
    block = P("row", "col", None)
    flat = P(("row", "col"))
    return jax.shard_map(
        per_device,
        mesh=mesh,
        in_specs=(block, block, P(), P(), P(), P(), P(), block),
        out_specs=(block, flat, flat, flat, flat, P()),
        check_vma=False,
    )
```

```python
import math

import jax
import jax.numpy as jnp
from jax import lax
from jax.experimental import pallas as pl
from jax.experimental.pallas import tpu as pltpu
from jax.sharding import PartitionSpec as P

D = 512
FF = 2048
HEADS = 8
WINDOW = 7
TILE = 8
RIM = WINDOW // 2
EPS = 1e-06
AXES = ("row", "col")
N_COL = 32
GRID_ROWS = 192
GRID_COLS = 256
ROWS = 24
COLS = 8
TOK = ROWS * COLS
TILES = ROWS // TILE
ER = 32
EC = 16
EXT = ER * EC
QT = TILE * TILE
ZROWS = 112
KT = 256
F32 = jnp.float32
BF16 = jnp.bfloat16
GELU_C = math.sqrt(2.0 / math.pi)


def nn(a, b):
    return lax.dot_general(a, b, (((1,), (0,)), ((), ())), preferred_element_type=F32)


def nt(a, b):
    return lax.dot_general(a, b, (((1,), (1,)), ((), ())), preferred_element_type=F32)


def tn(a, b):
    return lax.dot_general(a, b, (((0,), (0,)), ((), ())), preferred_element_type=F32)


def unit_of(x):
    inv = lax.rsqrt(jnp.mean(x * x, axis=-1, keepdims=True) + EPS)
    return x * inv, inv


def head_mask(rows, h):
    lane = lax.broadcasted_iota(jnp.int32, (rows, 256), 1)
    return (lane // 64) == h


def stack_heads(x):
    zero = jnp.zeros_like(x)
    return jnp.concatenate([jnp.where(head_mask(x.shape[0], h), x, zero) for h in range(4)], axis=0)


def unstack_heads(x):
    rows = x.shape[0] // 4
    out = jnp.where(head_mask(rows, 0), x[:rows], 0.0)
    for h in range(1, 4):
        out = out + jnp.where(head_mask(rows, h), x[h * rows : (h + 1) * rows], 0.0)
    return out


def prep_front_kernel(cot, w_down, gact):
    for c in range(4):
        gact[:, c * 512 : (c + 1) * 512] = nt(cot[...], w_down[c * 512 : (c + 1) * 512, :])


def prep_mask_kernel(coord, mask, bias):
    q = lax.broadcasted_iota(jnp.int32, (QT, KT), 0)
    k = lax.broadcasted_iota(jnp.int32, (QT, KT), 1)
    ki = k // EC
    kc = k % EC
    odd = coord[1] & 1
    near = kc - COLS + odd * (COLS + RIM)
    far = kc - COLS - RIM + (1 - odd) * (COLS + RIM)
    kj = jnp.where(kc < COLS, kc + RIM, jnp.where(kc < COLS + RIM, near, jnp.where(kc < COLS + 2 * RIM, far, -99)))
    da = ki - q // TILE
    db = kj - q % TILE
    slot = jnp.where((da >= 0) & (da < WINDOW) & (db >= 0) & (db < WINDOW), da * WINDOW + db, -1)
    allowed = [jnp.zeros((QT, KT), jnp.int32) for _ in range(TILES)]
    for s in range(WINDOW * WINDOW):
        here = slot == s
        for t in range(TILES):
            allowed[t] = jnp.where(here, mask[t, 0, s], allowed[t])
    gc = coord[1] * COLS + kj - RIM
    for t in range(TILES):
        gr = coord[0] * ROWS + t * TILE + ki - RIM
        ok = (allowed[t] == 1) & (gr >= 0) & (gr < GRID_ROWS) & (gc >= 0) & (gc < GRID_COLS)
        bias[t] = jnp.where(ok, 0.0, -1e30)


def prep_order_kernel(coord, pt_u, pt_k):
    me = coord[2]
    lane = lax.broadcasted_iota(jnp.int32, (512, 512), 1)
    p = lax.broadcasted_iota(jnp.int32, (512, 512), 0)
    core_z = ((p >> 3) & 1) * 128 + ((p >> 1) & 3) * 2 + (p >> 8)
    hi, lo = (p >> 6) & 3, (p >> 4) & 3
    here = me & 121
    pt_u[...] = jnp.where(lane == ((core_z + hi * 32 + lo * 8) ^ here) * 2 + (p & 1), 1.0, 0.0).astype(BF16)
    pt_k[...] = jnp.where(lane == ((core_z + hi * 8 + lo * 32) ^ here) * 2 + (p & 1), 1.0, 0.0).astype(BF16)


def attend(qt, keys, vals, bias_t):
    s = nt(stack_heads(qt), keys) * 0.125 + jnp.concatenate([bias_t] * 4, axis=0)
    e = jnp.exp(s - jnp.max(s, axis=-1, keepdims=True))
    prob = e / jnp.sum(e, axis=-1, keepdims=True)
    return prob, unstack_heads(nn(prob.astype(BF16), vals)).astype(BF16)


def middle_kernel(mid, tok, gains, w_qkv, bias, q_o, no_o, ne_o, kv_o, p_o, attn_o):
    unit_e, _ = unit_of(mid[...].reshape(ROWS * EC, D).astype(F32))
    ne = (unit_e * gains[0:1, :]).astype(BF16)
    ne_o[...] = ne
    kv_o[...] = nn(ne, w_qkv[:, D:]).astype(BF16)
    unit_o, _ = unit_of(tok[...].astype(F32))
    no = (unit_o * gains[0:1, :]).astype(BF16)
    no_o[...] = no
    q_o[...] = nn(no, w_qkv[:, :D]).astype(BF16)
    at = 128 - RIM * EC
    for g in range(2):
        cols = slice(g * 256, (g + 1) * 256)
        vcols = slice(D + g * 256, D + (g + 1) * 256)
        prob, o = attend(q_o[QT : 2 * QT, cols], kv_o[at : at + KT, cols], kv_o[at : at + KT, vcols], bias[1])
        p_o[g] = prob
        attn_o[:, cols] = o


def forward_kernel(
    coord, rim_a, rim_b, tok, cot, gains, w_qkv, w_out, w_up, gact, bias, pt_u, q_i, ne_i, kv_i, attn_i,
    u_keep, u_send, d_keep, d_send, gm_o, kv_o, p_o, ne_o, gain_o, attn_s, rows_s,
):
    odd = coord[0] & 1
    edge = RIM * EC
    at_a = pl.multiple_of(odd * (RIM + ROWS) * EC, EC)
    at_b = pl.multiple_of((1 - odd) * (RIM + ROWS) * EC, EC)
    end = (RIM + ROWS) * EC
    both = jnp.concatenate([rim_a[...].reshape(edge, D), rim_b[...].reshape(edge, D)], axis=0)
    unit_r, _ = unit_of(both.astype(F32))
    ne_r = (unit_r * gains[0:1, :]).astype(BF16)
    kv_r = nn(ne_r, w_qkv[:, D:]).astype(BF16)
    for ref, mid, rims in ((ne_o, ne_i, ne_r), (kv_o, kv_i, kv_r)):
        ref[edge:end, :] = mid[...]
        ref[pl.ds(at_a, edge), :] = rims[:edge]
        ref[pl.ds(at_b, edge), :] = rims[edge:]
        ref[end + edge :, :] = jnp.zeros((EXT - end - edge, ref.shape[1]), BF16)
    xt = tok[...].astype(F32)
    attn_s[QT : 2 * QT, :] = attn_i[...]
    for i, t in enumerate((0, 2)):
        rows = slice(t * 128, t * 128 + KT)
        for g in range(2):
            cols = slice(g * 256, (g + 1) * 256)
            vcols = slice(D + g * 256, D + (g + 1) * 256)
            prob, o = attend(q_i[t * QT : (t + 1) * QT, cols], kv_o[rows, cols], kv_o[rows, vcols], bias[t])
            p_o[i * 2 + g] = prob
            attn_s[t * QT : (t + 1) * QT, cols] = o
    attn = attn_s[...]
    mixed = (xt + nn(attn, w_out[...])).astype(BF16)
    um, inv_m = unit_of(mixed.astype(F32))
    nm = (um * gains[1:2, :]).astype(BF16)
    nmt = nt(pt_u[...], nm).astype(BF16)
    gn = jnp.zeros((TOK, D), F32)
    for c in range(4):
        cols = slice(c * 512, (c + 1) * 512)
        pre = nn(nm, w_up[:, cols])
        th = jnp.tanh(GELU_C * (pre + 0.044715 * (pre * pre * pre)))
        half = 0.5 * (1.0 + th)
        act = (pre * half).astype(BF16)
        slope = half + 0.5 * pre * (1.0 - th * th) * (GELU_C * (1.0 + 0.134145 * (pre * pre)))
        gp = (gact[:, cols] * slope).astype(BF16)
        gn = gn + nt(gp, w_up[:, cols])
        gu = nn(nmt, gp).astype(BF16)
        u_keep[:, c] = gu[:256].reshape(16, 16, D)
        u_send[:, c] = gu[256:].reshape(16, 16, D)
        rows_s[c & 1] = tn(act, cot[...]).reshape(64, 8, D)
        xh = (c & 1) ^ ((coord[2] >> 6) & 1)
        for y in range(4):
            for xl in range(2):
                for co, ref in ((0, d_keep), (1, d_send)):
                    at = (xl * 32 + y * 8 + co) ^ (coord[2] & 57)
                    part = jnp.concatenate([rows_s[c & 1, at + 2 * zl] for zl in range(4)], axis=0)
                    ref[y, xh * 2 + xl, c >> 1] = part.astype(BF16)
    g = gn * gains[1:2, :]
    gm = (cot[...].astype(F32) + inv_m * (g - um * jnp.mean(g * um, axis=-1, keepdims=True))).astype(BF16)
    gm_o[...] = gm
    gain_o[...] = jnp.sum(gn * um, axis=0, keepdims=True)
    go = nn(nt(pt_u[...], attn).astype(BF16), gm).astype(BF16)
    u_keep[:, 4] = go[:256].reshape(16, 16, D)
    u_send[:, 4] = go[256:].reshape(16, 16, D)


def backward_kernel(
    gm, w_out, q, kv, p_mid, p_out, ne, no, pt_u, pt_k,
    k_keep, k_send, dq_s, dkv_o,
):
    ga = nt(gm[...], w_out[...]).astype(BF16)
    for g in range(2):
        cols = slice(g * 256, (g + 1) * 256)
        vcols = slice(D + g * 256, D + (g + 1) * 256)
        left_k = left_v = None
        for t in range(TILES):
            rows = slice(t * 128, t * 128 + KT)
            prob = p_mid[g] if t == 1 else p_out[t + g]
            gas = stack_heads(ga[t * QT : (t + 1) * QT, cols])
            qs = stack_heads(q[t * QT : (t + 1) * QT, cols])
            gp = nt(gas, kv[rows, vcols])
            inner = jnp.sum(prob * gp, axis=-1, keepdims=True)
            ds = (prob * (gp - inner) * 0.125).astype(BF16)
            dq_s[t * QT : (t + 1) * QT, cols] = unstack_heads(nn(ds, kv[rows, cols])).astype(BF16)
            dk, dv = tn(ds, qs), tn(prob.astype(BF16), gas)
            top_k, top_v = dk[:128], dv[:128]
            if t:
                top_k, top_v = top_k + left_k, top_v + left_v
            left_k, left_v = dk[128:], dv[128:]
            dkv_o[t * 128 : t * 128 + 128, cols] = top_k.astype(BF16)
            dkv_o[t * 128 : t * 128 + 128, vcols] = top_v.astype(BF16)
        dkv_o[TILES * 128 :, cols] = left_k.astype(BF16)
        dkv_o[TILES * 128 :, vcols] = left_v.astype(BF16)
    dkv = dkv_o[...]
    gk = nn(nt(pt_k[...], ne[...]).astype(BF16), dkv).astype(BF16)
    gq = nn(nt(pt_u[...], no[...]).astype(BF16), dq_s[...]).astype(BF16)
    for at, out in ((0, k_keep), (256, k_send)):
        out[:16] = gq[at : at + 256].reshape(16, 16, D)
        for i in range(2):
            for j in range(16):
                out[16 + j * 2 + i] = gk[at + j * 16 : at + j * 16 + 16, i * D : (i + 1) * D]


def inputs_kernel(coord, dq, dkv, w_qkv, mid, rim_a, rim_b, tok, gain_mid, gne_o, gnq_o, gain_o, row_a, row_b, gne_s):
    gne = nt(dkv[...], w_qkv[:, D:])
    gnq = nt(dq[...], w_qkv[:, :D])
    gne_s[...] = gne[: (ROWS + 2 * RIM) * EC]
    gne_o[...] = gne[RIM * EC : (RIM + ROWS) * EC]
    gnq_o[...] = gnq
    gain_in = jnp.sum(gnq * unit_of(tok[...].astype(F32))[0], axis=0, keepdims=True)
    odd = coord[0] & 1
    for ref, at in ((rim_a, odd * (RIM + ROWS)), (mid, RIM), (rim_b, (1 - odd) * (RIM + ROWS))):
        size = ref.shape[0] * EC
        unit, _ = unit_of(ref[...].reshape(size, D).astype(F32))
        part = gne_s[pl.ds(pl.multiple_of(at * EC, EC), size), :]
        gain_in = gain_in + jnp.sum(part * unit, axis=0, keepdims=True)
    spread = jnp.concatenate([gain_in, gain_mid[...], jnp.zeros((14, D), F32)], axis=0).astype(BF16)
    gain_o[...] = spread
    for ref, at in ((row_a, odd * (RIM + ROWS)), (row_b, (1 - odd) * (RIM + ROWS))):
        rim = gne_s[pl.ds(pl.multiple_of(at * EC, EC), RIM * EC), :]
        ref[...] = rim.astype(BF16).reshape(RIM, EC, D)


def add2(a, b):
    return (a.astype(F32) + b.astype(F32)).astype(BF16)


def add4(parts):
    a, b, c, d = [v.astype(F32) for v in parts]
    return ((a + b) + (c + d)).astype(BF16)


def halves():
    return ((0, (1, 2), (0, 3)), (1, (3, 2), (0, 1)))


def join_down_kv_kernel(dk, dg, kk, kg, *outs):
    for h, away, stay in halves():
        for out, chunks in ((outs[h], away), (outs[2 + h], stay)):
            for i, d in enumerate(chunks):
                lo, at = d * 16 + h * 8, i * 12
                out[at : at + 8] = add2(dk[lo : lo + 8], dg[lo : lo + 8])
                lo = 16 + d * 8 + h * 4
                out[at + 8 : at + 12] = add2(kk[lo : lo + 4], kg[lo : lo + 4])


def join_up_q_kernel(uk, ug, kk, kg, gk, gg, ride, *outs):
    for h, away, stay in halves():
        for out, chunks in ((outs[h], away), (outs[2 + h], stay)):
            for i, d in enumerate(chunks):
                lo, at = d * 20 + h * 10, i * 12
                out[at : at + 10] = add2(uk[lo : lo + 10], ug[lo : lo + 10])
                lo = d * 4 + h * 2
                out[at + 10 : at + 12] = add2(kk[lo : lo + 2], kg[lo : lo + 2])
    gain = add2(gk[...], gg[...])
    outs[0][24] = gain
    outs[2][24] = gain
    outs[0][25:] = ride[...]


def second_kernel(p_got, q_got, p_keep, q_keep, p_send, q_send, p_own, q_own):
    p_own[:12] = add2(p_keep[:12], p_got[:12])
    p_send[:12] = add2(p_keep[12:24], p_got[12:24])
    q_own[...] = add2(q_keep[:12], q_got[:12])
    q_send[...] = add2(q_keep[12:], q_got[12:])
    if p_keep.shape[0] == 25:
        gain = add2(p_keep[24], p_got[24])
        p_own[12] = gain
        p_send[12] = gain


def sum_up_q_kernel(p_got, q_got, p_own, q_own, *outs):
    gain = add2(p_got[12], p_own[12])
    for h, got, own in ((0, p_got, p_own), (1, q_got, q_own)):
        for i in range(2):
            out = outs[2 * h + i]
            out[:5] = add2(got[i * 5 : i * 5 + 5], own[i * 5 : i * 5 + 5])
            out[5] = add2(got[10 + i], own[10 + i])
            out[6] = gain


def sum_down_kv_kernel(p_got, q_got, p_own, q_own, *outs):
    for h, got, own in ((0, p_got, p_own), (1, q_got, q_own)):
        for i in range(2):
            out = outs[2 * h + i]
            out[:4] = add2(got[i * 4 : i * 4 + 4], own[i * 4 : i * 4 + 4])
            out[4:] = add2(got[8 + i * 2 : 10 + i * 2], own[8 + i * 2 : 10 + i * 2])


def reduce_xy_kernel(*refs):
    out, flat_s = refs[8:]
    sums = [add4([r[...] for r in refs[:4]]).reshape(-1, D), add4([r[...] for r in refs[4:8]]).reshape(-1, D)]
    acc = jnp.concatenate(sums, axis=0)
    rows = acc.shape[0]
    per = ZROWS // 4
    i = lax.broadcasted_iota(jnp.int32, (8 * per, rows), 0)
    lane = lax.broadcasted_iota(jnp.int32, (8 * per, rows), 1)
    z = i // per
    r = i % per
    up = (r % 4) * 16 + z * 2 + r // 4
    down = 112 + z * 8 + (r - 8)
    o = 64 + z * 2 + (r - 16)
    part = (r - 18) % 3
    qkv = jnp.where(part == 0, 80, 160 + part * 16) + z * 2 + (r - 18) // 3
    gain = 96 + (r - 24)
    src = jnp.where(r < 8, up, jnp.where(r < 16, down, jnp.where(r < 18, o, jnp.where(r < 24, qkv, gain))))
    picked = nn(jnp.where((lane == src) & (r < 26), 1.0, 0.0).astype(BF16), acc)
    for j in range(4):
        flat_s[pl.ds(j, 8 * per, stride=4), :] = picked[:, j * 128 : (j + 1) * 128]
    out[...] = flat_s[...].astype(BF16).reshape(8, ZROWS, 128)


def reduce_z_kernel(got, up, down, o, qkv, gain):
    acc = got[0].astype(F32)
    for j in range(1, 8):
        acc = acc + got[j].astype(F32)
    acc = acc * (1.0 / math.sqrt(GRID_ROWS * GRID_COLS))
    at = 0
    for ref in (up, down, o, qkv):
        ref[...] = acc[at : at + ref.shape[0]]
        at += ref.shape[0]
    for r in range(2):
        for j in range(4):
            gain[r : r + 1, j * 128 : (j + 1) * 128] = acc[at + 4 * r + j : at + 4 * r + j + 1]


def call(body, outs, scratch, n_smem, n_in, flops, nbytes, mib):
    smem = pl.BlockSpec(memory_space=pltpu.SMEM)
    vmem = pl.BlockSpec(memory_space=pltpu.VMEM)
    return pl.pallas_call(
        body,
        out_shape=[jax.ShapeDtypeStruct(s, d) for s, d in outs],
        in_specs=[smem] * n_smem + [vmem] * n_in,
        out_specs=[vmem] * len(outs),
        scratch_shapes=scratch,
        compiler_params=pltpu.CompilerParams(vmem_limit_bytes=mib * 1024 * 1024),
        cost_estimate=pl.CostEstimate(flops=flops, bytes_accessed=nbytes, transcendentals=0),
    )


def pairs(stride, count, first):
    out = []
    for k in range(256):
        at = (k // stride) % count
        other = at + 1 if (at - first) % 2 == 0 else at - 1
        if 0 <= other < count:
            out.append((k, k + (other - at) * stride))
    return out


ROW_A, ROW_B = pairs(N_COL, 8, 1), pairs(N_COL, 8, 0)
COL_A, COL_B = pairs(1, N_COL, 1), pairs(1, N_COL, 0)
CORE_SWAP = [(k, k ^ 1) for k in range(256)]
X_BIT = 32
Y_BIT = 8
Z_GROUPS = [[zh * 128 + x * 32 + y * 8 + zl * 2 + c for zh in range(2) for zl in range(4)] for x in range(4) for y in range(4) for c in range(2)]


def send(x, perm):
    return lax.ppermute(x, AXES, perm)


def by(bits):
    return [(k, k ^ bits) for k in range(256)]


def to_three(chunks, bit):
    got = {d: send(chunks[d], by(bit * d)) for d in (2, 1, 3)}
    return [chunks[0], got[2], got[1], got[3]]


def exchange(x, groups):
    return lax.all_to_all(x, AXES, 0, 0, axis_index_groups=groups, tiled=True)


def per_device(tokens, cotangent, gains, w_qkv, w_out, w_up, w_down, tile_mask):
    row = lax.axis_index("row")
    col = lax.axis_index("col")
    coord = jnp.stack([row, col, row * N_COL + col]).astype(jnp.int32)
    tok = tokens.reshape(TOK, D)
    cot = cotangent.reshape(TOK, D)

    row_odd = (row & 1) == 1
    col_odd = (col & 1) == 1
    first, last = tokens[:, :RIM], tokens[:, COLS - RIM :]
    side_b = send(jnp.where(col_odd, first, last), COL_B)
    side_a = send(jnp.where(col_odd, last, first), COL_A)
    (bias,) = call(
        prep_mask_kernel, [((TILES, QT, KT), F32)], [], 2, 0, 2 * TOK * D * FF, 4_000_000, 8,
    )(coord, tile_mask)
    side_a, side_b, cot, bias, coord = lax.optimization_barrier((side_a, side_b, cot, bias, coord))
    mid = jnp.concatenate([tokens, side_a, side_b, jnp.zeros((ROWS, EC - COLS - 2 * RIM, D), BF16)], axis=1)
    rim_b = send(jnp.where(row_odd, mid[:RIM], mid[ROWS - RIM :]), ROW_B)
    rim_a = send(jnp.where(row_odd, mid[ROWS - RIM :], mid[:RIM]), ROW_A)
    pt_u, pt_k = call(
        prep_order_kernel, [((D, D), BF16)] * 2, [], 1, 0, 2 * TOK * D * FF, 4_000_000, 8,
    )(coord)
    (gact,) = call(
        prep_front_kernel, [((TOK, FF), F32)], [], 0, 2, 2 * TOK * D * FF, 4_000_000, 8,
    )(cot, w_down)

    q, no, ne_mid, kv_mid, p_mid, attn_mid = call(
        middle_kernel,
        [
            ((TOK, D), BF16), ((TOK, D), BF16), ((ROWS * EC, D), BF16), ((ROWS * EC, 2 * D), BF16),
            ((2, 256, KT), F32), ((QT, D), BF16),
        ],
        [], 0, 5, 600_000_000, 5_000_000, 10,
    )(mid, tok, gains, w_qkv, bias)

    half_u, half_d = ((16, 5, 16, D), BF16), ((4, 4, 2, 32, D), BF16)
    half_q, half_k = ((16, 16, D), BF16), ((48, 16, D), BF16)
    u_keep, u_send, d_keep, d_send, gm, kv, p_out, ne, gain_mid = call(
        forward_kernel,
        [
            half_u, half_u, half_d, half_d, ((TOK, D), BF16), ((EXT, 2 * D), BF16), ((4, 256, KT), F32),
            ((EXT, D), BF16), ((1, D), F32),
        ],
        [pltpu.VMEM((TOK, D), BF16), pltpu.VMEM((2, 64, 8, D), F32)], 1, 15, 4_000_000_000, 20_000_000, 16,
    )(coord, rim_a, rim_b, tok, cot, gains, w_qkv, w_out, w_up, gact, bias, pt_u, q, ne_mid, kv_mid, attn_mid)

    u_got = send(u_send, CORE_SWAP)
    d_got = send(d_send, CORE_SWAP)
    k_keep, k_send, dq, dkv = call(
        backward_kernel,
        [half_k, half_k, ((TOK, D), BF16), ((EXT, 2 * D), BF16)],
        [], 0, 10, 2_500_000_000, 10_000_000, 12,
    )(gm, w_out, q, kv, p_mid, p_out, ne, no, pt_u, pt_k)
    u_got, d_got, k_send = lax.optimization_barrier((u_got, d_got, k_send))
    k_got = send(k_send, CORE_SWAP)
    gne, gnq, gain, row_a, row_b = call(
        inputs_kernel,
        [
            ((ROWS * EC, D), F32), ((TOK, D), F32), ((16, D), BF16),
            ((RIM, EC, D), BF16), ((RIM, EC, D), BF16),
        ],
        [pltpu.VMEM(((ROWS + 2 * RIM) * EC, D), F32)], 1, 8, 600_000_000, 4_000_000, 6,
    )(coord, dq, dkv, w_qkv, mid, rim_a, rim_b, tok, gain_mid)
    gain_got = send(gain, CORE_SWAP)

    def place(x, axis, odd, end_if_odd, size):
        gap = size - RIM
        after = [(0, 0)] * 3
        before = [(0, 0)] * 3
        after[axis], before[axis] = (0, gap), (gap, 0)
        x = x.astype(F32)
        x_odd, x_even = (before, after) if end_if_odd else (after, before)
        return jnp.where(odd, jnp.pad(x, x_odd), jnp.pad(x, x_even))

    def join(body, ins, outs):
        return list(call(body, [(o, BF16) for o in outs], [], 0, len(ins), 1_000_000, 4_000_000, 6)(*ins))

    def first(sent, bit):
        return send(sent[0], by(bit)), send(sent[1], by(3 * bit))

    def second(sent, bit):
        return send(sent[0], by(3 * bit)), send(sent[1], by(bit))

    k_got, gnq = lax.optimization_barrier((k_got, gnq))
    b_p, b_q, *b_stay = join(
        join_down_kv_kernel, [d_keep.reshape(64, 16, D), d_got.reshape(64, 16, D), k_keep, k_got], [(24, 16, D)] * 4,
    )
    b_p, b_q, gain_got = lax.optimization_barrier((b_p, b_q, gain_got))
    b_first = first((b_p, b_q), Y_BIT)
    u_p, u_q, *u_stay = join(
        join_up_q_kernel, [u_keep.reshape(80, 16, D), u_got.reshape(80, 16, D), k_keep, k_got, gain, gain_got, row_b],
        [(28, 16, D), (24, 16, D), (25, 16, D), (24, 16, D)],
    )
    u_first = first((u_p, u_q), X_BIT)
    row_a = send(row_a, ROW_A)
    b_first, row_a = lax.optimization_barrier((b_first, row_a))
    u_p, u_q, *u_own = join(second_kernel, [*u_first, *u_stay], [(13, 16, D), (12, 16, D)] * 2)
    u_second = second((u_p, u_q), X_BIT)
    b_p, b_q, *b_own = join(second_kernel, [*b_first, *b_stay], [(12, 16, D)] * 4)
    b_second = second((b_p, b_q), Y_BIT)
    gne = gne.reshape(ROWS, EC, D)
    gne = gne + place(row_a, 0, row_odd, True, ROWS) + place(u_first[0][25:], 0, row_odd, False, ROWS)
    u = join(sum_up_q_kernel, [*u_second, *u_own], [(7, 16, D)] * 4)
    u = to_three(u, Y_BIT)
    b = join(sum_down_kv_kernel, [*b_second, *b_own], [(6, 16, D)] * 4)
    b = to_three(b, X_BIT)
    to_a = gne[:, COLS : COLS + RIM].astype(BF16)
    to_b = gne[:, COLS + RIM : COLS + 2 * RIM].astype(BF16)
    u, b, gne, to_a, to_b = lax.optimization_barrier((u, b, gne, to_a, to_b))
    (spread,) = call(
        reduce_xy_kernel, [((8, ZROWS, 128), BF16)], [pltpu.VMEM((8 * ZROWS, 128), F32)], 0, 8, 60_000_000, 4_000_000, 5,
    )(*u, *b)
    got_z = exchange(spread, Z_GROUPS)
    back_b, back_a = send(to_b, COL_B), send(to_a, COL_A)
    g_up, g_down, g_out, g_qkv, g_gains = call(
        reduce_z_kernel,
        [((32, 128), F32), ((32, 128), F32), ((8, 128), F32), ((24, 128), F32), ((2, D), F32)],
        [], 0, 1, 100_000_000_000, 400_000, 4,
    )(got_z)

    g_gains, back_a, back_b = lax.optimization_barrier((g_gains, back_a, back_b))
    gn = gne[:, :COLS] + place(back_a, 1, col_odd, True, COLS) + place(back_b, 1, col_odd, False, COLS)
    gn = gn + gnq.reshape(ROWS, COLS, D)
    unit, inv = unit_of(tokens.astype(F32))
    g1 = gn * gains[0]
    front = inv * (g1 - unit * jnp.mean(g1 * unit, axis=-1, keepdims=True))
    grad_tokens = (gm.reshape(ROWS, COLS, D).astype(F32) + front).astype(BF16)
    return (grad_tokens, g_qkv.reshape(-1), g_out.reshape(-1), g_up.reshape(-1), g_down.reshape(-1), g_gains)


def solution(mesh):
    block = P("row", "col", None)
    flat = P(("row", "col"))
    return jax.shard_map(
        per_device,
        mesh=mesh,
        in_specs=(block, block, P(), P(), P(), P(), P(), block),
        out_specs=(block, flat, flat, flat, flat, P()),
        check_vma=False,
    )
```

```python
import math

import jax
import jax.numpy as jnp
from jax import lax
from jax.experimental import pallas as pl
from jax.experimental.pallas import tpu as pltpu
from jax.sharding import PartitionSpec as P

D = 512
FF = 2048
HEADS = 8
WINDOW = 7
TILE = 8
RIM = WINDOW // 2
EPS = 1e-06
AXES = ("row", "col")
N_COL = 32
GRID_ROWS = 192
GRID_COLS = 256
ROWS = 24
COLS = 8
TOK = ROWS * COLS
TILES = ROWS // TILE
ER = 32
EC = 16
EXT = ER * EC
QT = TILE * TILE
ZROWS = 112
KT = 256
F32 = jnp.float32
BF16 = jnp.bfloat16
GELU_C = math.sqrt(2.0 / math.pi)


def nn(a, b):
    return lax.dot_general(a, b, (((1,), (0,)), ((), ())), preferred_element_type=F32)


def nt(a, b):
    return lax.dot_general(a, b, (((1,), (1,)), ((), ())), preferred_element_type=F32)


def tn(a, b):
    return lax.dot_general(a, b, (((0,), (0,)), ((), ())), preferred_element_type=F32)


def unit_of(x):
    inv = lax.rsqrt(jnp.mean(x * x, axis=-1, keepdims=True) + EPS)
    return x * inv, inv


def head_mask(rows, h):
    lane = lax.broadcasted_iota(jnp.int32, (rows, 256), 1)
    return (lane // 64) == h


def stack_heads(x):
    zero = jnp.zeros_like(x)
    return jnp.concatenate([jnp.where(head_mask(x.shape[0], h), x, zero) for h in range(4)], axis=0)


def unstack_heads(x):
    rows = x.shape[0] // 4
    out = jnp.where(head_mask(rows, 0), x[:rows], 0.0)
    for h in range(1, 4):
        out = out + jnp.where(head_mask(rows, h), x[h * rows : (h + 1) * rows], 0.0)
    return out


def prep_front_kernel(cot, w_down, gact):
    for c in range(4):
        gact[:, c * 512 : (c + 1) * 512] = nt(cot[...], w_down[c * 512 : (c + 1) * 512, :])


def prep_mask_kernel(coord, mask, bias):
    q = lax.broadcasted_iota(jnp.int32, (QT, KT), 0)
    k = lax.broadcasted_iota(jnp.int32, (QT, KT), 1)
    ki = k // EC
    kc = k % EC
    odd = coord[1] & 1
    near = kc - COLS + odd * (COLS + RIM)
    far = kc - COLS - RIM + (1 - odd) * (COLS + RIM)
    kj = jnp.where(kc < COLS, kc + RIM, jnp.where(kc < COLS + RIM, near, jnp.where(kc < COLS + 2 * RIM, far, -99)))
    da = ki - q // TILE
    db = kj - q % TILE
    slot = jnp.where((da >= 0) & (da < WINDOW) & (db >= 0) & (db < WINDOW), da * WINDOW + db, -1)
    allowed = [jnp.zeros((QT, KT), jnp.int32) for _ in range(TILES)]
    for s in range(WINDOW * WINDOW):
        here = slot == s
        for t in range(TILES):
            allowed[t] = jnp.where(here, mask[t, 0, s], allowed[t])
    gc = coord[1] * COLS + kj - RIM
    for t in range(TILES):
        gr = coord[0] * ROWS + t * TILE + ki - RIM
        ok = (allowed[t] == 1) & (gr >= 0) & (gr < GRID_ROWS) & (gc >= 0) & (gc < GRID_COLS)
        bias[t] = jnp.where(ok, 0.0, -1e30)


def prep_order_kernel(coord, pt_u, pt_k):
    me = coord[2]
    lane = lax.broadcasted_iota(jnp.int32, (512, 512), 1)
    p = lax.broadcasted_iota(jnp.int32, (512, 512), 0)
    core_z = ((p >> 3) & 1) * 128 + ((p >> 1) & 3) * 2 + (p >> 8)
    hi, lo = (p >> 6) & 3, (p >> 4) & 3
    here = me & 121
    pt_u[...] = jnp.where(lane == ((core_z + hi * 32 + lo * 8) ^ here) * 2 + (p & 1), 1.0, 0.0).astype(BF16)
    pt_k[...] = jnp.where(lane == ((core_z + hi * 8 + lo * 32) ^ here) * 2 + (p & 1), 1.0, 0.0).astype(BF16)


def attend(qt, keys, vals, bias_t):
    s = nt(stack_heads(qt * 0.125), keys) + jnp.concatenate([bias_t] * 4, axis=0)
    e = jnp.exp(s - jnp.max(s, axis=-1, keepdims=True))
    prob = e * (1.0 / jnp.sum(e, axis=-1, keepdims=True))
    return prob, unstack_heads(nn(prob.astype(BF16), vals)).astype(BF16)


def middle_kernel(mid, tok, gains, w_qkv, bias, q_o, no_o, ne_o, kv_o, p_o, attn_o):
    unit_e, _ = unit_of(mid[...].reshape(ROWS * EC, D).astype(F32))
    ne = (unit_e * gains[0:1, :]).astype(BF16)
    ne_o[...] = ne
    kv_o[...] = nn(ne, w_qkv[:, D:]).astype(BF16)
    unit_o, _ = unit_of(tok[...].astype(F32))
    no = (unit_o * gains[0:1, :]).astype(BF16)
    no_o[...] = no
    q_o[...] = nn(no, w_qkv[:, :D]).astype(BF16)
    at = 128 - RIM * EC
    for g in range(2):
        cols = slice(g * 256, (g + 1) * 256)
        vcols = slice(D + g * 256, D + (g + 1) * 256)
        prob, o = attend(q_o[QT : 2 * QT, cols], kv_o[at : at + KT, cols], kv_o[at : at + KT, vcols], bias[1])
        p_o[g] = prob
        attn_o[:, cols] = o


def forward_kernel(
    coord, rim_a, rim_b, tok, cot, gains, w_qkv, w_out, w_up, gact, bias, pt_u, q_i, ne_i, kv_i, attn_i,
    u_keep, u_send, d_keep, d_send, gm_o, kv_o, p_o, ne_o, gain_o, attn_s, rows_s,
):
    odd = coord[0] & 1
    edge = RIM * EC
    at_a = pl.multiple_of(odd * (RIM + ROWS) * EC, EC)
    at_b = pl.multiple_of((1 - odd) * (RIM + ROWS) * EC, EC)
    end = (RIM + ROWS) * EC
    both = jnp.concatenate([rim_a[...].reshape(edge, D), rim_b[...].reshape(edge, D)], axis=0)
    unit_r, _ = unit_of(both.astype(F32))
    ne_r = (unit_r * gains[0:1, :]).astype(BF16)
    kv_r = nn(ne_r, w_qkv[:, D:]).astype(BF16)
    for ref, mid, rims in ((ne_o, ne_i, ne_r), (kv_o, kv_i, kv_r)):
        ref[edge:end, :] = mid[...]
        ref[pl.ds(at_a, edge), :] = rims[:edge]
        ref[pl.ds(at_b, edge), :] = rims[edge:]
        ref[end + edge :, :] = jnp.zeros((EXT - end - edge, ref.shape[1]), BF16)
    xt = tok[...].astype(F32)
    attn_s[QT : 2 * QT, :] = attn_i[...]
    for i, t in enumerate((0, 2)):
        rows = slice(t * 128, t * 128 + KT)
        for g in range(2):
            cols = slice(g * 256, (g + 1) * 256)
            vcols = slice(D + g * 256, D + (g + 1) * 256)
            prob, o = attend(q_i[t * QT : (t + 1) * QT, cols], kv_o[rows, cols], kv_o[rows, vcols], bias[t])
            p_o[i * 2 + g] = prob
            attn_s[t * QT : (t + 1) * QT, cols] = o
    attn = attn_s[...]
    mixed = (xt + nn(attn, w_out[...])).astype(BF16)
    um, inv_m = unit_of(mixed.astype(F32))
    nm = (um * gains[1:2, :]).astype(BF16)
    nmt = nt(pt_u[...], nm).astype(BF16)
    gn = jnp.zeros((TOK, D), F32)
    for c in range(4):
        cols = slice(c * 512, (c + 1) * 512)
        pre = nn(nm, w_up[:, cols])
        th = jnp.tanh(GELU_C * (pre + 0.044715 * (pre * pre * pre)))
        half = 0.5 * (1.0 + th)
        act = (pre * half).astype(BF16)
        slope = half + 0.5 * pre * (1.0 - th * th) * (GELU_C * (1.0 + 0.134145 * (pre * pre)))
        gp = (gact[:, cols] * slope).astype(BF16)
        gn = gn + nt(gp, w_up[:, cols])
        gu = nn(nmt, gp).astype(BF16)
        u_keep[:, c] = gu[:256].reshape(16, 16, D)
        u_send[:, c] = gu[256:].reshape(16, 16, D)
        rows_s[c & 1] = tn(act, cot[...]).reshape(64, 8, D)
        xh = (c & 1) ^ ((coord[2] >> 6) & 1)
        for y in range(4):
            for xl in range(2):
                for co, ref in ((0, d_keep), (1, d_send)):
                    at = (xl * 32 + y * 8 + co) ^ (coord[2] & 57)
                    part = jnp.concatenate([rows_s[c & 1, at + 2 * zl] for zl in range(4)], axis=0)
                    ref[y, xh * 2 + xl, c >> 1] = part.astype(BF16)
    g = gn * gains[1:2, :]
    gm = (cot[...].astype(F32) + inv_m * (g - um * jnp.mean(g * um, axis=-1, keepdims=True))).astype(BF16)
    gm_o[...] = gm
    gain_o[...] = jnp.sum(gn * um, axis=0, keepdims=True)
    go = nn(nt(pt_u[...], attn).astype(BF16), gm).astype(BF16)
    u_keep[:, 4] = go[:256].reshape(16, 16, D)
    u_send[:, 4] = go[256:].reshape(16, 16, D)


def backward_kernel(
    gm, w_out, q, kv, p_mid, p_out, ne, no, pt_u, pt_k,
    k_keep, k_send, dq_s, dkv_o,
):
    ga = nt(gm[...], w_out[...]).astype(BF16)
    for g in range(2):
        cols = slice(g * 256, (g + 1) * 256)
        vcols = slice(D + g * 256, D + (g + 1) * 256)
        left_k = left_v = None
        for t in range(TILES):
            rows = slice(t * 128, t * 128 + KT)
            prob = p_mid[g] if t == 1 else p_out[t + g]
            gas = stack_heads(ga[t * QT : (t + 1) * QT, cols])
            qs = stack_heads(q[t * QT : (t + 1) * QT, cols])
            gp = nt(gas * 0.125, kv[rows, vcols])
            inner = jnp.sum(prob * gp, axis=-1, keepdims=True)
            ds = (prob * (gp - inner)).astype(BF16)
            dq_s[t * QT : (t + 1) * QT, cols] = unstack_heads(nn(ds, kv[rows, cols])).astype(BF16)
            dk, dv = tn(ds, qs), tn(prob.astype(BF16), gas)
            top_k, top_v = dk[:128], dv[:128]
            if t:
                top_k, top_v = top_k + left_k, top_v + left_v
            left_k, left_v = dk[128:], dv[128:]
            dkv_o[t * 128 : t * 128 + 128, cols] = top_k.astype(BF16)
            dkv_o[t * 128 : t * 128 + 128, vcols] = top_v.astype(BF16)
        dkv_o[TILES * 128 :, cols] = left_k.astype(BF16)
        dkv_o[TILES * 128 :, vcols] = left_v.astype(BF16)
    dkv = dkv_o[...]
    gk = nn(nt(pt_k[...], ne[...]).astype(BF16), dkv).astype(BF16)
    gq = nn(nt(pt_u[...], no[...]).astype(BF16), dq_s[...]).astype(BF16)
    for at, out in ((0, k_keep), (256, k_send)):
        out[:16] = gq[at : at + 256].reshape(16, 16, D)
        for i in range(2):
            for j in range(16):
                out[16 + j * 2 + i] = gk[at + j * 16 : at + j * 16 + 16, i * D : (i + 1) * D]


def inputs_kernel(coord, dq, dkv, w_qkv, mid, rim_a, rim_b, tok, gain_mid, gne_o, gnq_o, gain_o, row_a, row_b, gne_s):
    gne = nt(dkv[...], w_qkv[:, D:])
    gnq = nt(dq[...], w_qkv[:, :D])
    gne_s[...] = gne[: (ROWS + 2 * RIM) * EC]
    gne_o[...] = gne[RIM * EC : (RIM + ROWS) * EC]
    gnq_o[...] = gnq
    gain_in = jnp.sum(gnq * unit_of(tok[...].astype(F32))[0], axis=0, keepdims=True)
    odd = coord[0] & 1
    for ref, at in ((rim_a, odd * (RIM + ROWS)), (mid, RIM), (rim_b, (1 - odd) * (RIM + ROWS))):
        size = ref.shape[0] * EC
        unit, _ = unit_of(ref[...].reshape(size, D).astype(F32))
        part = gne_s[pl.ds(pl.multiple_of(at * EC, EC), size), :]
        gain_in = gain_in + jnp.sum(part * unit, axis=0, keepdims=True)
    spread = jnp.concatenate([gain_in, gain_mid[...], jnp.zeros((14, D), F32)], axis=0).astype(BF16)
    gain_o[...] = spread
    for ref, at in ((row_a, odd * (RIM + ROWS)), (row_b, (1 - odd) * (RIM + ROWS))):
        rim = gne_s[pl.ds(pl.multiple_of(at * EC, EC), RIM * EC), :]
        ref[...] = rim.astype(BF16).reshape(RIM, EC, D)


def add2(a, b):
    return (a.astype(F32) + b.astype(F32)).astype(BF16)


def add4(parts):
    a, b, c, d = [v.astype(F32) for v in parts]
    return ((a + b) + (c + d)).astype(BF16)


def halves():
    return ((0, (1, 2), (0, 3)), (1, (3, 2), (0, 1)))


def join_down_kv_kernel(dk, dg, kk, kg, *outs):
    for h, away, stay in halves():
        for out, chunks in ((outs[h], away), (outs[2 + h], stay)):
            for i, d in enumerate(chunks):
                lo, at = d * 16 + h * 8, i * 12
                out[at : at + 8] = add2(dk[lo : lo + 8], dg[lo : lo + 8])
                lo = 16 + d * 8 + h * 4
                out[at + 8 : at + 12] = add2(kk[lo : lo + 4], kg[lo : lo + 4])


def join_up_q_kernel(uk, ug, kk, kg, gk, gg, ride, *outs):
    for h, away, stay in halves():
        for out, chunks in ((outs[h], away), (outs[2 + h], stay)):
            for i, d in enumerate(chunks):
                lo, at = d * 20 + h * 10, i * 12
                out[at : at + 10] = add2(uk[lo : lo + 10], ug[lo : lo + 10])
                lo = d * 4 + h * 2
                out[at + 10 : at + 12] = add2(kk[lo : lo + 2], kg[lo : lo + 2])
    gain = add2(gk[...], gg[...])
    outs[0][24] = gain
    outs[2][24] = gain
    outs[0][25:] = ride[...]


def second_kernel(p_got, q_got, p_keep, q_keep, p_send, q_send, p_own, q_own):
    p_own[:12] = add2(p_keep[:12], p_got[:12])
    p_send[:12] = add2(p_keep[12:24], p_got[12:24])
    q_own[...] = add2(q_keep[:12], q_got[:12])
    q_send[...] = add2(q_keep[12:], q_got[12:])
    if p_keep.shape[0] == 25:
        gain = add2(p_keep[24], p_got[24])
        p_own[12] = gain
        p_send[12] = gain


def sum_up_q_kernel(p_got, q_got, p_own, q_own, *outs):
    gain = add2(p_got[12], p_own[12])
    for h, got, own in ((0, p_got, p_own), (1, q_got, q_own)):
        for i in range(2):
            out = outs[2 * h + i]
            out[:5] = add2(got[i * 5 : i * 5 + 5], own[i * 5 : i * 5 + 5])
            out[5] = add2(got[10 + i], own[10 + i])
            out[6] = gain


def sum_down_kv_kernel(p_got, q_got, p_own, q_own, *outs):
    for h, got, own in ((0, p_got, p_own), (1, q_got, q_own)):
        for i in range(2):
            out = outs[2 * h + i]
            out[:4] = add2(got[i * 4 : i * 4 + 4], own[i * 4 : i * 4 + 4])
            out[4:] = add2(got[8 + i * 2 : 10 + i * 2], own[8 + i * 2 : 10 + i * 2])


def reduce_xy_kernel(*refs):
    out, flat_s = refs[8:]
    sums = [add4([r[...] for r in refs[:4]]).reshape(-1, D), add4([r[...] for r in refs[4:8]]).reshape(-1, D)]
    acc = jnp.concatenate(sums, axis=0)
    rows = acc.shape[0]
    per = ZROWS // 4
    i = lax.broadcasted_iota(jnp.int32, (8 * per, rows), 0)
    lane = lax.broadcasted_iota(jnp.int32, (8 * per, rows), 1)
    z = i // per
    r = i % per
    up = (r % 4) * 16 + z * 2 + r // 4
    down = 112 + z * 8 + (r - 8)
    o = 64 + z * 2 + (r - 16)
    part = (r - 18) % 3
    qkv = jnp.where(part == 0, 80, 160 + part * 16) + z * 2 + (r - 18) // 3
    gain = 96 + (r - 24)
    src = jnp.where(r < 8, up, jnp.where(r < 16, down, jnp.where(r < 18, o, jnp.where(r < 24, qkv, gain))))
    picked = nn(jnp.where((lane == src) & (r < 26), 1.0, 0.0).astype(BF16), acc)
    for j in range(4):
        flat_s[pl.ds(j, 8 * per, stride=4), :] = picked[:, j * 128 : (j + 1) * 128]
    out[...] = flat_s[...].astype(BF16).reshape(8, ZROWS, 128)


def reduce_z_kernel(got, up, down, o, qkv, gain):
    acc = got[0].astype(F32)
    for j in range(1, 8):
        acc = acc + got[j].astype(F32)
    acc = acc * (1.0 / math.sqrt(GRID_ROWS * GRID_COLS))
    at = 0
    for ref in (up, down, o, qkv):
        ref[...] = acc[at : at + ref.shape[0]]
        at += ref.shape[0]
    for r in range(2):
        for j in range(4):
            gain[r : r + 1, j * 128 : (j + 1) * 128] = acc[at + 4 * r + j : at + 4 * r + j + 1]


def call(body, outs, scratch, n_smem, n_in, flops, nbytes, mib):
    smem = pl.BlockSpec(memory_space=pltpu.SMEM)
    vmem = pl.BlockSpec(memory_space=pltpu.VMEM)
    return pl.pallas_call(
        body,
        out_shape=[jax.ShapeDtypeStruct(s, d) for s, d in outs],
        in_specs=[smem] * n_smem + [vmem] * n_in,
        out_specs=[vmem] * len(outs),
        scratch_shapes=scratch,
        compiler_params=pltpu.CompilerParams(vmem_limit_bytes=mib * 1024 * 1024),
        cost_estimate=pl.CostEstimate(flops=flops, bytes_accessed=nbytes, transcendentals=0),
    )


def pairs(stride, count, first):
    out = []
    for k in range(256):
        at = (k // stride) % count
        other = at + 1 if (at - first) % 2 == 0 else at - 1
        if 0 <= other < count:
            out.append((k, k + (other - at) * stride))
    return out


ROW_A, ROW_B = pairs(N_COL, 8, 1), pairs(N_COL, 8, 0)
COL_A, COL_B = pairs(1, N_COL, 1), pairs(1, N_COL, 0)
CORE_SWAP = [(k, k ^ 1) for k in range(256)]
X_BIT = 32
Y_BIT = 8
Z_GROUPS = [[zh * 128 + x * 32 + y * 8 + zl * 2 + c for zh in range(2) for zl in range(4)] for x in range(4) for y in range(4) for c in range(2)]


def send(x, perm):
    return lax.ppermute(x, AXES, perm)


def by(bits):
    return [(k, k ^ bits) for k in range(256)]


def to_three(chunks, bit):
    got = {d: send(chunks[d], by(bit * d)) for d in (2, 1, 3)}
    return [chunks[0], got[2], got[1], got[3]]


def exchange(x, groups):
    return lax.all_to_all(x, AXES, 0, 0, axis_index_groups=groups, tiled=True)


def per_device(tokens, cotangent, gains, w_qkv, w_out, w_up, w_down, tile_mask):
    row = lax.axis_index("row")
    col = lax.axis_index("col")
    coord = jnp.stack([row, col, row * N_COL + col]).astype(jnp.int32)
    tok = tokens.reshape(TOK, D)
    cot = cotangent.reshape(TOK, D)

    row_odd = (row & 1) == 1
    col_odd = (col & 1) == 1
    first, last = tokens[:, :RIM], tokens[:, COLS - RIM :]
    side_b = send(jnp.where(col_odd, first, last), COL_B)
    side_a = send(jnp.where(col_odd, last, first), COL_A)
    (bias,) = call(
        prep_mask_kernel, [((TILES, QT, KT), F32)], [], 2, 0, 2 * TOK * D * FF, 4_000_000, 8,
    )(coord, tile_mask)
    side_a, side_b, cot, bias, coord = lax.optimization_barrier((side_a, side_b, cot, bias, coord))
    mid = jnp.concatenate([tokens, side_a, side_b, jnp.zeros((ROWS, EC - COLS - 2 * RIM, D), BF16)], axis=1)
    rim_b = send(jnp.where(row_odd, mid[:RIM], mid[ROWS - RIM :]), ROW_B)
    rim_a = send(jnp.where(row_odd, mid[ROWS - RIM :], mid[:RIM]), ROW_A)
    pt_u, pt_k = call(
        prep_order_kernel, [((D, D), BF16)] * 2, [], 1, 0, 2 * TOK * D * FF, 4_000_000, 8,
    )(coord)
    (gact,) = call(
        prep_front_kernel, [((TOK, FF), F32)], [], 0, 2, 2 * TOK * D * FF, 4_000_000, 8,
    )(cot, w_down)

    q, no, ne_mid, kv_mid, p_mid, attn_mid = call(
        middle_kernel,
        [
            ((TOK, D), BF16), ((TOK, D), BF16), ((ROWS * EC, D), BF16), ((ROWS * EC, 2 * D), BF16),
            ((2, 256, KT), F32), ((QT, D), BF16),
        ],
        [], 0, 5, 600_000_000, 5_000_000, 10,
    )(mid, tok, gains, w_qkv, bias)

    half_u, half_d = ((16, 5, 16, D), BF16), ((4, 4, 2, 32, D), BF16)
    half_q, half_k = ((16, 16, D), BF16), ((48, 16, D), BF16)
    u_keep, u_send, d_keep, d_send, gm, kv, p_out, ne, gain_mid = call(
        forward_kernel,
        [
            half_u, half_u, half_d, half_d, ((TOK, D), BF16), ((EXT, 2 * D), BF16), ((4, 256, KT), F32),
            ((EXT, D), BF16), ((1, D), F32),
        ],
        [pltpu.VMEM((TOK, D), BF16), pltpu.VMEM((2, 64, 8, D), F32)], 1, 15, 4_000_000_000, 20_000_000, 16,
    )(coord, rim_a, rim_b, tok, cot, gains, w_qkv, w_out, w_up, gact, bias, pt_u, q, ne_mid, kv_mid, attn_mid)

    u_got = send(u_send, CORE_SWAP)
    d_got = send(d_send, CORE_SWAP)
    k_keep, k_send, dq, dkv = call(
        backward_kernel,
        [half_k, half_k, ((TOK, D), BF16), ((EXT, 2 * D), BF16)],
        [], 0, 10, 2_500_000_000, 10_000_000, 12,
    )(gm, w_out, q, kv, p_mid, p_out, ne, no, pt_u, pt_k)
    u_got, d_got, k_send = lax.optimization_barrier((u_got, d_got, k_send))
    k_got = send(k_send, CORE_SWAP)
    gne, gnq, gain, row_a, row_b = call(
        inputs_kernel,
        [
            ((ROWS * EC, D), F32), ((TOK, D), F32), ((16, D), BF16),
            ((RIM, EC, D), BF16), ((RIM, EC, D), BF16),
        ],
        [pltpu.VMEM(((ROWS + 2 * RIM) * EC, D), F32)], 1, 8, 600_000_000, 4_000_000, 6,
    )(coord, dq, dkv, w_qkv, mid, rim_a, rim_b, tok, gain_mid)
    gain_got = send(gain, CORE_SWAP)

    def place(x, axis, odd, end_if_odd, size):
        gap = size - RIM
        after = [(0, 0)] * 3
        before = [(0, 0)] * 3
        after[axis], before[axis] = (0, gap), (gap, 0)
        x = x.astype(F32)
        x_odd, x_even = (before, after) if end_if_odd else (after, before)
        return jnp.where(odd, jnp.pad(x, x_odd), jnp.pad(x, x_even))

    def join(body, ins, outs):
        return list(call(body, [(o, BF16) for o in outs], [], 0, len(ins), 1_000_000, 4_000_000, 6)(*ins))

    def first(sent, bit):
        return send(sent[0], by(bit)), send(sent[1], by(3 * bit))

    def second(sent, bit):
        return send(sent[0], by(3 * bit)), send(sent[1], by(bit))

    k_got, gnq = lax.optimization_barrier((k_got, gnq))
    b_p, b_q, *b_stay = join(
        join_down_kv_kernel, [d_keep.reshape(64, 16, D), d_got.reshape(64, 16, D), k_keep, k_got], [(24, 16, D)] * 4,
    )
    b_p, b_q, gain_got = lax.optimization_barrier((b_p, b_q, gain_got))
    b_first = first((b_p, b_q), Y_BIT)
    u_p, u_q, *u_stay = join(
        join_up_q_kernel, [u_keep.reshape(80, 16, D), u_got.reshape(80, 16, D), k_keep, k_got, gain, gain_got, row_b],
        [(28, 16, D), (24, 16, D), (25, 16, D), (24, 16, D)],
    )
    u_first = first((u_p, u_q), X_BIT)
    row_a = send(row_a, ROW_A)
    b_first, row_a = lax.optimization_barrier((b_first, row_a))
    u_p, u_q, *u_own = join(second_kernel, [*u_first, *u_stay], [(13, 16, D), (12, 16, D)] * 2)
    u_second = second((u_p, u_q), X_BIT)
    b_p, b_q, *b_own = join(second_kernel, [*b_first, *b_stay], [(12, 16, D)] * 4)
    b_second = second((b_p, b_q), Y_BIT)
    gne = gne.reshape(ROWS, EC, D)
    gne = gne + place(row_a, 0, row_odd, True, ROWS) + place(u_first[0][25:], 0, row_odd, False, ROWS)
    u = join(sum_up_q_kernel, [*u_second, *u_own], [(7, 16, D)] * 4)
    u = to_three(u, Y_BIT)
    b = join(sum_down_kv_kernel, [*b_second, *b_own], [(6, 16, D)] * 4)
    b = to_three(b, X_BIT)
    to_a = gne[:, COLS : COLS + RIM].astype(BF16)
    to_b = gne[:, COLS + RIM : COLS + 2 * RIM].astype(BF16)
    u, b, gne, to_a, to_b = lax.optimization_barrier((u, b, gne, to_a, to_b))
    (spread,) = call(
        reduce_xy_kernel, [((8, ZROWS, 128), BF16)], [pltpu.VMEM((8 * ZROWS, 128), F32)], 0, 8, 60_000_000, 4_000_000, 5,
    )(*u, *b)
    got_z = exchange(spread, Z_GROUPS)
    back_b, back_a = send(to_b, COL_B), send(to_a, COL_A)
    g_up, g_down, g_out, g_qkv, g_gains = call(
        reduce_z_kernel,
        [((32, 128), F32), ((32, 128), F32), ((8, 128), F32), ((24, 128), F32), ((2, D), F32)],
        [], 0, 1, 100_000_000_000, 400_000, 4,
    )(got_z)

    g_gains, back_a, back_b = lax.optimization_barrier((g_gains, back_a, back_b))
    gn = gne[:, :COLS] + place(back_a, 1, col_odd, True, COLS) + place(back_b, 1, col_odd, False, COLS)
    gn = gn + gnq.reshape(ROWS, COLS, D)
    unit, inv = unit_of(tokens.astype(F32))
    g1 = gn * gains[0]
    front = inv * (g1 - unit * jnp.mean(g1 * unit, axis=-1, keepdims=True))
    grad_tokens = (gm.reshape(ROWS, COLS, D).astype(F32) + front).astype(BF16)
    return (grad_tokens, g_qkv.reshape(-1), g_out.reshape(-1), g_up.reshape(-1), g_down.reshape(-1), g_gains)


def solution(mesh):
    block = P("row", "col", None)
    flat = P(("row", "col"))
    return jax.shard_map(
        per_device,
        mesh=mesh,
        in_specs=(block, block, P(), P(), P(), P(), P(), block),
        out_specs=(block, flat, flat, flat, flat, P()),
        check_vma=False,
    )
```
